32 devices in a mesh: dp: 8 (over z, y), seq: 4 (over x, core).
Axes of the slice: x: 2, y: 2, z: 4, core: 2. Of those that a mesh axis runs over, the one named last changes fastest.
Arguments:
- tokens: bfloat16 [8, 1024, 2048], P('dp', 'seq'), may hold values from -6 to 6
- cotangent: bfloat16 [8, 1024, 2048], P('dp', 'seq'), may hold values from -6 to 6
- lengths: int32 [8], P('dp'), may hold values from 256 to 1024, as said below
- norm_gain: float32 [2048], replicated, may hold values from 0.5 to 1.5
- w_in: float32 [2048, 8512], P(('dp', 'seq')), may hold values from -0.125 to 0.125
- conv_w: float32 [4352, 4], replicated, may hold values from -3 to 3
- conv_b: float32 [4352], replicated, may hold values from -3 to 3
- dt_bias: float32 [64], replicated, may hold values from -5 to -3
- a_log: float32 [64], replicated
- skip_scale: float32 [64], replicated, may hold values from 0.5 to 1.5
- gate_gain: float32 [4096], replicated, may hold values from 0.5 to 1.5
- w_out: float32 [4096, 2048], P(('dp', 'seq')), may hold values from -0.09375 to 0.09375
Outputs:
- output: bfloat16 [8, 1024, 2048], P('dp', 'seq')
- input_grad: float32 [8, 1024, 2048], P('dp', 'seq')
- grad_norm_gain: float32 [2048], replicated
- grad_w_in: float32 [2048, 8512], P(('dp', 'seq'))
- grad_conv_w: float32 [4352, 4], replicated
- grad_conv_b: float32 [4352], replicated
- grad_dt_bias: float32 [64], replicated
- grad_a_log: float32 [64], replicated
- grad_skip_scale: float32 [64], replicated
- grad_gate_gain: float32 [4096], replicated
- grad_w_out: float32 [4096, 2048], P(('dp', 'seq'))
The draws below stay inside these ranges and needn't reach their ends.
Inputs may be any that keep to these rules, and one draw needn't show every extreme that they name: Slot s holds 1024 positions; the first lengths[s] are tokens, the rest padding. Some slot is full in every draw.
All inputs are finite; a program needn't handle non-finite values.
Results may differ from the reference program's by a relative error of at most 0.018.
Values may be sent and summed in bfloat16 or wider, within the bound.
A program may use at most 256 MiB of HBM per device.

```python
import jax
import jax.numpy as jnp
from jax import lax

D = 2048
HEADS = 64
HEADDIM = 64
STATE = 128
KERNEL = 4
STRETCH = 256
INNER = 4096
CHANNELS = 4352
PROJECTED = 8512
LEN = 1024
SEQS = 8


def draw_lengths(key, part):
    key = jax.random.fold_in(key, 11)
    value_key, full_key = jax.random.split(key)
    values = jax.random.randint(value_key, (SEQS,), LEN // 4, LEN + 1)
    full_slot = jax.random.randint(full_key, (), 0, SEQS)
    return jnp.where(jnp.arange(SEQS) == full_slot, LEN, values).astype(jnp.int32)


def draw_a_log(key, part):
    key = jax.random.fold_in(key, 23)
    pick_key, slow_key, fast_key = jax.random.split(key, 3)
    share = 0.5
    chosen = jax.random.uniform(pick_key, (HEADS,)) < share
    slow = jnp.log(jax.random.uniform(slow_key, (HEADS,), minval=0.5, maxval=2.0) / (0.02 * LEN))
    fast = -jnp.log(0.02 * jax.random.uniform(fast_key, (HEADS,), minval=30.0, maxval=50.0))
    return jnp.where(chosen, slow, fast).astype(jnp.float32)


def block_levels(rng, extent, cuts, least, high):
    factor_of, own = 1.0, jax.random.fold_in(rng, 6)
    for position, parts in cuts:
        steps = jnp.exp(jax.random.uniform(jax.random.fold_in(own, position), (parts,), jnp.float32, least / len(cuts), high / len(cuts)))
        factor_of = factor_of * jnp.repeat(steps, extent[position] // parts).reshape([-1 if axis == position else 1 for axis in range(len(extent))])
    return factor_of


def noise(stream_key, shape, spread, bound, cuts=(), kind=jnp.bfloat16):
    loudness = block_levels(stream_key, shape, cuts, -0.22, 0.18) if cuts else 1.0
    drawn = jax.random.normal(stream_key, shape, jnp.float32) * spread * loudness
    return jnp.minimum(jnp.maximum(drawn, -bound), bound).astype(kind)


def setup_inputs(seed: int = 0) -> dict:
    arg_keys = jax.random.split(jax.random.key(seed), 13)
    tokens = noise(arg_keys[0], (SEQS, LEN, D), 1.0, 6.0, ((0, 8), (1, 4)))
    cotangent = noise(arg_keys[1], (SEQS, LEN, D), 1.0, 6.0, ((0, 8), (1, 4)))
    lengths = draw_lengths(jax.random.fold_in(arg_keys[12], 71), 0)
    norm_gain = jnp.clip(1.0 + 0.1 * jax.random.normal(arg_keys[3], (D,), jnp.float32), 0.5, 1.5)
    w_in = noise(arg_keys[4], (D, PROJECTED), D ** -0.5, 0.125, ((0, 32),), jnp.float32)
    conv_w = noise(arg_keys[5], (CHANNELS, KERNEL), KERNEL ** -0.5, 3.0, (), jnp.float32)
    conv_b = noise(arg_keys[6], (CHANNELS,), 0.5, 3.0, (), jnp.float32)
    dt_bias = jnp.clip(jax.random.uniform(arg_keys[7], (HEADS,), jnp.float32, -5.0, -3.0), -5.0, -3.0)
    a_log = draw_a_log(jax.random.fold_in(arg_keys[12], 71), 0)
    skip_scale = jnp.clip(jax.random.uniform(arg_keys[9], (HEADS,), jnp.float32, 0.5, 1.5), 0.5, 1.5)
    gate_gain = jnp.clip(1.0 + 0.1 * jax.random.normal(arg_keys[10], (INNER,), jnp.float32), 0.5, 1.5)
    w_out = noise(arg_keys[11], (INNER, D), INNER ** -0.5, 0.09375, ((0, 32),), jnp.float32)
    return {"tokens": tokens, "cotangent": cotangent, "lengths": lengths, "norm_gain": norm_gain, "w_in": w_in, "conv_w": conv_w, "conv_b": conv_b, "dt_bias": dt_bias, "a_log": a_log, "skip_scale": skip_scale, "gate_gain": gate_gain, "w_out": w_out}


EPSILON = 1e-05
HIGH = lax.Precision.HIGHEST

@jax.custom_vjp
def low(v):
    return lax.optimization_barrier(v.astype(jnp.bfloat16)).astype(jnp.float32)

@jax.custom_vjp
def low_back(v):
    return v

def low_keep(v):
    return (low(v), None)

def low_pass(kept, grad):
    return (grad,)

def back_keep(v):
    return (v, None)

def back_low(kept, grad):
    return (low(grad),)
low.defvjp(low_keep, low_pass)
low_back.defvjp(back_keep, back_low)

def stretch_step(carry_state, block_x, block_step, block_decay, block_b, block_c):
    running = jnp.cumsum(block_decay, 0).T
    width = block_x.shape[0]
    causal = jnp.arange(width)[:, None] >= jnp.arange(width)[None, :]
    differ = running[:, :, None] - running[:, None, :]
    decay = jnp.where(causal[None], jnp.exp(jnp.where(causal[None], differ, 0.0)), 0.0)
    products = jnp.dot(block_c, block_b.T, precision=HIGH)
    mixing = products[None] * decay * block_step.T[:, None, :]
    within = jnp.einsum('hts,shp->thp', mixing, block_x, precision=HIGH)
    entering = jnp.exp(running.T)[:, :, None] * jnp.einsum('tn,hpn->thp', block_c, carry_state, precision=HIGH)
    to_end = jnp.exp(running[:, -1:] - running) * block_step.T
    new_state = jnp.exp(running[:, -1])[:, None, None] * carry_state + jnp.einsum('hs,shp,sn->hpn', to_end, block_x, block_b, precision=HIGH)
    return (new_state, within + entering)

def state_space(heads_x, time_step, log_decay, b_in, c_out):
    span_rows = heads_x.shape[0]
    blocks_count = span_rows // STRETCH
    blocks = (heads_x.reshape(blocks_count, STRETCH, HEADS, HEADDIM), time_step.reshape(blocks_count, STRETCH, HEADS), log_decay.reshape(blocks_count, STRETCH, HEADS), b_in.reshape(blocks_count, STRETCH, STATE), c_out.reshape(blocks_count, STRETCH, STATE))

    def advance(carry_state, pieces):
        return stretch_step(carry_state, *pieces)
    final, outputs = lax.scan(jax.checkpoint(advance), jnp.zeros((HEADS, HEADDIM, STATE), jnp.float32), blocks)
    return (outputs.reshape(span_rows, HEADS, HEADDIM), final)

def convolve(padded, conv_w, conv_b):
    span_rows = padded.shape[0] - KERNEL + 1
    summed = conv_b[None, :]
    for offset in range(KERNEL):
        summed = summed + conv_w[:, offset][None, :] * padded[offset:offset + span_rows]
    return jax.nn.silu(summed)

def mixer_in(padded, dt_raw, conv_w, conv_b, dt_bias, a_log):
    active = convolve(padded, conv_w, conv_b)
    span_rows = active.shape[0]
    heads_x = active[:, :INNER].reshape(span_rows, HEADS, HEADDIM)
    b_in = active[:, INNER:INNER + STATE]
    c_out = active[:, INNER + STATE:]
    time_step = jax.nn.softplus(dt_raw + dt_bias)
    log_decay = time_step * -jnp.exp(a_log)
    return (heads_x, time_step, log_decay, b_in, c_out)

def gated(scanned, gate_in, gate_gain):
    product = scanned * jax.nn.silu(gate_in)
    return product * lax.rsqrt(lax.optimization_barrier(jnp.mean(product * product, -1, keepdims=True)) + EPSILON) * gate_gain

def layer(inputs, valid_mask, norm_gain, w_in, conv_w, conv_b, dt_bias, a_log, skip_scale, gate_gain, w_out):
    normed = low(inputs * lax.rsqrt(lax.optimization_barrier(jnp.mean(inputs * inputs, -1, keepdims=True)) + EPSILON) * norm_gain)
    projected = low_back(low(jnp.dot(normed, low(w_in), precision=HIGH)))
    gate_in = projected[:, :INNER]
    conv_in = projected[:, INNER:INNER + CHANNELS]
    dt_raw = projected[:, INNER + CHANNELS:]
    padded = jnp.concatenate([jnp.zeros((KERNEL - 1, CHANNELS), jnp.float32), conv_in], 0)
    heads_x, time_step, log_decay, b_in, c_out = mixer_in(padded, dt_raw, conv_w, conv_b, dt_bias, a_log)
    scanned, final = state_space(heads_x, time_step, log_decay, b_in, c_out)
    scanned = (scanned + skip_scale[None, :, None] * heads_x).reshape(-1, INNER)
    mixed = low(gated(scanned, gate_in, gate_gain))
    branch = low_back(jnp.dot(mixed, low(w_out), precision=HIGH))
    return valid_mask[:, None] * (inputs + branch)

def reference(tokens, cotangent, lengths, norm_gain, w_in, conv_w, conv_b, dt_bias, a_log, skip_scale, gate_gain, w_out):
    params = (norm_gain, w_in, conv_w, conv_b, dt_bias, a_log, skip_scale, gate_gain, w_out)

    def per_sequence(totals, item):
        seq_tokens, seq_cotangent, seq_length = item
        valid_mask = (jnp.arange(LEN, dtype=jnp.int32) < seq_length).astype(jnp.float32)

        def forward(inputs, *weights):
            return layer(inputs, valid_mask, *weights)
        result, pull = jax.vjp(forward, seq_tokens.astype(jnp.float32), *params)
        grads = pull(seq_cotangent.astype(jnp.float32))
        totals = tuple((summed + grad for summed, grad in zip(totals, grads[1:])))
        return (totals, (result.astype(jnp.bfloat16), grads[0]))
    zero_grads = tuple((jnp.zeros_like(param) for param in params))
    totals, (outputs, input_grad) = lax.scan(per_sequence, zero_grads, (tokens, cotangent, lengths))
    return (outputs, input_grad, totals[0], totals[1], totals[2], totals[3], totals[4], totals[5], totals[6], totals[7], totals[8])
```

```python
import functools

import jax
import jax.numpy as jnp
from jax import lax
from jax.experimental import pallas as pl
from jax.experimental.pallas import tpu as pltpu
from jax.sharding import Mesh
from jax.sharding import PartitionSpec as P

D = 2048
HEADS = 64
HEADDIM = 64
STATE = 128
KERNEL = 4
STRETCH = 256
INNER = 4096
CHANNELS = 4352
EPSILON = 1e-05
HIGH = lax.Precision.HIGHEST
BF16 = jnp.bfloat16
F32 = jnp.float32
GROUP = ("y", "seq")


def mm(a, b):
    return jnp.dot(a.astype(BF16), b.astype(BF16), preferred_element_type=F32)


def mm_last(a, b):
    return lax.dot_general(
        a.astype(BF16), b.astype(BF16), (((1,), (1,)), ((), ())), preferred_element_type=F32
    )


def iota(shape, axis):
    return lax.broadcasted_iota(jnp.int32, shape, axis)


def head_times(raw, bias, a_log):
    pre = raw + bias
    step = jnp.maximum(pre, 0.0) + jnp.log1p(jnp.exp(-jnp.abs(pre)))
    log_decay = step * -jnp.exp(a_log)
    width = raw.shape[1]
    upper = (iota((width, width), 0) <= iota((width, width), 1)).astype(F32)
    running = jnp.dot(log_decay, upper, precision=HIGH, preferred_element_type=F32)
    return pre, step, log_decay, running


def over_channels(values, pair):
    left = values[:, 2 * pair : 2 * pair + 1]
    right = values[:, 2 * pair + 1 : 2 * pair + 2]
    lane = iota((values.shape[0], 2 * HEADDIM), 1)
    return jnp.where(lane < HEADDIM, left, right)


def spread(values):
    pairs = values.shape[1] // 2
    return jnp.concatenate([over_channels(values, i) for i in range(pairs)], axis=1)


def convolved(block, halo, conv_w, conv_b):
    rows = block.shape[0]
    joined = jnp.concatenate([halo, block], axis=0)
    base = halo.shape[0] - KERNEL + 1
    shifted = [joined[base + k : base + k + rows] for k in range(KERNEL)]
    total = conv_b
    for k in range(KERNEL):
        total = total + conv_w[k : k + 1] * shifted[k]
    return total, shifted


def forward_kernel(
    x_ref, gate_ref, bc_ref, bct_ref, dt_ref, wx_ref, bx_ref, bias_ref, alog_ref, skip_ref,
    scanned_ref, state_ref, state, halo,
):
    @pl.when(pl.program_id(1) == 0)
    def _():
        state[...] = jnp.zeros_like(state)
        halo[...] = jnp.zeros_like(halo)

    rows, channels = x_ref.shape
    raw = x_ref[...].astype(F32)
    conv, _ = convolved(raw, halo[...], wx_ref[...], bx_ref[...])
    halo[...] = raw[rows - 8 :]
    xs = conv / (1.0 + jnp.exp(-conv))
    _, step_t, _, run_t = head_times(dt_ref[...], bias_ref[...], alog_ref[...])
    run = run_t.T
    xdt = xs * spread(step_t.T)
    b_t = bct_ref[:STATE]
    c = bc_ref[:, STATE:]
    causal = iota((rows, rows), 0) >= iota((rows, rows), 1)
    products = jnp.where(causal, mm(c, b_t), 0.0)
    entering = state[...]
    state_ref[0] = entering
    inward = mm(c, entering) * spread(jnp.exp(run))
    skipped = skip_ref[...] * xs
    lane = iota((rows, 2 * HEADDIM), 1)
    for pair in range(channels // 128):
        cols = slice(pair * 128, pair * 128 + 128)
        part = xdt[:, cols]
        total = inward[:, cols] + skipped[:, cols]
        for side in range(2):
            h = 2 * pair + side
            decay = jnp.exp(jnp.minimum(run[:, h : h + 1] - run_t[h : h + 1], 0.0))
            own = (lane < HEADDIM) if side == 0 else (lane >= HEADDIM)
            total = total + mm(products * decay, jnp.where(own, part, 0.0))
        scanned_ref[:, cols] = total
    last = run[rows - 1 :]
    to_end = spread(jnp.exp(last - run))
    state[...] = entering * spread(jnp.exp(last)) + mm(b_t, xdt * to_end)


def backward_kernel(
    x_ref, halo_ref, gate_ref, bc_ref, bct_ref, dt_ref, wx_ref, bx_ref, bias_ref, alog_ref, skip_ref,
    gain_ref, scanned_ref, state_ref, mixed_grad_ref, norms_ref,
    grad_ref, dbc_ref, ddt_ref, sums_ref, heads_ref,
    lam, rim,
):
    step_id = pl.program_id(1)
    first = (pl.program_id(0) == 0) & (step_id == 0)

    @pl.when(first)
    def _():
        sums_ref[...] = jnp.zeros_like(sums_ref)
        heads_ref[...] = jnp.zeros_like(heads_ref)

    @pl.when(step_id == 0)
    def _():
        lam[...] = jnp.zeros_like(lam)
        rim[...] = jnp.zeros_like(rim)

    rows, channels = x_ref.shape
    heads = channels // HEADDIM
    gate = gate_ref[...].astype(F32)
    scanned = scanned_ref[...]
    mixed_grad = mixed_grad_ref[...].astype(F32)
    norms = norms_ref[...].T
    r = norms[:, 0:1]
    inner = norms[:, 1:2]
    sig = 1.0 / (1.0 + jnp.exp(-gate))
    silu = gate * sig
    product = scanned * silu
    product_grad = r * (mixed_grad * gain_ref[...]) - product * (r * r * r * inner)
    sums_ref[5:6] += jnp.sum(mixed_grad * product * r, 0, keepdims=True)
    dy = product_grad * silu
    grad_ref[:, :channels] = (product_grad * scanned * (sig * (1.0 + gate * (1.0 - sig)))).astype(BF16)

    raw = x_ref[...].astype(F32)
    before = jnp.where(step_id == pl.num_programs(1) - 1, 0.0, halo_ref[...].astype(F32))
    conv, shifted = convolved(raw, before, wx_ref[...], bx_ref[...])
    sig_c = 1.0 / (1.0 + jnp.exp(-conv))
    xs = conv * sig_c
    sums_ref[6:7] += jnp.sum(dy * xs, 0, keepdims=True)
    pre, step_t, decay_t, run_t = head_times(dt_ref[...], bias_ref[...], alog_ref[...])
    run = run_t.T
    step = spread(step_t.T)
    xdt = xs * step
    b = bc_ref[:, :STATE]
    c = bc_ref[:, STATE:]
    b_t = bct_ref[:STATE]
    c_t = bct_ref[STATE:]
    causal = iota((rows, rows), 0) >= iota((rows, rows), 1)
    products = jnp.where(causal, mm(c, b_t), 0.0)
    entering = state_ref[0]
    leaving = lam[...]
    last = run[rows - 1 :]
    to_end = spread(jnp.exp(last - run))
    whole = spread(jnp.exp(last))
    dye = dy * spread(jnp.exp(run))
    xend = xdt * to_end
    inward = dye * mm(c, entering)
    outward_grad = mm(b, leaving) * to_end
    outward = outward_grad * xdt
    dc_t = mm_last(entering, dye)
    db_t = mm_last(leaving, xend)
    kept = leaving * whole
    lam[...] = kept + mm(c_t, dye)

    dy_t = dy.T.astype(BF16)
    lane = iota((rows, 2 * HEADDIM), 1)
    wide = iota((rows, heads), 1)
    dproducts = jnp.zeros((rows, rows), F32)
    row_sums = jnp.zeros((rows, heads), F32)
    col_sums = []
    dxdt_t = []
    for h in range(heads):
        cols = slice((h // 2) * 128, (h // 2) * 128 + 128)
        own = (lane < HEADDIM) if h % 2 == 0 else (lane >= HEADDIM)
        decay = jnp.exp(jnp.minimum(run[:, h : h + 1] - run_t[h : h + 1], 0.0))
        weights = products * decay
        dweights = mm_last(dy[:, cols], jnp.where(own, xdt[:, cols], 0.0))
        dproducts = dproducts + dweights * decay
        shares = dweights * weights
        row_sums = jnp.where(wide == h, jnp.sum(shares, 1, keepdims=True), row_sums)
        col_sums.append(jnp.sum(shares, 0, keepdims=True))
        dxdt_t.append(mm(dy_t[h * HEADDIM : (h + 1) * HEADDIM], weights))
    dproducts = jnp.where(causal, dproducts, 0.0)
    dc_t = dc_t + mm_last(b_t, dproducts)
    db_t = db_t + mm(c_t, dproducts)
    dbc_ref[:STATE] = db_t
    dbc_ref[STATE:] = dc_t
    dxdt = jnp.concatenate(dxdt_t, 0).T + outward_grad

    member = (iota((heads, channels), 1) // HEADDIM == iota((heads, channels), 0)).astype(F32)

    def per_head(values):
        return lax.dot_general(
            member, values, (((1,), (1,)), ((), ())), precision=HIGH, preferred_element_type=F32
        )

    out_t = per_head(outward)
    run_grad = per_head(inward) - out_t + row_sums.T - jnp.concatenate(col_sums, 0)
    at_end = jnp.sum(out_t, 1, keepdims=True) + jnp.sum(per_head(kept * entering), 1, keepdims=True)
    lower = (iota((rows, rows), 0) >= iota((rows, rows), 1)).astype(F32)
    decay_grad = at_end + jnp.dot(run_grad, lower, precision=HIGH, preferred_element_type=F32)
    step_grad = per_head(dxdt * xs) - jnp.exp(alog_ref[...]) * decay_grad
    dt_grad = step_grad / (1.0 + jnp.exp(-pre))
    ddt_ref[...] = dt_grad.astype(BF16)
    heads_ref[:, 0:1] += jnp.sum(dt_grad, 1, keepdims=True)
    heads_ref[:, 1:2] += jnp.sum(decay_grad * decay_t, 1, keepdims=True)

    dx = dxdt * step + skip_ref[...] * dy
    dconv = dx * (sig_c * (1.0 + conv * (1.0 - sig_c)))
    sums_ref[4:5] += jnp.sum(dconv, 0, keepdims=True)
    for k in range(KERNEL):
        sums_ref[k : k + 1] += jnp.sum(dconv * shifted[k], 0, keepdims=True)
    joined = jnp.concatenate([dconv, rim[...]], 0)
    rim[...] = dconv[:8]
    dx_in = wx_ref[KERNEL - 1 : KERNEL] * dconv
    for k in range(KERNEL - 1):
        ahead = KERNEL - 1 - k
        dx_in = dx_in + wx_ref[k : k + 1] * joined[ahead : ahead + rows]
    grad_ref[:, channels:] = dx_in.astype(BF16)


def whole_spec(array):
    return pl.BlockSpec(array.shape, lambda q, i: (0,) * array.ndim)


def scan_forward(projected, bc, bc_t, dt_t, params, seqs):
    total, channels = projected.shape[0], projected.shape[1] // 2
    heads = channels // HEADDIM
    steps = total // seqs // STRETCH
    row = lambda q, i: q * steps + i
    return pl.pallas_call(
        forward_kernel,
        grid=(seqs, steps),
        in_specs=[
            pl.BlockSpec((STRETCH, channels), lambda q, i: (row(q, i), 1)),
            pl.BlockSpec((STRETCH, channels), lambda q, i: (row(q, i), 0)),
            pl.BlockSpec((STRETCH, 2 * STATE), lambda q, i: (row(q, i), 0)),
            pl.BlockSpec((2 * STATE, STRETCH), lambda q, i: (0, row(q, i))),
            pl.BlockSpec((heads, STRETCH), lambda q, i: (0, row(q, i))),
        ]
        + [whole_spec(p) for p in params],
        out_specs=[
            pl.BlockSpec((STRETCH, channels), lambda q, i: (row(q, i), 0)),
            pl.BlockSpec((1, STATE, channels), lambda q, i: (row(q, i), 0, 0)),
        ],
        out_shape=[
            jax.ShapeDtypeStruct((total, channels), F32),
            jax.ShapeDtypeStruct((seqs * steps, STATE, channels), F32),
        ],
        scratch_shapes=[pltpu.VMEM((STATE, channels), F32), pltpu.VMEM((8, channels), F32)],
        compiler_params=pltpu.CompilerParams(vmem_limit_bytes=48 << 20),
        name="scan_forward",
    )(projected, projected, bc, bc_t, dt_t, *params)


def scan_backward(projected, bc, bc_t, dt_t, params, gain, scanned, states, mixed_grad, norms, seqs):
    total, channels = projected.shape[0], projected.shape[1] // 2
    heads = channels // HEADDIM
    steps = total // seqs // STRETCH
    row = lambda q, i: q * steps + steps - 1 - i
    halo_row = lambda q, i: jnp.maximum(row(q, i) * (STRETCH // 16) - 1, 0)
    return pl.pallas_call(
        backward_kernel,
        grid=(seqs, steps),
        in_specs=[
            pl.BlockSpec((STRETCH, channels), lambda q, i: (row(q, i), 1)),
            pl.BlockSpec((16, channels), lambda q, i: (halo_row(q, i), 1)),
            pl.BlockSpec((STRETCH, channels), lambda q, i: (row(q, i), 0)),
            pl.BlockSpec((STRETCH, 2 * STATE), lambda q, i: (row(q, i), 0)),
            pl.BlockSpec((2 * STATE, STRETCH), lambda q, i: (0, row(q, i))),
            pl.BlockSpec((heads, STRETCH), lambda q, i: (0, row(q, i))),
        ]
        + [whole_spec(p) for p in params]
        + [
            whole_spec(gain),
            pl.BlockSpec((STRETCH, channels), lambda q, i: (row(q, i), 0)),
            pl.BlockSpec((1, STATE, channels), lambda q, i: (row(q, i), 0, 0)),
            pl.BlockSpec((STRETCH, channels), lambda q, i: (row(q, i), 0)),
            pl.BlockSpec((8, STRETCH), lambda q, i: (0, row(q, i))),
        ],
        out_specs=[
            pl.BlockSpec((STRETCH, 2 * channels), lambda q, i: (row(q, i), 0)),
            pl.BlockSpec((2 * STATE, STRETCH), lambda q, i: (0, row(q, i))),
            pl.BlockSpec((heads, STRETCH), lambda q, i: (0, row(q, i))),
            pl.BlockSpec((8, channels), lambda q, i: (0, 0)),
            pl.BlockSpec((heads, 128), lambda q, i: (0, 0)),
        ],
        out_shape=[
            jax.ShapeDtypeStruct((total, 2 * channels), BF16),
            jax.ShapeDtypeStruct((2 * STATE, total), F32),
            jax.ShapeDtypeStruct((heads, total), BF16),
            jax.ShapeDtypeStruct((8, channels), F32),
            jax.ShapeDtypeStruct((heads, 128), F32),
        ],
        scratch_shapes=[pltpu.VMEM((STATE, channels), F32), pltpu.VMEM((8, channels), F32)],
        compiler_params=pltpu.CompilerParams(vmem_limit_bytes=56 << 20),
        name="scan_backward",
    )(projected, projected, projected, bc, bc_t, dt_t, *params, gain, scanned, states, mixed_grad, norms)


def shift_later(values, by, seqs):
    if by == 0:
        return values
    split = values.reshape(values.shape[0], seqs, -1)
    moved = jnp.pad(split, ((0, 0), (0, 0), (by, 0)))[:, :, : split.shape[2]]
    return moved.reshape(values.shape)


def shift_earlier(values, by, seqs):
    if by == 0:
        return values
    split = values.reshape(values.shape[0], seqs, -1)
    moved = jnp.pad(split, ((0, 0), (0, 0), (0, by)))[:, :, by:]
    return moved.reshape(values.shape)


class Layout:
    def __init__(self, planes, group, rows_out):
        self.planes, self.group = planes, group
        self.aligned = rows_out % HEADDIM == 0
        self.blocks = planes if self.aligned else 1
        self.block = INNER // group // self.blocks
        self.heads = HEADS // group
        self.channels = INNER // group
        self.small = 2 * STATE // group

    def pieces(self, values, unit):
        rows = values.shape[0]
        parts = values.reshape(rows, self.blocks, self.group, self.block // HEADDIM * unit)
        return parts.transpose(0, 2, 1, 3).reshape(rows, self.group, -1)

    def joined(self, values, unit):
        rows = values.shape[0]
        parts = values.reshape(rows, self.group, self.blocks, self.block // HEADDIM * unit)
        return parts.transpose(0, 2, 1, 3).reshape(rows, -1)

    def columns(self, w):
        gate = self.pieces(w[:, :INNER], HEADDIM)
        x = self.pieces(w[:, INNER : 2 * INNER], HEADDIM)
        bc = w[:, 2 * INNER : INNER + CHANNELS].reshape(w.shape[0], self.group, self.small)
        dt = self.pieces(w[:, INNER + CHANNELS :], 1)
        return jnp.concatenate([gate, x, bc, dt], 2)

    def uncolumns(self, g):
        c, s = self.channels, self.small
        gate = self.joined(g[:, :, :c], HEADDIM)
        x = self.joined(g[:, :, c : 2 * c], HEADDIM)
        bc = g[:, :, 2 * c : 2 * c + s].reshape(g.shape[0], -1)
        dt = self.joined(g[:, :, 2 * c + s :], 1)
        return jnp.concatenate([gate, x, bc, dt], 1)


def body(
    tokens, cotangent, lengths, norm_gain, w_in, conv_w, conv_b, dt_bias, a_log, skip_scale, gate_gain, w_out,
):
    row_count = tokens.shape[1]
    planes, group = lax.axis_size("z"), lax.axis_size("y") * lax.axis_size("seq")
    seqs = lax.axis_size("y")
    rank = lax.axis_index("y") * lax.axis_size("seq") + lax.axis_index("seq")
    lay = Layout(planes, group, w_out.shape[0])
    channels, small = lay.channels, lay.small
    inputs = tokens.reshape(row_count, D).astype(F32)
    position = lax.axis_index("seq") * row_count + jnp.arange(row_count, dtype=jnp.int32)
    valid_mask = (position < lengths[0]).astype(F32)[:, None]
    rms = lax.rsqrt(jnp.mean(inputs * inputs, -1, keepdims=True) + EPSILON)
    normed = (inputs * rms * norm_gain).astype(BF16)
    masked_cot = cotangent.reshape(row_count, D).astype(F32) * valid_mask
    branch_grad = masked_cot.astype(BF16)

    pieces = lay.columns(w_in.astype(BF16)).reshape(w_in.shape[0], -1)
    plane_rows = lax.all_to_all(pieces, GROUP, split_axis=1, concat_axis=0, tiled=True)
    w_own = lax.all_gather(plane_rows, "z", axis=0, tiled=True)
    w_main, w_small = w_own[:, : 2 * channels], w_own[:, 2 * channels :]
    if lay.aligned:
        out_own = lax.all_gather(w_out.astype(BF16), "z", axis=0, tiled=True)
    else:
        out_all = lax.all_gather(w_out.astype(BF16), ("z",) + GROUP, axis=0, tiled=True)
        out_own = lax.dynamic_slice_in_dim(out_all, rank * channels, channels, 0)

    def own(values, unit):
        return lax.dynamic_index_in_dim(lay.pieces(values, unit), rank, 1, keepdims=False)

    conv_wx = own(conv_w[:INNER].T, HEADDIM)
    conv_bx = own(conv_b[None, :INNER], HEADDIM)
    bias_own = own(dt_bias[None], 1).T
    a_own = own(a_log[None], 1).T
    skip_own = jnp.repeat(own(skip_scale[None], 1), HEADDIM, 1)
    gain_own = own(gate_gain[None], HEADDIM)
    params = (conv_wx, conv_bx, bias_own, a_own, skip_own)

    normed_all = lax.all_gather(normed, GROUP, axis=0, tiled=True)
    projected = jnp.dot(normed_all, w_main, preferred_element_type=F32).astype(BF16)
    small_t = lax.dot_general(
        w_small, normed_all, (((0,), (1,)), ((), ())), preferred_element_type=F32
    ).astype(BF16)
    dt_t = small_t[small:].astype(F32)
    bc_in = lax.all_gather(small_t[:small], GROUP, axis=0, tiled=True).astype(F32)
    conv_bc = conv_b[INNER:, None]
    for k in range(KERNEL):
        conv_bc = conv_bc + conv_w[INNER:, k : k + 1] * shift_later(bc_in, KERNEL - 1 - k, seqs)
    bc_t = jax.nn.silu(conv_bc).astype(BF16)
    bc = bc_t.T

    scanned, states = scan_forward(projected, bc, bc_t, dt_t, params, seqs)

    grad_all = lax.all_gather(branch_grad, GROUP, axis=0, tiled=True)
    mixed_grad = lax.dot_general(
        grad_all, out_own, (((1,), (1,)), ((), ())), preferred_element_type=F32
    )
    product = scanned * jax.nn.silu(projected[:, :channels].astype(F32))
    sums = lax.psum(
        jnp.stack([jnp.sum(product * product, 1), jnp.sum(mixed_grad * gain_own * product, 1)]), GROUP
    )
    r = lax.rsqrt(sums[0] / INNER + EPSILON)
    norms = jnp.concatenate([r[None], sums[1:] / INNER, jnp.zeros((6, r.shape[0]), F32)], 0)
    mixed = (product * r[:, None] * gain_own).astype(BF16)

    branch = lax.psum_scatter(
        jnp.dot(mixed, out_own, preferred_element_type=F32).astype(BF16),
        GROUP, scatter_dimension=0, tiled=True,
    ).astype(F32)
    output = (valid_mask * (inputs + branch)).astype(BF16)
    out_part = lax.dot_general(
        mixed, grad_all, (((0,), (0,)), ((), ())), preferred_element_type=F32
    ).astype(BF16)
    if lay.aligned:
        grad_w_out = lax.psum_scatter(out_part, "z", scatter_dimension=0, tiled=True).astype(F32)
    else:
        placed = lax.dynamic_update_slice_in_dim(jnp.zeros((INNER, D), BF16), out_part, rank * channels, 0)
        grad_w_out = lax.psum_scatter(placed, ("z",) + GROUP, scatter_dimension=0, tiled=True).astype(F32)

    proj_grad, dbc_t, ddt_t, sums_x, sums_h = scan_backward(
        projected, bc, bc_t, dt_t, params, gain_own, scanned, states, mixed_grad, norms, seqs
    )
    dbc = lax.psum_scatter(dbc_t, GROUP, scatter_dimension=0, tiled=True)
    own_rows = lambda v: lax.dynamic_slice_in_dim(v, rank * small, small, 0)
    conv_own, in_own, w_bc = own_rows(conv_bc), own_rows(bc_in), own_rows(conv_w[INNER:])
    sig = jax.nn.sigmoid(conv_own)
    dconv = dbc * sig * (1.0 + conv_own * (1.0 - sig))
    din = 0.0
    grad_w_bc = []
    for k in range(KERNEL):
        grad_w_bc.append(jnp.sum(dconv * shift_later(in_own, KERNEL - 1 - k, seqs), 1))
        din = din + w_bc[:, k : k + 1] * shift_earlier(dconv, KERNEL - 1 - k, seqs)
    small_grad_t = jnp.concatenate([din.astype(BF16), ddt_t], 0)

    contract_rows = (((0,), (0,)), ((), ()))
    in_main = lax.dot_general(normed_all, proj_grad, contract_rows, preferred_element_type=F32)
    in_small = lax.dot_general(
        normed_all, small_grad_t, (((0,), (1,)), ((), ())), preferred_element_type=F32
    )
    in_part = jnp.concatenate([in_main.astype(BF16), in_small.astype(BF16)], 1)
    in_rows = lax.psum_scatter(in_part, "z", scatter_dimension=0, tiled=True)
    in_pieces = lax.all_to_all(in_rows, GROUP, split_axis=0, concat_axis=1, tiled=True)
    grad_w_in = lay.uncolumns(in_pieces.reshape(w_in.shape[0], group, -1).astype(F32))

    normed_part = lax.dot_general(
        proj_grad, w_main, (((1,), (1,)), ((), ())), preferred_element_type=F32
    ) + lax.dot_general(small_grad_t, w_small, (((0,), (1,)), ((), ())), preferred_element_type=F32)
    normed_grad = lax.psum_scatter(
        normed_part.astype(BF16), GROUP, scatter_dimension=0, tiled=True
    ).astype(F32)
    g = normed_grad * norm_gain
    input_grad = masked_cot + rms * g - inputs * (rms ** 3 * jnp.mean(g * inputs, -1, keepdims=True))
    norm_gain_grad = jnp.sum(normed_grad * inputs * rms, 0)

    own_sums = jnp.concatenate(
        [
            sums_x[: KERNEL + 2].reshape(-1),
            jnp.sum(sums_x[KERNEL + 2].reshape(-1, HEADDIM), 1),
            sums_h[:, 0],
            sums_h[:, 1],
            jnp.stack(grad_w_bc).reshape(-1),
            jnp.sum(dconv, 1),
        ]
    )
    count = own_sums.shape[0]
    everyone = lax.all_gather(jnp.concatenate([own_sums, norm_gain_grad]), ("z",) + GROUP)
    grad_norm_gain = jnp.sum(everyone[:, count:], 0)
    by_rank = jnp.sum(everyone[:, :count].reshape(planes, group, count), 0)
    at = 0

    def take(size):
        nonlocal at
        at += size
        return by_rank[:, at - size : at]

    taken_x = take((KERNEL + 2) * channels).reshape(group, KERNEL + 2, channels).transpose(1, 0, 2)
    full_x = lay.joined(taken_x, HEADDIM)
    grad_skip, grad_bias, grad_a = (
        lay.joined(take(lay.heads)[None], 1)[0] for _ in range(3)
    )
    conv_w_bc = take(KERNEL * small).reshape(group, KERNEL, small).transpose(1, 0, 2).reshape(KERNEL, -1)
    conv_b_bc = take(small).reshape(-1)
    grad_conv_w = jnp.concatenate([full_x[:KERNEL], conv_w_bc], 1).T
    grad_conv_b = jnp.concatenate([full_x[KERNEL], conv_b_bc])
    return (
        output.reshape(tokens.shape),
        input_grad.reshape(1, row_count, D),
        grad_norm_gain,
        grad_w_in,
        grad_conv_w,
        grad_conv_b,
        grad_bias,
        grad_a,
        grad_skip,
        full_x[KERNEL + 1],
        grad_w_out,
    )


def solution(mesh):
    dp, seq = mesh.shape["dp"], mesh.shape["seq"]
    inner_mesh = Mesh(mesh.devices.reshape(dp // 2, 2, seq), ("z", "y", "seq"))
    placed = P(("z", "y"), "seq", None)
    rows = P(("z", "y", "seq"), None)
    in_specs = (placed, placed, P(("z", "y")), P(), rows, P(), P(), P(), P(), P(), P(), rows)
    out_specs = (placed, placed, P(), rows, P(), P(), P(), P(), P(), P(), rows)
    return jax.shard_map(body, mesh=inner_mesh, in_specs=in_specs, out_specs=out_specs, check_vma=False)
```

```python
import functools

import jax
import jax.numpy as jnp
from jax import lax
from jax.experimental import pallas as pl
from jax.experimental.pallas import tpu as pltpu
from jax.sharding import Mesh
from jax.sharding import PartitionSpec as P

D = 2048
HEADS = 64
HEADDIM = 64
STATE = 128
KERNEL = 4
STRETCH = 256
INNER = 4096
CHANNELS = 4352
EPSILON = 1e-05
HIGH = lax.Precision.HIGHEST
BF16 = jnp.bfloat16
F32 = jnp.float32
GROUP = ("y", "seq")


def mm(a, b):
    return jnp.dot(a.astype(BF16), b.astype(BF16), preferred_element_type=F32)


def mm_last(a, b):
    return lax.dot_general(
        a.astype(BF16), b.astype(BF16), (((1,), (1,)), ((), ())), preferred_element_type=F32
    )


def iota(shape, axis):
    return lax.broadcasted_iota(jnp.int32, shape, axis)


def head_times(raw, bias, a_log):
    pre = raw + bias
    step = jnp.maximum(pre, 0.0) + jnp.log1p(jnp.exp(-jnp.abs(pre)))
    log_decay = step * -jnp.exp(a_log)
    width = raw.shape[1]
    upper = (iota((width, width), 0) <= iota((width, width), 1)).astype(F32)
    running = jnp.dot(log_decay, upper, precision=HIGH, preferred_element_type=F32)
    return pre, step, log_decay, running


def over_channels(values, pair):
    left = values[:, 2 * pair : 2 * pair + 1]
    right = values[:, 2 * pair + 1 : 2 * pair + 2]
    lane = iota((values.shape[0], 2 * HEADDIM), 1)
    return jnp.where(lane < HEADDIM, left, right)


def spread(values):
    pairs = values.shape[1] // 2
    return jnp.concatenate([over_channels(values, i) for i in range(pairs)], axis=1)


def convolved(block, halo, conv_w, conv_b):
    rows = block.shape[0]
    joined = jnp.concatenate([halo, block], axis=0)
    base = halo.shape[0] - KERNEL + 1
    shifted = [joined[base + k : base + k + rows] for k in range(KERNEL)]
    total = conv_b
    for k in range(KERNEL):
        total = total + conv_w[k : k + 1] * shifted[k]
    return total, shifted


MESH = pl.DeviceIdType.MESH


def remote(src, dst, send_sem, recv_sem, device):
    return pltpu.make_async_remote_copy(
        src_ref=src, dst_ref=dst, send_sem=send_sem, recv_sem=recv_sem,
        device_id=device, device_id_type=MESH,
    )


class Place:
    def __init__(self, planes, ny, ns):
        self.planes, self.ny, self.ns, self.group = planes, ny, ns, ny * ns
        self.z, self.y, self.s = lax.axis_index("z"), lax.axis_index("y"), lax.axis_index("seq")
        self.rank = self.y * ns + self.s
        self.up, self.down = (self.z + 1, self.y, self.s), (self.z - 1, self.y, self.s)
        self.has_up, self.has_down = self.z < planes - 1, self.z > 0

    def member(self, rank):
        return (self.z, rank // self.ns, lax.rem(rank, self.ns))

    def peer(self, i):
        return lax.rem(self.rank + i, self.group)

    def far(self):
        chips = self.ns // 2
        x, core = self.s // 2, lax.rem(self.s, 2)
        for dy in range(self.ny):
            for dx in range(chips):
                if dy or dx:
                    yield lax.rem(self.y + dy, self.ny) * self.ns + lax.rem(x + dx, chips) * 2 + core

    def sibling(self, rank):
        return rank + 1 - 2 * lax.rem(rank, 2)

    def greet(self):
        barrier = pltpu.get_barrier_semaphore()
        for i in range(1, self.group):
            pl.semaphore_signal(barrier, inc=1, device_id=self.member(self.peer(i)), device_id_type=MESH)

        @pl.when(self.has_up)
        def _():
            pl.semaphore_signal(barrier, inc=1, device_id=self.up, device_id_type=MESH)

        @pl.when(self.has_down)
        def _():
            pl.semaphore_signal(barrier, inc=1, device_id=self.down, device_id_type=MESH)

        count = self.group - 1 + self.has_up.astype(jnp.int32) + self.has_down.astype(jnp.int32)
        pl.semaphore_wait(barrier, count)


def project_kernel(
    planes, ny, ns, cut, heads,
    pm_ref, ps_ref, nm_ref,
    proj_ref, bct_ref, dt_ref, nall_ref, wm_ref, ws_ref,
    wmain, wsmall, normed, acc, outb, bcb,
    am_send, am_recv, as_send, as_recv, n_send, n_recv, f_send, b_send, b_recv,
    up_send, up_recv, down_send, down_recv, sup_send, sup_recv, sdown_send, sdown_recv, local_sem,
):
    at = Place(planes, ny, ns)
    group, rank, z = at.group, at.rank, at.z
    piece = pm_ref.shape[1]
    plane_rows = piece * group
    total, slab = normed.shape[0], 256
    own_rows = nm_ref.shape[0]
    small = bcb.shape[0] // group
    part = plane_rows // cut

    def rows_of(r):
        return pl.ds(pl.multiple_of(z * plane_rows + r * piece, piece), piece)

    def block_rows(p, q):
        return pl.ds(pl.multiple_of(p * plane_rows + q * part, part), part)

    def plane_block(p):
        return pl.ds(pl.multiple_of(p * plane_rows, plane_rows), plane_rows)

    def norm_rows(r):
        return pl.ds(pl.multiple_of(r * own_rows, own_rows), own_rows)

    own_copies = [
        pltpu.make_async_copy(pm_ref.at[rank], wmain.at[rows_of(rank)], local_sem.at[0]),
        pltpu.make_async_copy(ps_ref.at[rank], wsmall.at[rows_of(rank)], local_sem.at[1]),
        pltpu.make_async_copy(nm_ref, normed.at[norm_rows(rank)], local_sem.at[2]),
    ]
    for copy in own_copies:
        copy.start()
    at.greet()

    def main_piece(r, i):
        return remote(pm_ref.at[r], wmain.at[rows_of(rank)], am_send.at[i], am_recv.at[rank], at.member(r))

    def small_piece(r, i):
        return remote(ps_ref.at[r], wsmall.at[rows_of(rank)], as_send.at[i], as_recv.at[rank], at.member(r))

    def norm_piece(r, i):
        return remote(nm_ref, normed.at[norm_rows(rank)], n_send.at[i], n_recv.at[rank], at.member(r))

    for i in range(1, group):
        small_piece(at.peer(i), i).start()
    for i in range(1, group):
        main_piece(at.peer(i), i).start()
    far = list(at.far())
    sibling = at.sibling(rank)
    norm_piece(sibling, 0).start()
    for i, r in enumerate(far):
        norm_piece(r, i + 1).start()
    acc[...] = jnp.zeros_like(acc)
    for copy in own_copies:
        copy.wait()

    for i in range(1, group):
        r = at.peer(i)
        remote(ps_ref.at[r], wsmall.at[rows_of(r)], as_send.at[i], as_recv.at[r], at.member(r)).wait_recv()

    def small_up(p, j):
        return remote(wsmall.at[plane_block(p)], wsmall.at[plane_block(p)], sup_send.at[j], sup_recv.at[j], at.up)

    def small_down(p, j):
        return remote(wsmall.at[plane_block(p)], wsmall.at[plane_block(p)], sdown_send.at[j], sdown_recv.at[j], at.down)

    def wide_up(p, q, k):
        return remote(wmain.at[block_rows(p, q)], wmain.at[block_rows(p, q)], up_send.at[k], up_recv.at[k], at.up)

    def wide_down(p, q, k):
        return remote(wmain.at[block_rows(p, q)], wmain.at[block_rows(p, q)], down_send.at[k], down_recv.at[k], at.down)

    def each_way(p, above, fn_up, fn_down):
        @pl.when(at.has_up & jnp.logical_not(above))
        def _():
            fn_up()

        @pl.when(at.has_down & above)
        def _():
            fn_down()

    @pl.when(at.has_up)
    def _():
        small_up(z, 0).start()

    @pl.when(at.has_down)
    def _():
        small_down(z, 0).start()

    ranks_in = group // cut
    for q in range(cut):
        for r in range(q * ranks_in, (q + 1) * ranks_in):
            @pl.when(rank != r)
            def _():
                remote(pm_ref.at[r], wmain.at[rows_of(r)], am_send.at[0], am_recv.at[r], at.member(r)).wait_recv()

        @pl.when(at.has_up)
        def _():
            wide_up(z, q, q).start()

        @pl.when(at.has_down)
        def _():
            wide_down(z, q, q).start()

    def small_step(j, _):
        @pl.when(z + j < planes)
        def _():
            small_down(z + j, j - 1).wait_recv()

            @pl.when(at.has_down)
            def _():
                small_down(z + j, j).start()

        @pl.when(z - j >= 0)
        def _():
            small_up(z - j, j - 1).wait_recv()

            @pl.when(at.has_up)
            def _():
                small_up(z - j, j).start()

        return 0

    lax.fori_loop(1, planes, small_step, 0)

    def relay(i, r):
        norm_piece_in = remote(nm_ref, normed.at[norm_rows(r)], n_send.at[i + 1], n_recv.at[r], at.member(r))
        norm_piece_in.wait_recv()
        remote(normed.at[norm_rows(r)], normed.at[norm_rows(r)], f_send.at[i], n_recv.at[r], at.member(sibling)).start()

    def norm_done():
        for r in [sibling] + [at.sibling(r) for r in far]:
            remote(nm_ref, normed.at[norm_rows(r)], n_send.at[0], n_recv.at[r], at.member(sibling)).wait_recv()

    def plane_in_turn(j):
        return lax.rem(jnp.where(2 * z < planes, z + j, z - j + planes), planes)

    slabs = total // slab

    def product(index):
        j, m = index // slabs, lax.rem(index, slabs)
        p = plane_in_turn(j)
        rows = pl.ds(pl.multiple_of(m * slab, slab), slab)
        lanes = pl.ds(pl.multiple_of(p * plane_rows, 128), plane_rows)
        return rows, acc[rows, :] + jnp.dot(
            normed[rows, lanes], wmain[plane_block(p), :], preferred_element_type=F32
        )

    def narrow(m, _):
        rows = pl.ds(pl.multiple_of(m * slab, slab), slab)
        value = jnp.dot(normed[rows, :], wsmall[...], preferred_element_type=F32).T
        bcb[pl.ds(pl.multiple_of(rank * small, small), small), rows] = value[:small].astype(BF16)
        dt_ref[:, rows] = value[small : small + heads].astype(BF16).astype(F32)
        return 0

    def bc_piece(r, i, owner):
        rows = pl.ds(pl.multiple_of(owner * small, small), small)
        return remote(bcb.at[rows], bcb.at[rows], b_send.at[i], b_recv.at[owner], at.member(r))

    steps = (planes - 1) * cut
    busy = (planes - 2) * cut
    per_step = -(-(planes - 1) * slabs // cut)

    def wide_step(k, _):
        j, q = k // cut + 1, lax.rem(k, cut)

        @pl.when(z + j < planes)
        def _():
            wide_down(z + j, q, k).wait_recv()

            @pl.when(at.has_down)
            def _():
                wide_down(z + j, q, k + cut).start()

        @pl.when(z - j >= 0)
        def _():
            wide_up(z - j, q, k).wait_recv()

            @pl.when(at.has_up)
            def _():
                wide_up(z - j, q, k + cut).start()

        return 0

    marks = [cut + i * max(busy - cut, 0) // len(far) for i in range(len(far))]
    last = 0
    for i, r in enumerate(far):
        lax.fori_loop(last, marks[i], wide_step, 0)
        last = marks[i]
        relay(i, r)
    lax.fori_loop(last, busy, wide_step, 0)
    norm_done()
    lax.fori_loop(0, slabs, narrow, 0)
    for i in range(1, group):
        bc_piece(at.peer(i), i, rank).start()
    nall_copy = pltpu.make_async_copy(normed, nall_ref, local_sem.at[0])
    nall_copy.start()
    ws_copy = pltpu.make_async_copy(wsmall, ws_ref, local_sem.at[1])
    ws_copy.start()

    def busy_step(k, _):
        wide_step(k, 0)

        def one(i, _):
            rows, value = product(jnp.minimum((k - busy) * per_step + i, (planes - 1) * slabs))

            @pl.when((k - busy) * per_step + i < (planes - 1) * slabs)
            def _():
                acc[rows, :] = value

            return 0

        lax.fori_loop(0, per_step, one, 0)
        return 0

    lax.fori_loop(busy, steps, busy_step, 0)
    wm_copy = pltpu.make_async_copy(wmain, wm_ref, local_sem.at[2])
    wm_copy.start()

    def out_copy(m):
        rows = pl.ds(pl.multiple_of(m * slab, slab), slab)
        return pltpu.make_async_copy(outb.at[rows], proj_ref.at[rows], local_sem.at[4 + m])

    def final(m, _):
        rows, value = product((planes - 1) * slabs + m)
        outb[rows, :] = value.astype(BF16)
        out_copy(m).start()
        return 0

    lax.fori_loop(0, slabs, final, 0)

    for i in range(1, group):
        r = at.peer(i)
        bc_piece(r, i, r).wait_recv()
    bct_copy = pltpu.make_async_copy(bcb, bct_ref, local_sem.at[3])
    bct_copy.start()
    for i in range(1, group):
        r = at.peer(i)
        main_piece(r, i).wait_send()
        small_piece(r, i).wait_send()
        bc_piece(r, i, rank).wait_send()
    norm_piece(sibling, 0).wait_send()
    for i, r in enumerate(far):
        norm_piece(r, i + 1).wait_send()
        remote(normed.at[norm_rows(r)], normed.at[norm_rows(r)], f_send.at[i], n_recv.at[r], at.member(sibling)).wait_send()

    def small_sent(j, _):
        @pl.when((z + j < planes) & at.has_down)
        def _():
            small_down(z + j, j).wait_send()

        @pl.when((z - j >= 0) & at.has_up)
        def _():
            small_up(z - j, j).wait_send()

        return 0

    lax.fori_loop(0, planes, small_sent, 0)

    def wide_sent(k, _):
        j, q = k // cut, lax.rem(k, cut)

        @pl.when((z + j < planes) & at.has_down)
        def _():
            wide_down(z + j, q, k).wait_send()

        @pl.when((z - j >= 0) & at.has_up)
        def _():
            wide_up(z - j, q, k).wait_send()

        return 0

    lax.fori_loop(0, planes * cut, wide_sent, 0)
    nall_copy.wait()
    ws_copy.wait()
    wm_copy.wait()
    bct_copy.wait()
    lax.fori_loop(0, slabs, lambda m, _: (out_copy(m).wait(), 0)[1], 0)


def gather_project(pieces, pieces_small, normed, planes, ny, ns, heads):
    group, rows, width = pieces.shape
    total = normed.shape[0] * group
    cut = 1
    while cut * 2 <= min(group, 32 // planes):
        cut *= 2
    dma = pltpu.SemaphoreType.DMA
    anywhere = pl.BlockSpec(memory_space=pl.ANY)
    return pl.pallas_call(
        functools.partial(project_kernel, planes, ny, ns, cut, heads),
        in_specs=[anywhere] * 3,
        out_specs=[anywhere, anywhere, pl.BlockSpec(memory_space=pltpu.VMEM), anywhere, anywhere, anywhere],
        out_shape=[
            jax.ShapeDtypeStruct((total, width), BF16),
            jax.ShapeDtypeStruct((2 * STATE, total), BF16),
            jax.ShapeDtypeStruct((heads, total), F32),
            jax.ShapeDtypeStruct((total, D), BF16),
            jax.ShapeDtypeStruct((D, width), BF16),
            jax.ShapeDtypeStruct((D, 128), BF16),
        ],
        scratch_shapes=[
            pltpu.VMEM((D, width), BF16),
            pltpu.VMEM((D, 128), BF16),
            pltpu.VMEM((total, D), BF16),
            pltpu.VMEM((total, width), F32),
            pltpu.VMEM((total, width), BF16),
            pltpu.VMEM((2 * STATE, total), BF16),
            dma((group,)), dma((group,)), dma((group,)), dma((group,)),
            dma((group,)), dma((group,)), dma((group,)), dma((group,)), dma((group,)),
            dma((planes * cut,)), dma((planes * cut,)), dma((planes * cut,)), dma((planes * cut,)),
            dma((planes,)), dma((planes,)), dma((planes,)), dma((planes,)),
            dma((4 + total // 256,)),
        ],
        compiler_params=pltpu.CompilerParams(
            collective_id=1, has_side_effects=True, vmem_limit_bytes=58 << 20
        ),
        name="gather_project",
    )(pieces, pieces_small, normed)


def forward_kernel(
    x_ref, gate_ref, bc_ref, bct_ref, dt_ref, wx_ref, bx_ref, bias_ref, alog_ref, skip_ref,
    scanned_ref, state_ref, state, halo,
):
    @pl.when(pl.program_id(1) == 0)
    def _():
        state[...] = jnp.zeros_like(state)
        halo[...] = jnp.zeros_like(halo)

    rows, channels = x_ref.shape
    raw = x_ref[...].astype(F32)
    conv, _ = convolved(raw, halo[...], wx_ref[...], bx_ref[...])
    halo[...] = raw[rows - 8 :]
    xs = conv / (1.0 + jnp.exp(-conv))
    _, step_t, _, run_t = head_times(dt_ref[...], bias_ref[...], alog_ref[...])
    run = run_t.T
    xdt = xs * spread(step_t.T)
    b_t = bct_ref[:STATE]
    c = bc_ref[:, STATE:]
    causal = iota((rows, rows), 0) >= iota((rows, rows), 1)
    products = jnp.where(causal, mm(c, b_t), 0.0)
    entering = state[...]
    state_ref[0] = entering
    inward = mm(c, entering) * spread(jnp.exp(run))
    skipped = skip_ref[...] * xs
    lane = iota((rows, 2 * HEADDIM), 1)
    for pair in range(channels // 128):
        cols = slice(pair * 128, pair * 128 + 128)
        part = xdt[:, cols]
        total = inward[:, cols] + skipped[:, cols]
        for side in range(2):
            h = 2 * pair + side
            decay = jnp.exp(jnp.minimum(run[:, h : h + 1] - run_t[h : h + 1], 0.0))
            own = (lane < HEADDIM) if side == 0 else (lane >= HEADDIM)
            total = total + mm(products * decay, jnp.where(own, part, 0.0))
        scanned_ref[:, cols] = total
    last = run[rows - 1 :]
    to_end = spread(jnp.exp(last - run))
    state[...] = entering * spread(jnp.exp(last)) + mm(b_t, xdt * to_end)


def backward_kernel(
    x_ref, halo_ref, gate_ref, bc_ref, bct_ref, dt_ref, wx_ref, bx_ref, bias_ref, alog_ref, skip_ref,
    gain_ref, scanned_ref, state_ref, mixed_grad_ref, norms_ref,
    grad_ref, dbc_ref, ddt_ref, sums_ref, heads_ref,
    lam, rim,
):
    step_id = pl.program_id(1)
    first = (pl.program_id(0) == 0) & (step_id == 0)

    @pl.when(first)
    def _():
        sums_ref[...] = jnp.zeros_like(sums_ref)
        heads_ref[...] = jnp.zeros_like(heads_ref)

    @pl.when(step_id == 0)
    def _():
        lam[...] = jnp.zeros_like(lam)
        rim[...] = jnp.zeros_like(rim)

    rows, channels = x_ref.shape
    heads = channels // HEADDIM
    gate = gate_ref[...].astype(F32)
    scanned = scanned_ref[...]
    mixed_grad = mixed_grad_ref[...].astype(F32)
    norms = norms_ref[...].T
    r = norms[:, 0:1]
    inner = norms[:, 1:2]
    sig = 1.0 / (1.0 + jnp.exp(-gate))
    silu = gate * sig
    product = scanned * silu
    product_grad = r * (mixed_grad * gain_ref[...]) - product * (r * r * r * inner)
    sums_ref[5:6] += jnp.sum(mixed_grad * product * r, 0, keepdims=True)
    dy = product_grad * silu
    grad_ref[:, :channels] = (product_grad * scanned * (sig * (1.0 + gate * (1.0 - sig)))).astype(BF16)

    raw = x_ref[...].astype(F32)
    before = jnp.where(step_id == pl.num_programs(1) - 1, 0.0, halo_ref[...].astype(F32))
    conv, shifted = convolved(raw, before, wx_ref[...], bx_ref[...])
    sig_c = 1.0 / (1.0 + jnp.exp(-conv))
    xs = conv * sig_c
    sums_ref[6:7] += jnp.sum(dy * xs, 0, keepdims=True)
    pre, step_t, decay_t, run_t = head_times(dt_ref[...], bias_ref[...], alog_ref[...])
    run = run_t.T
    step = spread(step_t.T)
    xdt = xs * step
    b = bc_ref[:, :STATE]
    c = bc_ref[:, STATE:]
    b_t = bct_ref[:STATE]
    c_t = bct_ref[STATE:]
    causal = iota((rows, rows), 0) >= iota((rows, rows), 1)
    products = jnp.where(causal, mm(c, b_t), 0.0)
    entering = state_ref[0]
    leaving = lam[...]
    last = run[rows - 1 :]
    to_end = spread(jnp.exp(last - run))
    whole = spread(jnp.exp(last))
    dye = dy * spread(jnp.exp(run))
    xend = xdt * to_end
    inward = dye * mm(c, entering)
    outward_grad = mm(b, leaving) * to_end
    outward = outward_grad * xdt
    dc_t = mm_last(entering, dye)
    db_t = mm_last(leaving, xend)
    kept = leaving * whole
    lam[...] = kept + mm(c_t, dye)

    dy_t = dy.T.astype(BF16)
    lane = iota((rows, 2 * HEADDIM), 1)
    wide = iota((rows, heads), 1)
    dproducts = jnp.zeros((rows, rows), F32)
    row_sums = jnp.zeros((rows, heads), F32)
    col_sums = []
    dxdt_t = []
    for h in range(heads):
        cols = slice((h // 2) * 128, (h // 2) * 128 + 128)
        own = (lane < HEADDIM) if h % 2 == 0 else (lane >= HEADDIM)
        decay = jnp.exp(jnp.minimum(run[:, h : h + 1] - run_t[h : h + 1], 0.0))
        weights = products * decay
        dweights = mm_last(dy[:, cols], jnp.where(own, xdt[:, cols], 0.0))
        dproducts = dproducts + dweights * decay
        shares = dweights * weights
        row_sums = jnp.where(wide == h, jnp.sum(shares, 1, keepdims=True), row_sums)
        col_sums.append(jnp.sum(shares, 0, keepdims=True))
        dxdt_t.append(mm(dy_t[h * HEADDIM : (h + 1) * HEADDIM], weights))
    dproducts = jnp.where(causal, dproducts, 0.0)
    dc_t = dc_t + mm_last(b_t, dproducts)
    db_t = db_t + mm(c_t, dproducts)
    dbc_ref[:STATE] = db_t
    dbc_ref[STATE:] = dc_t
    dxdt = jnp.concatenate(dxdt_t, 0).T + outward_grad

    member = (iota((heads, channels), 1) // HEADDIM == iota((heads, channels), 0)).astype(F32)

    def per_head(values):
        return lax.dot_general(
            member, values, (((1,), (1,)), ((), ())), precision=HIGH, preferred_element_type=F32
        )

    out_t = per_head(outward)
    run_grad = per_head(inward) - out_t + row_sums.T - jnp.concatenate(col_sums, 0)
    at_end = jnp.sum(out_t, 1, keepdims=True) + jnp.sum(per_head(kept * entering), 1, keepdims=True)
    lower = (iota((rows, rows), 0) >= iota((rows, rows), 1)).astype(F32)
    decay_grad = at_end + jnp.dot(run_grad, lower, precision=HIGH, preferred_element_type=F32)
    step_grad = per_head(dxdt * xs) - jnp.exp(alog_ref[...]) * decay_grad
    dt_grad = step_grad / (1.0 + jnp.exp(-pre))
    ddt_ref[...] = dt_grad.astype(BF16)
    heads_ref[:, 0:1] += jnp.sum(dt_grad, 1, keepdims=True)
    heads_ref[:, 1:2] += jnp.sum(decay_grad * decay_t, 1, keepdims=True)

    dx = dxdt * step + skip_ref[...] * dy
    dconv = dx * (sig_c * (1.0 + conv * (1.0 - sig_c)))
    sums_ref[4:5] += jnp.sum(dconv, 0, keepdims=True)
    for k in range(KERNEL):
        sums_ref[k : k + 1] += jnp.sum(dconv * shifted[k], 0, keepdims=True)
    joined = jnp.concatenate([dconv, rim[...]], 0)
    rim[...] = dconv[:8]
    dx_in = wx_ref[KERNEL - 1 : KERNEL] * dconv
    for k in range(KERNEL - 1):
        ahead = KERNEL - 1 - k
        dx_in = dx_in + wx_ref[k : k + 1] * joined[ahead : ahead + rows]
    grad_ref[:, channels:] = dx_in.astype(BF16)


def whole_spec(array):
    return pl.BlockSpec(array.shape, lambda q, i: (0,) * array.ndim)


def scan_forward(projected, bc, bc_t, dt_t, params, seqs):
    total, channels = projected.shape[0], projected.shape[1] // 2
    heads = channels // HEADDIM
    steps = total // seqs // STRETCH
    row = lambda q, i: q * steps + i
    return pl.pallas_call(
        forward_kernel,
        grid=(seqs, steps),
        in_specs=[
            pl.BlockSpec((STRETCH, channels), lambda q, i: (row(q, i), 1)),
            pl.BlockSpec((STRETCH, channels), lambda q, i: (row(q, i), 0)),
            pl.BlockSpec((STRETCH, 2 * STATE), lambda q, i: (row(q, i), 0)),
            pl.BlockSpec((2 * STATE, STRETCH), lambda q, i: (0, row(q, i))),
            pl.BlockSpec((heads, STRETCH), lambda q, i: (0, row(q, i))),
        ]
        + [whole_spec(p) for p in params],
        out_specs=[
            pl.BlockSpec((STRETCH, channels), lambda q, i: (row(q, i), 0)),
            pl.BlockSpec((1, STATE, channels), lambda q, i: (row(q, i), 0, 0)),
        ],
        out_shape=[
            jax.ShapeDtypeStruct((total, channels), F32),
            jax.ShapeDtypeStruct((seqs * steps, STATE, channels), F32),
        ],
        scratch_shapes=[pltpu.VMEM((STATE, channels), F32), pltpu.VMEM((8, channels), F32)],
        compiler_params=pltpu.CompilerParams(vmem_limit_bytes=48 << 20),
        name="scan_forward",
    )(projected, projected, bc, bc_t, dt_t, *params)


def scan_backward(projected, bc, bc_t, dt_t, params, gain, scanned, states, mixed_grad, norms, seqs):
    total, channels = projected.shape[0], projected.shape[1] // 2
    heads = channels // HEADDIM
    steps = total // seqs // STRETCH
    row = lambda q, i: q * steps + steps - 1 - i
    halo_row = lambda q, i: jnp.maximum(row(q, i) * (STRETCH // 16) - 1, 0)
    return pl.pallas_call(
        backward_kernel,
        grid=(seqs, steps),
        in_specs=[
            pl.BlockSpec((STRETCH, channels), lambda q, i: (row(q, i), 1)),
            pl.BlockSpec((16, channels), lambda q, i: (halo_row(q, i), 1)),
            pl.BlockSpec((STRETCH, channels), lambda q, i: (row(q, i), 0)),
            pl.BlockSpec((STRETCH, 2 * STATE), lambda q, i: (row(q, i), 0)),
            pl.BlockSpec((2 * STATE, STRETCH), lambda q, i: (0, row(q, i))),
            pl.BlockSpec((heads, STRETCH), lambda q, i: (0, row(q, i))),
        ]
        + [whole_spec(p) for p in params]
        + [
            whole_spec(gain),
            pl.BlockSpec((STRETCH, channels), lambda q, i: (row(q, i), 0)),
            pl.BlockSpec((1, STATE, channels), lambda q, i: (row(q, i), 0, 0)),
            pl.BlockSpec((STRETCH, channels), lambda q, i: (row(q, i), 0)),
            pl.BlockSpec((8, STRETCH), lambda q, i: (0, row(q, i))),
        ],
        out_specs=[
            pl.BlockSpec((STRETCH, 2 * channels), lambda q, i: (row(q, i), 0)),
            pl.BlockSpec((2 * STATE, STRETCH), lambda q, i: (0, row(q, i))),
            pl.BlockSpec((heads, STRETCH), lambda q, i: (0, row(q, i))),
            pl.BlockSpec((8, channels), lambda q, i: (0, 0)),
            pl.BlockSpec((heads, 128), lambda q, i: (0, 0)),
        ],
        out_shape=[
            jax.ShapeDtypeStruct((total, 2 * channels), BF16),
            jax.ShapeDtypeStruct((2 * STATE, total), F32),
            jax.ShapeDtypeStruct((heads, total), BF16),
            jax.ShapeDtypeStruct((8, channels), F32),
            jax.ShapeDtypeStruct((heads, 128), F32),
        ],
        scratch_shapes=[pltpu.VMEM((STATE, channels), F32), pltpu.VMEM((8, channels), F32)],
        compiler_params=pltpu.CompilerParams(vmem_limit_bytes=56 << 20),
        name="scan_backward",
    )(projected, projected, projected, bc, bc_t, dt_t, *params, gain, scanned, states, mixed_grad, norms)


def shift_later(values, by, seqs):
    if by == 0:
        return values
    split = values.reshape(values.shape[0], seqs, -1)
    moved = jnp.pad(split, ((0, 0), (0, 0), (by, 0)))[:, :, : split.shape[2]]
    return moved.reshape(values.shape)


def shift_earlier(values, by, seqs):
    if by == 0:
        return values
    split = values.reshape(values.shape[0], seqs, -1)
    moved = jnp.pad(split, ((0, 0), (0, 0), (0, by)))[:, :, by:]
    return moved.reshape(values.shape)


class Layout:
    def __init__(self, planes, group, rows_out):
        self.planes, self.group = planes, group
        self.aligned = rows_out % HEADDIM == 0
        self.blocks = planes if self.aligned else 1
        self.block = INNER // group // self.blocks
        self.heads = HEADS // group
        self.channels = INNER // group
        self.small = 2 * STATE // group

    def pieces(self, values, unit):
        rows = values.shape[0]
        parts = values.reshape(rows, self.blocks, self.group, self.block // HEADDIM * unit)
        return parts.transpose(0, 2, 1, 3).reshape(rows, self.group, -1)

    def joined(self, values, unit):
        rows = values.shape[0]
        parts = values.reshape(rows, self.group, self.blocks, self.block // HEADDIM * unit)
        return parts.transpose(0, 2, 1, 3).reshape(rows, -1)

    def columns(self, w):
        gate = self.pieces(w[:, :INNER], HEADDIM)
        x = self.pieces(w[:, INNER : 2 * INNER], HEADDIM)
        bc = w[:, 2 * INNER : INNER + CHANNELS].reshape(w.shape[0], self.group, self.small)
        dt = self.pieces(w[:, INNER + CHANNELS :], 1)
        return jnp.concatenate([gate, x, bc, dt], 2)

    def uncolumns(self, g):
        c, s = self.channels, self.small
        gate = self.joined(g[:, :, :c], HEADDIM)
        x = self.joined(g[:, :, c : 2 * c], HEADDIM)
        bc = g[:, :, 2 * c : 2 * c + s].reshape(g.shape[0], -1)
        dt = self.joined(g[:, :, 2 * c + s :], 1)
        return jnp.concatenate([gate, x, bc, dt], 1)


def body(
    tokens, cotangent, lengths, norm_gain, w_in, conv_w, conv_b, dt_bias, a_log, skip_scale, gate_gain, w_out,
):
    row_count = tokens.shape[1]
    planes, group = lax.axis_size("z"), lax.axis_size("y") * lax.axis_size("seq")
    seqs = lax.axis_size("y")
    rank = lax.axis_index("y") * lax.axis_size("seq") + lax.axis_index("seq")
    lay = Layout(planes, group, w_out.shape[0])
    channels, small = lay.channels, lay.small
    inputs = tokens.reshape(row_count, D).astype(F32)
    position = lax.axis_index("seq") * row_count + jnp.arange(row_count, dtype=jnp.int32)
    valid_mask = (position < lengths[0]).astype(F32)[:, None]
    rms = lax.rsqrt(jnp.mean(inputs * inputs, -1, keepdims=True) + EPSILON)
    normed = (inputs * rms * norm_gain).astype(BF16)
    masked_cot = cotangent.reshape(row_count, D).astype(F32) * valid_mask
    branch_grad = masked_cot.astype(BF16)

    columns = lay.columns(w_in.astype(BF16)).transpose(1, 0, 2)
    pieces = columns[:, :, : 2 * channels]
    pieces_small = jnp.pad(columns[:, :, 2 * channels :], ((0, 0), (0, 0), (0, 128 - small - lay.heads)))
    if lay.aligned:
        out_own = lax.all_gather(w_out.astype(BF16), "z", axis=0, tiled=True)
    else:
        out_all = lax.all_gather(w_out.astype(BF16), ("z",) + GROUP, axis=0, tiled=True)
        out_own = lax.dynamic_slice_in_dim(out_all, rank * channels, channels, 0)

    def own(values, unit):
        return lax.dynamic_index_in_dim(lay.pieces(values, unit), rank, 1, keepdims=False)

    conv_wx = own(conv_w[:INNER].T, HEADDIM)
    conv_bx = own(conv_b[None, :INNER], HEADDIM)
    bias_own = own(dt_bias[None], 1).T
    a_own = own(a_log[None], 1).T
    skip_own = jnp.repeat(own(skip_scale[None], 1), HEADDIM, 1)
    gain_own = own(gate_gain[None], HEADDIM)
    params = (conv_wx, conv_bx, bias_own, a_own, skip_own)

    projected, bc_raw, dt_t, normed_all, w_main, w_small = gather_project(
        pieces, pieces_small, normed, planes, lax.axis_size("y"), lax.axis_size("seq"), lay.heads
    )
    w_small = w_small[:, : small + lay.heads]
    bc_in = bc_raw.astype(F32)
    conv_bc = conv_b[INNER:, None]
    for k in range(KERNEL):
        conv_bc = conv_bc + conv_w[INNER:, k : k + 1] * shift_later(bc_in, KERNEL - 1 - k, seqs)
    bc_t = jax.nn.silu(conv_bc).astype(BF16)
    bc = bc_t.T

    scanned, states = scan_forward(projected, bc, bc_t, dt_t, params, seqs)

    grad_all = lax.all_gather(branch_grad, GROUP, axis=0, tiled=True)
    mixed_grad = lax.dot_general(
        grad_all, out_own, (((1,), (1,)), ((), ())), preferred_element_type=F32
    )
    product = scanned * jax.nn.silu(projected[:, :channels].astype(F32))
    sums = lax.psum(
        jnp.stack([jnp.sum(product * product, 1), jnp.sum(mixed_grad * gain_own * product, 1)]), GROUP
    )
    r = lax.rsqrt(sums[0] / INNER + EPSILON)
    norms = jnp.concatenate([r[None], sums[1:] / INNER, jnp.zeros((6, r.shape[0]), F32)], 0)
    mixed = (product * r[:, None] * gain_own).astype(BF16)

    branch = lax.psum_scatter(
        jnp.dot(mixed, out_own, preferred_element_type=F32).astype(BF16),
        GROUP, scatter_dimension=0, tiled=True,
    ).astype(F32)
    output = (valid_mask * (inputs + branch)).astype(BF16)
    out_part = lax.dot_general(
        mixed, grad_all, (((0,), (0,)), ((), ())), preferred_element_type=F32
    ).astype(BF16)
    if lay.aligned:
        grad_w_out = lax.psum_scatter(out_part, "z", scatter_dimension=0, tiled=True).astype(F32)
    else:
        placed = lax.dynamic_update_slice_in_dim(jnp.zeros((INNER, D), BF16), out_part, rank * channels, 0)
        grad_w_out = lax.psum_scatter(placed, ("z",) + GROUP, scatter_dimension=0, tiled=True).astype(F32)

    proj_grad, dbc_t, ddt_t, sums_x, sums_h = scan_backward(
        projected, bc, bc_t, dt_t, params, gain_own, scanned, states, mixed_grad, norms, seqs
    )
    dbc = lax.psum_scatter(dbc_t, GROUP, scatter_dimension=0, tiled=True)
    own_rows = lambda v: lax.dynamic_slice_in_dim(v, rank * small, small, 0)
    conv_own, in_own, w_bc = own_rows(conv_bc), own_rows(bc_in), own_rows(conv_w[INNER:])
    sig = jax.nn.sigmoid(conv_own)
    dconv = dbc * sig * (1.0 + conv_own * (1.0 - sig))
    din = 0.0
    grad_w_bc = []
    for k in range(KERNEL):
        grad_w_bc.append(jnp.sum(dconv * shift_later(in_own, KERNEL - 1 - k, seqs), 1))
        din = din + w_bc[:, k : k + 1] * shift_earlier(dconv, KERNEL - 1 - k, seqs)
    small_grad_t = jnp.concatenate([din.astype(BF16), ddt_t], 0)

    contract_rows = (((0,), (0,)), ((), ()))
    in_main = lax.dot_general(normed_all, proj_grad, contract_rows, preferred_element_type=F32)
    in_small = lax.dot_general(
        normed_all, small_grad_t, (((0,), (1,)), ((), ())), preferred_element_type=F32
    )
    in_part = jnp.concatenate([in_main.astype(BF16), in_small.astype(BF16)], 1)
    in_rows = lax.psum_scatter(in_part, "z", scatter_dimension=0, tiled=True)
    in_pieces = lax.all_to_all(in_rows, GROUP, split_axis=0, concat_axis=1, tiled=True)
    grad_w_in = lay.uncolumns(in_pieces.reshape(w_in.shape[0], group, -1).astype(F32))

    normed_part = lax.dot_general(
        proj_grad, w_main, (((1,), (1,)), ((), ())), preferred_element_type=F32
    ) + lax.dot_general(small_grad_t, w_small, (((0,), (1,)), ((), ())), preferred_element_type=F32)
    normed_grad = lax.psum_scatter(
        normed_part.astype(BF16), GROUP, scatter_dimension=0, tiled=True
    ).astype(F32)
    g = normed_grad * norm_gain
    input_grad = masked_cot + rms * g - inputs * (rms ** 3 * jnp.mean(g * inputs, -1, keepdims=True))
    norm_gain_grad = jnp.sum(normed_grad * inputs * rms, 0)

    own_sums = jnp.concatenate(
        [
            sums_x[: KERNEL + 2].reshape(-1),
            jnp.sum(sums_x[KERNEL + 2].reshape(-1, HEADDIM), 1),
            sums_h[:, 0],
            sums_h[:, 1],
            jnp.stack(grad_w_bc).reshape(-1),
            jnp.sum(dconv, 1),
        ]
    )
    count = own_sums.shape[0]
    everyone = lax.all_gather(jnp.concatenate([own_sums, norm_gain_grad]), ("z",) + GROUP)
    grad_norm_gain = jnp.sum(everyone[:, count:], 0)
    by_rank = jnp.sum(everyone[:, :count].reshape(planes, group, count), 0)
    at = 0

    def take(size):
        nonlocal at
        at += size
        return by_rank[:, at - size : at]

    taken_x = take((KERNEL + 2) * channels).reshape(group, KERNEL + 2, channels).transpose(1, 0, 2)
    full_x = lay.joined(taken_x, HEADDIM)
    grad_skip, grad_bias, grad_a = (
        lay.joined(take(lay.heads)[None], 1)[0] for _ in range(3)
    )
    conv_w_bc = take(KERNEL * small).reshape(group, KERNEL, small).transpose(1, 0, 2).reshape(KERNEL, -1)
    conv_b_bc = take(small).reshape(-1)
    grad_conv_w = jnp.concatenate([full_x[:KERNEL], conv_w_bc], 1).T
    grad_conv_b = jnp.concatenate([full_x[KERNEL], conv_b_bc])
    return (
        output.reshape(tokens.shape),
        input_grad.reshape(1, row_count, D),
        grad_norm_gain,
        grad_w_in,
        grad_conv_w,
        grad_conv_b,
        grad_bias,
        grad_a,
        grad_skip,
        full_x[KERNEL + 1],
        grad_w_out,
    )


def solution(mesh):
    dp, seq = mesh.shape["dp"], mesh.shape["seq"]
    inner_mesh = Mesh(mesh.devices.reshape(dp // 2, 2, seq), ("z", "y", "seq"))
    placed = P(("z", "y"), "seq", None)
    rows = P(("z", "y", "seq"), None)
    in_specs = (placed, placed, P(("z", "y")), P(), rows, P(), P(), P(), P(), P(), P(), rows)
    out_specs = (placed, placed, P(), rows, P(), P(), P(), P(), P(), P(), rows)
    return jax.shard_map(body, mesh=inner_mesh, in_specs=in_specs, out_specs=out_specs, check_vma=False)
```

```python
import functools

import jax
import jax.numpy as jnp
from jax import lax
from jax.experimental import pallas as pl
from jax.experimental.pallas import tpu as pltpu
from jax.sharding import Mesh
from jax.sharding import PartitionSpec as P

D = 2048
HEADS = 64
HEADDIM = 64
STATE = 128
KERNEL = 4
STRETCH = 256
INNER = 4096
CHANNELS = 4352
EPSILON = 1e-05
HIGH = lax.Precision.HIGHEST
BF16 = jnp.bfloat16
F32 = jnp.float32
GROUP = ("y", "seq")


def mm(a, b):
    return jnp.dot(a.astype(BF16), b.astype(BF16), preferred_element_type=F32)


def mm_last(a, b):
    return lax.dot_general(
        a.astype(BF16), b.astype(BF16), (((1,), (1,)), ((), ())), preferred_element_type=F32
    )


def iota(shape, axis):
    return lax.broadcasted_iota(jnp.int32, shape, axis)


def head_times(raw, bias, a_log):
    pre = raw + bias
    step = jnp.maximum(pre, 0.0) + jnp.log1p(jnp.exp(-jnp.abs(pre)))
    log_decay = step * -jnp.exp(a_log)
    width = raw.shape[1]
    upper = (iota((width, width), 0) <= iota((width, width), 1)).astype(F32)
    running = jnp.dot(log_decay, upper, precision=HIGH, preferred_element_type=F32)
    return pre, step, log_decay, running


def over_channels(values, pair):
    left = values[:, 2 * pair : 2 * pair + 1]
    right = values[:, 2 * pair + 1 : 2 * pair + 2]
    lane = iota((values.shape[0], 2 * HEADDIM), 1)
    return jnp.where(lane < HEADDIM, left, right)


def spread(values):
    pairs = values.shape[1] // 2
    return jnp.concatenate([over_channels(values, i) for i in range(pairs)], axis=1)


def convolved(block, halo, conv_w, conv_b):
    rows = block.shape[0]
    joined = jnp.concatenate([halo, block], axis=0)
    base = halo.shape[0] - KERNEL + 1
    shifted = [joined[base + k : base + k + rows] for k in range(KERNEL)]
    total = conv_b
    for k in range(KERNEL):
        total = total + conv_w[k : k + 1] * shifted[k]
    return total, shifted


MESH = pl.DeviceIdType.MESH


def remote(src, dst, send_sem, recv_sem, device):
    return pltpu.make_async_remote_copy(
        src_ref=src, dst_ref=dst, send_sem=send_sem, recv_sem=recv_sem,
        device_id=device, device_id_type=MESH,
    )


class Place:
    def __init__(self, planes, ny, ns):
        self.planes, self.ny, self.ns, self.group = planes, ny, ns, ny * ns
        self.z, self.y, self.s = lax.axis_index("z"), lax.axis_index("y"), lax.axis_index("seq")
        self.rank = self.y * ns + self.s
        self.up, self.down = (self.z + 1, self.y, self.s), (self.z - 1, self.y, self.s)
        self.has_up, self.has_down = self.z < planes - 1, self.z > 0

    def member(self, rank):
        return (self.z, rank // self.ns, lax.rem(rank, self.ns))

    def peer(self, i):
        return lax.rem(self.rank + i, self.group)

    def far(self):
        chips = self.ns // 2
        x, core = self.s // 2, lax.rem(self.s, 2)
        for dy in range(self.ny):
            for dx in range(chips):
                if dy or dx:
                    yield lax.rem(self.y + dy, self.ny) * self.ns + lax.rem(x + dx, chips) * 2 + core

    def sibling(self, rank):
        return rank + 1 - 2 * lax.rem(rank, 2)

    def greet(self):
        barrier = pltpu.get_barrier_semaphore()
        for i in range(1, self.group):
            pl.semaphore_signal(barrier, inc=1, device_id=self.member(self.peer(i)), device_id_type=MESH)

        @pl.when(self.has_up)
        def _():
            pl.semaphore_signal(barrier, inc=1, device_id=self.up, device_id_type=MESH)

        @pl.when(self.has_down)
        def _():
            pl.semaphore_signal(barrier, inc=1, device_id=self.down, device_id_type=MESH)

        count = self.group - 1 + self.has_up.astype(jnp.int32) + self.has_down.astype(jnp.int32)
        pl.semaphore_wait(barrier, count)


def project_kernel(
    planes, ny, ns, cut, heads,
    pm_ref, ps_ref, nm_ref,
    proj_ref, bct_ref, dt_ref, nt_ref, wm_ref, ws_ref,
    wmain, wsmall, normed, acc, outb, bcb, turned,
    am_send, am_recv, as_send, as_recv, n_send, n_recv, f_send, b_send, b_recv,
    up_send, up_recv, down_send, down_recv, sup_send, sup_recv, sdown_send, sdown_recv, local_sem, turn_sem,
):
    at = Place(planes, ny, ns)
    group, rank, z = at.group, at.rank, at.z
    piece = pm_ref.shape[1]
    plane_rows = piece * group
    total, slab = normed.shape[0], 256
    own_rows = nm_ref.shape[0]
    small = bcb.shape[0] // group
    part = plane_rows // cut

    def rows_of(r):
        return pl.ds(pl.multiple_of(z * plane_rows + r * piece, piece), piece)

    def block_rows(p, q):
        return pl.ds(pl.multiple_of(p * plane_rows + q * part, part), part)

    def plane_block(p):
        return pl.ds(pl.multiple_of(p * plane_rows, plane_rows), plane_rows)

    def norm_rows(r):
        return pl.ds(pl.multiple_of(r * own_rows, own_rows), own_rows)

    own_copies = [
        pltpu.make_async_copy(pm_ref.at[rank], wmain.at[rows_of(rank)], local_sem.at[0]),
        pltpu.make_async_copy(ps_ref.at[rank], wsmall.at[rows_of(rank)], local_sem.at[1]),
        pltpu.make_async_copy(nm_ref, normed.at[norm_rows(rank)], local_sem.at[2]),
    ]
    for copy in own_copies:
        copy.start()
    at.greet()

    def main_piece(r, i):
        return remote(pm_ref.at[r], wmain.at[rows_of(rank)], am_send.at[i], am_recv.at[rank], at.member(r))

    def small_piece(r, i):
        return remote(ps_ref.at[r], wsmall.at[rows_of(rank)], as_send.at[i], as_recv.at[rank], at.member(r))

    def norm_piece(r, i):
        return remote(nm_ref, normed.at[norm_rows(rank)], n_send.at[i], n_recv.at[rank], at.member(r))

    for i in range(1, group):
        small_piece(at.peer(i), i).start()
    for i in range(1, group):
        main_piece(at.peer(i), i).start()
    far = list(at.far())
    sibling = at.sibling(rank)
    norm_piece(sibling, 0).start()
    for i, r in enumerate(far):
        norm_piece(r, i + 1).start()
    acc[...] = jnp.zeros_like(acc)
    for copy in own_copies:
        copy.wait()

    for i in range(1, group):
        r = at.peer(i)
        remote(ps_ref.at[r], wsmall.at[rows_of(r)], as_send.at[i], as_recv.at[r], at.member(r)).wait_recv()

    def small_up(p, j):
        return remote(wsmall.at[plane_block(p)], wsmall.at[plane_block(p)], sup_send.at[j], sup_recv.at[j], at.up)

    def small_down(p, j):
        return remote(wsmall.at[plane_block(p)], wsmall.at[plane_block(p)], sdown_send.at[j], sdown_recv.at[j], at.down)

    def wide_up(p, q, k):
        return remote(wmain.at[block_rows(p, q)], wmain.at[block_rows(p, q)], up_send.at[k], up_recv.at[k], at.up)

    def wide_down(p, q, k):
        return remote(wmain.at[block_rows(p, q)], wmain.at[block_rows(p, q)], down_send.at[k], down_recv.at[k], at.down)

    def each_way(p, above, fn_up, fn_down):
        @pl.when(at.has_up & jnp.logical_not(above))
        def _():
            fn_up()

        @pl.when(at.has_down & above)
        def _():
            fn_down()

    @pl.when(at.has_up)
    def _():
        small_up(z, 0).start()

    @pl.when(at.has_down)
    def _():
        small_down(z, 0).start()

    ranks_in = group // cut
    for q in range(cut):
        for r in range(q * ranks_in, (q + 1) * ranks_in):
            @pl.when(rank != r)
            def _():
                remote(pm_ref.at[r], wmain.at[rows_of(r)], am_send.at[0], am_recv.at[r], at.member(r)).wait_recv()

        @pl.when(at.has_up)
        def _():
            wide_up(z, q, q).start()

        @pl.when(at.has_down)
        def _():
            wide_down(z, q, q).start()

    def small_step(j, _):
        @pl.when(z + j < planes)
        def _():
            small_down(z + j, j - 1).wait_recv()

            @pl.when(at.has_down)
            def _():
                small_down(z + j, j).start()

        @pl.when(z - j >= 0)
        def _():
            small_up(z - j, j - 1).wait_recv()

            @pl.when(at.has_up)
            def _():
                small_up(z - j, j).start()

        return 0

    lax.fori_loop(1, planes, small_step, 0)

    def relay(i, r):
        norm_piece_in = remote(nm_ref, normed.at[norm_rows(r)], n_send.at[i + 1], n_recv.at[r], at.member(r))
        norm_piece_in.wait_recv()
        remote(normed.at[norm_rows(r)], normed.at[norm_rows(r)], f_send.at[i], n_recv.at[r], at.member(sibling)).start()

    def norm_done():
        for r in [sibling] + [at.sibling(r) for r in far]:
            remote(nm_ref, normed.at[norm_rows(r)], n_send.at[0], n_recv.at[r], at.member(sibling)).wait_recv()

    def plane_in_turn(j):
        return lax.rem(jnp.where(2 * z < planes, z + j, z - j + planes), planes)

    slabs = total // slab

    def product(index):
        j, m = index // slabs, lax.rem(index, slabs)
        p = plane_in_turn(j)
        rows = pl.ds(pl.multiple_of(m * slab, slab), slab)
        lanes = pl.ds(pl.multiple_of(p * plane_rows, 128), plane_rows)
        return rows, acc[rows, :] + jnp.dot(
            normed[rows, lanes], wmain[plane_block(p), :], preferred_element_type=F32
        )

    def narrow(m, _):
        rows = pl.ds(pl.multiple_of(m * slab, slab), slab)
        value = jnp.dot(normed[rows, :], wsmall[...], preferred_element_type=F32).T
        bcb[pl.ds(pl.multiple_of(rank * small, small), small), rows] = value[:small].astype(BF16)
        dt_ref[:, rows] = value[small : small + heads].astype(BF16).astype(F32)
        return 0

    def bc_piece(r, i, owner):
        rows = pl.ds(pl.multiple_of(owner * small, small), small)
        return remote(bcb.at[rows], bcb.at[rows], b_send.at[i], b_recv.at[owner], at.member(r))

    steps = (planes - 1) * cut
    busy = (planes - 2) * cut
    per_step = -(-(planes - 1) * slabs // cut)

    def wide_step(k, _):
        j, q = k // cut + 1, lax.rem(k, cut)

        @pl.when(z + j < planes)
        def _():
            wide_down(z + j, q, k).wait_recv()

            @pl.when(at.has_down)
            def _():
                wide_down(z + j, q, k + cut).start()

        @pl.when(z - j >= 0)
        def _():
            wide_up(z - j, q, k).wait_recv()

            @pl.when(at.has_up)
            def _():
                wide_up(z - j, q, k + cut).start()

        return 0

    marks = [cut + i * max(busy - cut, 0) // len(far) for i in range(len(far))]
    last = 0
    for i, r in enumerate(far):
        lax.fori_loop(last, marks[i], wide_step, 0)
        last = marks[i]
        relay(i, r)
    lax.fori_loop(last, busy, wide_step, 0)
    norm_done()
    lax.fori_loop(0, slabs, narrow, 0)
    for i in range(1, group):
        bc_piece(at.peer(i), i, rank).start()

    def turn_copy(m):
        rows = pl.ds(pl.multiple_of(m * slab, slab), slab)
        return pltpu.make_async_copy(turned.at[lax.rem(m, 2)], nt_ref.at[:, rows], turn_sem.at[lax.rem(m, 2)])

    def turn(m):
        @pl.when(m >= 2)
        def _():
            turn_copy(m - 2).wait()

        rows = pl.ds(pl.multiple_of(m * slab, slab), slab)
        turned[lax.rem(m, 2)] = normed[rows, :].T
        turn_copy(m).start()

    ws_copy = pltpu.make_async_copy(wsmall, ws_ref, local_sem.at[1])
    ws_copy.start()

    def busy_step(k, _):
        wide_step(k, 0)

        def one(i, _):
            rows, value = product(jnp.minimum((k - busy) * per_step + i, (planes - 1) * slabs))

            @pl.when((k - busy) * per_step + i < (planes - 1) * slabs)
            def _():
                acc[rows, :] = value

            return 0

        lax.fori_loop(0, per_step, one, 0)

        def other(i, _):
            @pl.when((k - busy) * turns + i < slabs)
            def _():
                turn((k - busy) * turns + i)

            return 0

        lax.fori_loop(0, turns, other, 0)
        return 0

    turns = -(-slabs // cut)
    lax.fori_loop(busy, steps, busy_step, 0)
    wm_copy = pltpu.make_async_copy(wmain, wm_ref, local_sem.at[2])
    wm_copy.start()

    def out_copy(m):
        rows = pl.ds(pl.multiple_of(m * slab, slab), slab)
        return pltpu.make_async_copy(outb.at[rows], proj_ref.at[rows], local_sem.at[4 + m])

    def final(m, _):
        rows, value = product((planes - 1) * slabs + m)
        outb[rows, :] = value.astype(BF16)
        out_copy(m).start()
        return 0

    lax.fori_loop(0, slabs, final, 0)

    for i in range(1, group):
        r = at.peer(i)
        bc_piece(r, i, r).wait_recv()
    bct_copy = pltpu.make_async_copy(bcb, bct_ref, local_sem.at[3])
    bct_copy.start()
    for i in range(1, group):
        r = at.peer(i)
        main_piece(r, i).wait_send()
        small_piece(r, i).wait_send()
        bc_piece(r, i, rank).wait_send()
    norm_piece(sibling, 0).wait_send()
    for i, r in enumerate(far):
        norm_piece(r, i + 1).wait_send()
        remote(normed.at[norm_rows(r)], normed.at[norm_rows(r)], f_send.at[i], n_recv.at[r], at.member(sibling)).wait_send()

    def small_sent(j, _):
        @pl.when((z + j < planes) & at.has_down)
        def _():
            small_down(z + j, j).wait_send()

        @pl.when((z - j >= 0) & at.has_up)
        def _():
            small_up(z - j, j).wait_send()

        return 0

    lax.fori_loop(0, planes, small_sent, 0)

    def wide_sent(k, _):
        j, q = k // cut, lax.rem(k, cut)

        @pl.when((z + j < planes) & at.has_down)
        def _():
            wide_down(z + j, q, k).wait_send()

        @pl.when((z - j >= 0) & at.has_up)
        def _():
            wide_up(z - j, q, k).wait_send()

        return 0

    lax.fori_loop(0, planes * cut, wide_sent, 0)
    turn_copy(slabs - 2).wait()
    turn_copy(slabs - 1).wait()
    ws_copy.wait()
    wm_copy.wait()
    bct_copy.wait()
    lax.fori_loop(0, slabs, lambda m, _: (out_copy(m).wait(), 0)[1], 0)


def gather_project(pieces, pieces_small, normed, planes, ny, ns, heads):
    group, rows, width = pieces.shape
    total = normed.shape[0] * group
    cut = 1
    while cut * 2 <= min(group, 32 // planes):
        cut *= 2
    dma = pltpu.SemaphoreType.DMA
    anywhere = pl.BlockSpec(memory_space=pl.ANY)
    return pl.pallas_call(
        functools.partial(project_kernel, planes, ny, ns, cut, heads),
        in_specs=[anywhere] * 3,
        out_specs=[anywhere, anywhere, pl.BlockSpec(memory_space=pltpu.VMEM), anywhere, anywhere, anywhere],
        out_shape=[
            jax.ShapeDtypeStruct((total, width), BF16),
            jax.ShapeDtypeStruct((2 * STATE, total), BF16),
            jax.ShapeDtypeStruct((heads, total), F32),
            jax.ShapeDtypeStruct((D, total), BF16),
            jax.ShapeDtypeStruct((D, width), BF16),
            jax.ShapeDtypeStruct((D, 128), BF16),
        ],
        scratch_shapes=[
            pltpu.VMEM((D, width), BF16),
            pltpu.VMEM((D, 128), BF16),
            pltpu.VMEM((total, D), BF16),
            pltpu.VMEM((total, width), F32),
            pltpu.VMEM((total, width), BF16),
            pltpu.VMEM((2 * STATE, total), BF16),
            pltpu.VMEM((2, D, 256), BF16),
            dma((group,)), dma((group,)), dma((group,)), dma((group,)),
            dma((group,)), dma((group,)), dma((group,)), dma((group,)), dma((group,)),
            dma((planes * cut,)), dma((planes * cut,)), dma((planes * cut,)), dma((planes * cut,)),
            dma((planes,)), dma((planes,)), dma((planes,)), dma((planes,)),
            dma((4 + total // 256,)), dma((2,)),
        ],
        compiler_params=pltpu.CompilerParams(
            collective_id=1, has_side_effects=True, vmem_limit_bytes=58 << 20
        ),
        name="gather_project",
    )(pieces, pieces_small, normed)


def grads_kernel(
    planes, ny, ns, cut,
    nt_ref, dp_ref, wm_ref, ws_ref, dbc_ref, ddt_ref, raw_ref, cw_ref,
    gw_ref, gs_ref, ng_ref, bsum_ref,
    ntb, dp, wmain, dw, passing, dsmall, spassing, smalls, bcs, raw, sib_out, sib_in, far_in, own,
    a_send, a_recv, as_send, as_recv, b_send, b_recv, x_send, x_recv, f_send, f_recv,
    up_send, up_recv, down_send, down_recv, sup_send, sup_recv, sdown_send, sdown_recv, local_sem, nt_sem,
):
    at = Place(planes, ny, ns)
    group, rank, z = at.group, at.rank, at.z
    total, width = dp.shape
    plane_rows = D // planes
    piece, part = plane_rows // group, plane_rows // cut
    block = total // group
    chips = group // 2
    chips_x = ns // 2
    small = bcs.shape[1]
    heads = ddt_ref.shape[0]
    span = total // ny
    rows_small = smalls.shape[0]

    def plane_in_turn(j):
        return lax.rem(jnp.where(2 * z < planes, z + j, z - j + planes), planes)

    def nt_plane(i):
        return plane_in_turn(lax.rem(2 * planes - 1 - i, planes))

    def nt_copy(i):
        rows = pl.ds(pl.multiple_of(nt_plane(i) * plane_rows, plane_rows), plane_rows)
        return pltpu.make_async_copy(nt_ref.at[rows], ntb.at[lax.rem(i, 2)], nt_sem.at[lax.rem(i, 2)])

    nt_copy(0).start()
    dp_copy = pltpu.make_async_copy(dp_ref, dp, local_sem.at[0])
    dp_copy.start()
    nt_copy(1).start()
    wm_copy = pltpu.make_async_copy(wm_ref, wmain, local_sem.at[1])
    wm_copy.start()
    own_small = pl.ds(pl.multiple_of(rank * small, small), small)
    raw_copy = pltpu.make_async_copy(raw_ref.at[own_small], raw, local_sem.at[2])
    raw_copy.start()
    bcs_copy = pltpu.make_async_copy(dbc_ref.at[own_small], bcs.at[rank], local_sem.at[3])
    bcs_copy.start()
    at.greet()

    def bc_piece(r, i, owner):
        rows = pl.ds(pl.multiple_of(r * small, small), small)
        return remote(dbc_ref.at[rows], bcs.at[owner], b_send.at[i], b_recv.at[owner], at.member(r))

    for i in range(1, group):
        bc_piece(at.peer(i), i, rank).start()
    dp_copy.wait()

    half = min(256, plane_rows)

    def weight_plane(i):
        p = nt_plane(i)
        nt_copy(i).wait()

        def one(h, _):
            rows = pl.ds(pl.multiple_of(h * half, half), half)
            there = pl.ds(pl.multiple_of(p * plane_rows + h * half, half), half)
            dw[there, :] = jnp.dot(ntb[lax.rem(i, 2), rows, :], dp[...], preferred_element_type=F32)
            return 0

        lax.fori_loop(0, plane_rows // half, one, 0)
        nt_copy(i + 2).start()

    def narrow_plane(i):
        nt_copy(i).wait()
        dsmall[nt_plane(i)] = mm_last(smalls[...], ntb[lax.rem(i, 2)])

        @pl.when(i + 2 < 2 * planes)
        def _():
            nt_copy(i + 2).start()

    def rows_in(p, q):
        return pl.ds(pl.multiple_of(p * plane_rows + q * part, part), part)

    def wide_up(t, q, k):
        ref = passing.at[rows_in(t + 1, q)]
        return remote(ref, ref, up_send.at[k], up_recv.at[k], at.up)

    def wide_down(t, q, k):
        ref = passing.at[rows_in(t, q)]
        return remote(ref, ref, down_send.at[k], down_recv.at[k], at.down)

    def small_up(t, j):
        return remote(spassing.at[t + 1], spassing.at[t + 1], sup_send.at[j], sup_recv.at[j], at.up)

    def small_down(t, j):
        return remote(spassing.at[t], spassing.at[t], sdown_send.at[j], sdown_recv.at[j], at.down)

    def wide_step(k):
        j, q = k // cut, lax.rem(k, cut)
        t = planes - 1 - j

        @pl.when(t > z)
        def _():
            here = rows_in(t + 1, q)

            @pl.when(at.has_down)
            def _():
                wide_up(t, q, k).wait_recv()
                passing[here, :] = (dw[rows_in(t, q), :] + passing[here, :].astype(F32)).astype(BF16)

            @pl.when(jnp.logical_not(at.has_down))
            def _():
                passing[here, :] = dw[rows_in(t, q), :].astype(BF16)

            wide_up(t, q, k).start()

        @pl.when(j < z)
        def _():
            here = rows_in(j, q)

            @pl.when(at.has_up)
            def _():
                wide_down(j, q, k).wait_recv()
                passing[here, :] = (dw[here, :] + passing[here, :].astype(F32)).astype(BF16)

            @pl.when(jnp.logical_not(at.has_up))
            def _():
                passing[here, :] = dw[here, :].astype(BF16)

            wide_down(j, q, k).start()

    def small_step(j, _):
        t = planes - 1 - j

        @pl.when(t > z)
        def _():
            @pl.when(at.has_down)
            def _():
                small_up(t, j).wait_recv()
                spassing[t + 1] = (dsmall[t] + spassing[t + 1].astype(F32)).astype(BF16)

            @pl.when(jnp.logical_not(at.has_down))
            def _():
                spassing[t + 1] = dsmall[t].astype(BF16)

            small_up(t, j).start()

        @pl.when(j < z)
        def _():
            @pl.when(at.has_up)
            def _():
                small_down(j, j).wait_recv()
                spassing[j] = (dsmall[j] + spassing[j].astype(F32)).astype(BF16)

            @pl.when(jnp.logical_not(at.has_up))
            def _():
                spassing[j] = dsmall[j].astype(BF16)

            small_down(j, j).start()

        return 0

    def far_rank(i):
        x, core = at.s // 2, lax.rem(at.s, 2)
        return (
            lax.rem(at.y + i // chips_x, ny) * ns + lax.rem(x + lax.rem(i, chips_x), chips_x) * 2 + core
        )

    sibling = at.sibling(rank)

    def normed_part(r):
        rows = pl.ds(pl.multiple_of(r * block, block), block)
        turned = smalls[:, rows].T
        return mm_last(dp[rows, :], wmain[...]) + mm_last(turned, ws_ref[:, :rows_small])

    def to_sibling(i):
        return remote(sib_out.at[i], sib_in.at[i], x_send.at[i], x_recv.at[i], at.member(sibling))

    def to_far(i):
        return remote(sib_in.at[i], far_in.at[i - 1], f_send.at[i], f_recv.at[i], at.member(far_rank(i)))

    def first_task(n):
        i = lax.rem(n + 1, chips)
        sib_out[i] = normed_part(at.sibling(far_rank(i))).astype(BF16)
        to_sibling(i).start()

    def second_task(n):
        i = lax.rem(n + 1, chips)
        value = normed_part(far_rank(i))
        to_sibling(i).wait_recv()
        value = value + sib_in[i].astype(F32)

        @pl.when(i > 0)
        def _():
            sib_in[i] = value.astype(BF16)
            to_far(i).start()

        @pl.when(i == 0)
        def _():
            own[...] = value

    def tasks_step(k, _):
        wide_step(k)

        @pl.when(k < chips)
        def _():
            first_task(k)

        @pl.when((k >= chips) & (k < 2 * chips))
        def _():
            second_task(k - chips)

        return 0

    def plain_step(k, _):
        wide_step(k)
        return 0

    ahead = planes if planes > 4 else 2
    for i in range(ahead):
        weight_plane(i)

    raw_copy.wait()
    bcs_copy.wait()
    for i in range(1, group):
        r = at.peer(i)
        bc_piece(r, i, r).wait_recv()
    dbc = bcs[0].astype(F32)
    for r in range(1, group):
        dbc = dbc + bcs[r].astype(F32)
    values = raw[...].astype(F32)
    place = lax.rem(iota(values.shape, 1), span)
    later = [jnp.where(place >= n, pltpu.roll(values, n, 1), 0.0) if n else values for n in range(KERNEL)]
    conv = cw_ref[:, KERNEL : KERNEL + 1]
    for k in range(KERNEL):
        conv = conv + cw_ref[:, k : k + 1] * later[KERNEL - 1 - k]
    sig = 1.0 / (1.0 + jnp.exp(-conv))
    dconv = dbc * (sig * (1.0 + conv * (1.0 - sig)))
    din = jnp.zeros_like(dconv)
    bsum_ref[...] = jnp.zeros_like(bsum_ref)
    bsum_ref[:, KERNEL : KERNEL + 1] = jnp.sum(dconv, 1, keepdims=True)
    for k in range(KERNEL):
        n = KERNEL - 1 - k
        bsum_ref[:, k : k + 1] = jnp.sum(dconv * later[n], 1, keepdims=True)
        moved = jnp.where(place < span - n, pltpu.roll(dconv, total - n, 1), 0.0) if n else dconv
        din = din + cw_ref[:, k : k + 1] * moved
    filler = jnp.zeros((rows_small - small - heads, total), F32)
    smalls[...] = jnp.concatenate([din, ddt_ref[...].astype(F32), filler], 0).astype(BF16)
    wm_copy.wait()

    steps = (planes - 1) * cut
    lax.fori_loop(0, 2 * chips, tasks_step, 0)
    start = 2 * chips
    for i in range(ahead, planes):
        weight_plane(i)
        stop = min(max((i - ahead + 2) * cut, start), steps)
        lax.fori_loop(start, stop, plain_step, 0)
        start = stop
    for i in range(planes, 2 * planes):
        narrow_plane(i)
        if i == planes + 1 and start < steps:
            stop = start + (steps - start) // 2
            lax.fori_loop(start, stop, plain_step, 0)
            start = stop
    lax.fori_loop(0, planes - 1, small_step, 0)
    lax.fori_loop(start, steps, plain_step, 0)

    @pl.when(at.has_down)
    def _():
        small_up(z, planes - 1 - z).wait_recv()

    @pl.when(at.has_up)
    def _():
        small_down(z, z).wait_recv()

    nothing = jnp.zeros((rows_small, plane_rows), F32)
    spassing[z] = (
        dsmall[z]
        + jnp.where(at.has_down, spassing[z + 1].astype(F32), nothing)
        + jnp.where(at.has_up, spassing[z].astype(F32), nothing)
    ).astype(BF16)

    def small_out(r, i, owner):
        lanes = pl.ds(pl.multiple_of(r * piece // 128 * 128, 128), 128)
        return remote(
            spassing.at[z, :, lanes], gs_ref.at[owner], as_send.at[i], as_recv.at[owner], at.member(r)
        )

    own_lanes = pl.ds(pl.multiple_of(rank * piece // 128 * 128, 128), 128)
    small_kept = pltpu.make_async_copy(spassing.at[z, :, own_lanes], gs_ref.at[rank], local_sem.at[2])
    small_kept.start()
    for i in range(1, group):
        small_out(at.peer(i), i, rank).start()

    def piece_rows(r):
        return pl.ds(pl.multiple_of(z * plane_rows + r * piece, piece), piece)

    def wide_out(r, owner):
        return remote(
            passing.at[piece_rows(r)], gw_ref.at[owner], a_send.at[r], a_recv.at[owner], at.member(r)
        )

    wide_kept = pltpu.make_async_copy(passing.at[piece_rows(rank)], gw_ref.at[rank], local_sem.at[3])

    def last_step(q, _):
        here = rows_in(z, q)

        @pl.when(at.has_down)
        def _():
            wide_up(z, q, (planes - 1 - z) * cut + q).wait_recv()

        @pl.when(at.has_up)
        def _():
            wide_down(z, q, z * cut + q).wait_recv()

        nothing = jnp.zeros((part, width), F32)
        passing[here, :] = (
            dw[here, :]
            + jnp.where(at.has_down, passing[rows_in(z + 1, q), :].astype(F32), nothing)
            + jnp.where(at.has_up, passing[here, :].astype(F32), nothing)
        ).astype(BF16)
        for n in range(group // cut):
            r = q * (group // cut) + n

            @pl.when(r != rank)
            def _():
                wide_out(r, rank).start()

            @pl.when(r == rank)
            def _():
                wide_kept.start()

        return 0

    lax.fori_loop(0, cut, last_step, 0)

    value = own[...]
    for i in range(1, chips):
        to_far(i).wait_recv()
        value = value + far_in[i - 1].astype(F32)
    ng_ref[...] = value

    for i in range(1, group):
        r = at.peer(i)
        bc_piece(r, i, rank).wait_send()
        small_out(r, i, rank).wait_send()
        small_out(r, i, r).wait_recv()
        wide_out(r, rank).wait_send()
        wide_out(r, r).wait_recv()
    small_kept.wait()
    wide_kept.wait()
    for i in range(chips):
        to_sibling(i).wait_send()
        if i:
            to_far(i).wait_send()

    def wide_sent(k, _):
        j, q = k // cut, lax.rem(k, cut)

        @pl.when(planes - 1 - j > z)
        def _():
            wide_up(planes - 1 - j, q, k).wait_send()

        @pl.when(j < z)
        def _():
            wide_down(j, q, k).wait_send()

        return 0

    lax.fori_loop(0, steps, wide_sent, 0)

    def small_sent(j, _):
        @pl.when(planes - 1 - j > z)
        def _():
            small_up(planes - 1 - j, j).wait_send()

        @pl.when(j < z)
        def _():
            small_down(j, j).wait_send()

        return 0

    lax.fori_loop(0, planes - 1, small_sent, 0)


def project_grads(normed_t, proj_grad, w_main, w_small, dbc_t, ddt_t, bc_raw, conv_own, planes, ny, ns):
    total, width = proj_grad.shape
    group = ny * ns
    small, heads = 2 * STATE // group, ddt_t.shape[0]
    rows_small = -(-(small + heads) // 16) * 16
    plane_rows = D // planes
    block = total // group
    chips = group // 2
    cut = 1
    while cut * 2 <= min(group, 32 // planes):
        cut *= 2
    dma = pltpu.SemaphoreType.DMA
    anywhere = pl.BlockSpec(memory_space=pl.ANY)
    vmem = pl.BlockSpec(memory_space=pltpu.VMEM)
    return pl.pallas_call(
        functools.partial(grads_kernel, planes, ny, ns, cut),
        in_specs=[anywhere, anywhere, anywhere, vmem, anywhere, vmem, anywhere, vmem],
        out_specs=[anywhere, anywhere, vmem, vmem],
        out_shape=[
            jax.ShapeDtypeStruct((group, plane_rows // group, width), BF16),
            jax.ShapeDtypeStruct((group, rows_small, 128), BF16),
            jax.ShapeDtypeStruct((block, D), F32),
            jax.ShapeDtypeStruct((small, 128), F32),
        ],
        scratch_shapes=[
            pltpu.VMEM((2, plane_rows, total), BF16),
            pltpu.VMEM((total, width), BF16),
            pltpu.VMEM((D, width), BF16),
            pltpu.VMEM((D, width), F32),
            pltpu.VMEM((D + plane_rows, width), BF16),
            pltpu.VMEM((planes, rows_small, plane_rows), F32),
            pltpu.VMEM((planes + 1, rows_small, plane_rows), BF16),
            pltpu.VMEM((rows_small, total), BF16),
            pltpu.VMEM((group, small, total), BF16),
            pltpu.VMEM((small, total), BF16),
            pltpu.VMEM((chips, block, D), BF16),
            pltpu.VMEM((chips, block, D), BF16),
            pltpu.VMEM((chips - 1, block, D), BF16),
            pltpu.VMEM((block, D), F32),
            dma((group,)), dma((group,)), dma((group,)), dma((group,)), dma((group,)), dma((group,)),
            dma((chips,)), dma((chips,)), dma((chips,)), dma((chips,)),
            dma((planes * cut,)), dma((planes * cut,)), dma((planes * cut,)), dma((planes * cut,)),
            dma((planes,)), dma((planes,)), dma((planes,)), dma((planes,)),
            dma((4,)), dma((2,)),
        ],
        compiler_params=pltpu.CompilerParams(
            collective_id=2, has_side_effects=True, vmem_limit_bytes=60 << 20
        ),
        name="project_grads",
    )(normed_t, proj_grad, w_main, w_small, dbc_t, ddt_t, bc_raw, conv_own)


def exchange_kernel(planes, ny, ns, mine_ref, out_ref, along, summed, z_send, z_recv, p_send, p_recv):
    at = Place(planes, ny, ns)
    group, rank, z = at.group, at.rank, at.z
    barrier = pltpu.get_barrier_semaphore()
    for i in range(1, planes):
        pl.semaphore_signal(
            barrier, inc=1, device_id=(lax.rem(z + i, planes), at.y, at.s), device_id_type=MESH
        )
    for i in range(1, group):
        pl.semaphore_signal(barrier, inc=1, device_id=at.member(at.peer(i)), device_id_type=MESH)
    pl.semaphore_wait(barrier, planes + group - 2)

    def over_z(p, i, owner):
        return remote(mine_ref, along.at[owner], z_send.at[i], z_recv.at[owner], (p, at.y, at.s))

    for i in range(1, planes):
        over_z(lax.rem(z + i, planes), i, z).start()
    total = mine_ref[...]
    for i in range(1, planes):
        p = lax.rem(z + i, planes)
        over_z(p, i, p).wait_recv()
        total = total + along[p]
    summed[...] = total

    def over_plane(r, i, owner):
        return remote(summed, out_ref.at[owner], p_send.at[i], p_recv.at[owner], at.member(r))

    for i in range(1, group):
        over_plane(at.peer(i), i, rank).start()
    out_ref[rank] = total
    for i in range(1, group):
        r = at.peer(i)
        over_plane(r, i, r).wait_recv()
        over_plane(r, i, rank).wait_send()
    for i in range(1, planes):
        over_z(lax.rem(z + i, planes), i, z).wait_send()


def exchange(mine, planes, ny, ns):
    group = ny * ns
    dma = pltpu.SemaphoreType.DMA
    vmem = pl.BlockSpec(memory_space=pltpu.VMEM)
    return pl.pallas_call(
        functools.partial(exchange_kernel, planes, ny, ns),
        in_specs=[vmem],
        out_specs=vmem,
        out_shape=jax.ShapeDtypeStruct((group,) + mine.shape, F32),
        scratch_shapes=[
            pltpu.VMEM((planes,) + mine.shape, F32),
            pltpu.VMEM(mine.shape, F32),
            dma((planes,)), dma((planes,)), dma((group,)), dma((group,)),
        ],
        compiler_params=pltpu.CompilerParams(collective_id=3, has_side_effects=True),
        name="exchange",
    )(mine)


def forward_kernel(
    x_ref, gate_ref, bc_ref, bct_ref, dt_ref, wx_ref, bx_ref, bias_ref, alog_ref, skip_ref,
    scanned_ref, state_ref, state, halo,
):
    @pl.when(pl.program_id(1) == 0)
    def _():
        state[...] = jnp.zeros_like(state)
        halo[...] = jnp.zeros_like(halo)

    rows, channels = x_ref.shape
    raw = x_ref[...].astype(F32)
    conv, _ = convolved(raw, halo[...], wx_ref[...], bx_ref[...])
    halo[...] = raw[rows - 8 :]
    xs = conv / (1.0 + jnp.exp(-conv))
    _, step_t, _, run_t = head_times(dt_ref[...], bias_ref[...], alog_ref[...])
    run = run_t.T
    xdt = xs * spread(step_t.T)
    b_t = bct_ref[:STATE]
    c = bc_ref[:, STATE:]
    causal = iota((rows, rows), 0) >= iota((rows, rows), 1)
    products = jnp.where(causal, mm(c, b_t), 0.0)
    entering = state[...]
    state_ref[0] = entering
    inward = mm(c, entering) * spread(jnp.exp(run))
    skipped = skip_ref[...] * xs
    lane = iota((rows, 2 * HEADDIM), 1)
    for pair in range(channels // 128):
        cols = slice(pair * 128, pair * 128 + 128)
        part = xdt[:, cols]
        total = inward[:, cols] + skipped[:, cols]
        for side in range(2):
            h = 2 * pair + side
            decay = jnp.exp(jnp.minimum(run[:, h : h + 1] - run_t[h : h + 1], 0.0))
            own = (lane < HEADDIM) if side == 0 else (lane >= HEADDIM)
            total = total + mm(products * decay, jnp.where(own, part, 0.0))
        scanned_ref[:, cols] = total
    last = run[rows - 1 :]
    to_end = spread(jnp.exp(last - run))
    state[...] = entering * spread(jnp.exp(last)) + mm(b_t, xdt * to_end)


def backward_kernel(
    x_ref, halo_ref, gate_ref, bc_ref, bct_ref, dt_ref, wx_ref, bx_ref, bias_ref, alog_ref, skip_ref,
    gain_ref, scanned_ref, state_ref, mixed_grad_ref, norms_ref,
    grad_ref, dbc_ref, ddt_ref, sums_ref, heads_ref,
    lam, rim,
):
    step_id = pl.program_id(1)
    first = (pl.program_id(0) == 0) & (step_id == 0)

    @pl.when(first)
    def _():
        sums_ref[...] = jnp.zeros_like(sums_ref)
        heads_ref[...] = jnp.zeros_like(heads_ref)

    @pl.when(step_id == 0)
    def _():
        lam[...] = jnp.zeros_like(lam)
        rim[...] = jnp.zeros_like(rim)

    rows, channels = x_ref.shape
    heads = channels // HEADDIM
    gate = gate_ref[...].astype(F32)
    scanned = scanned_ref[...]
    mixed_grad = mixed_grad_ref[...].astype(F32)
    norms = norms_ref[...].T
    r = norms[:, 0:1]
    inner = norms[:, 1:2]
    sig = 1.0 / (1.0 + jnp.exp(-gate))
    silu = gate * sig
    product = scanned * silu
    product_grad = r * (mixed_grad * gain_ref[...]) - product * (r * r * r * inner)
    sums_ref[5:6] += jnp.sum(mixed_grad * product * r, 0, keepdims=True)
    dy = product_grad * silu
    grad_ref[:, :channels] = (product_grad * scanned * (sig * (1.0 + gate * (1.0 - sig)))).astype(BF16)

    raw = x_ref[...].astype(F32)
    before = jnp.where(step_id == pl.num_programs(1) - 1, 0.0, halo_ref[...].astype(F32))
    conv, shifted = convolved(raw, before, wx_ref[...], bx_ref[...])
    sig_c = 1.0 / (1.0 + jnp.exp(-conv))
    xs = conv * sig_c
    sums_ref[6:7] += jnp.sum(dy * xs, 0, keepdims=True)
    pre, step_t, decay_t, run_t = head_times(dt_ref[...], bias_ref[...], alog_ref[...])
    run = run_t.T
    step = spread(step_t.T)
    xdt = xs * step
    b = bc_ref[:, :STATE]
    c = bc_ref[:, STATE:]
    b_t = bct_ref[:STATE]
    c_t = bct_ref[STATE:]
    causal = iota((rows, rows), 0) >= iota((rows, rows), 1)
    products = jnp.where(causal, mm(c, b_t), 0.0)
    entering = state_ref[0]
    leaving = lam[...]
    last = run[rows - 1 :]
    to_end = spread(jnp.exp(last - run))
    whole = spread(jnp.exp(last))
    dye = dy * spread(jnp.exp(run))
    xend = xdt * to_end
    inward = dye * mm(c, entering)
    outward_grad = mm(b, leaving) * to_end
    outward = outward_grad * xdt
    dc_t = mm_last(entering, dye)
    db_t = mm_last(leaving, xend)
    kept = leaving * whole
    lam[...] = kept + mm(c_t, dye)

    dy_t = dy.T.astype(BF16)
    lane = iota((rows, 2 * HEADDIM), 1)
    wide = iota((rows, heads), 1)
    dproducts = jnp.zeros((rows, rows), F32)
    row_sums = jnp.zeros((rows, heads), F32)
    col_sums = []
    dxdt_t = []
    for h in range(heads):
        cols = slice((h // 2) * 128, (h // 2) * 128 + 128)
        own = (lane < HEADDIM) if h % 2 == 0 else (lane >= HEADDIM)
        decay = jnp.exp(jnp.minimum(run[:, h : h + 1] - run_t[h : h + 1], 0.0))
        weights = products * decay
        dweights = mm_last(dy[:, cols], jnp.where(own, xdt[:, cols], 0.0))
        dproducts = dproducts + dweights * decay
        shares = dweights * weights
        row_sums = jnp.where(wide == h, jnp.sum(shares, 1, keepdims=True), row_sums)
        col_sums.append(jnp.sum(shares, 0, keepdims=True))
        dxdt_t.append(mm(dy_t[h * HEADDIM : (h + 1) * HEADDIM], weights))
    dproducts = jnp.where(causal, dproducts, 0.0)
    dc_t = dc_t + mm_last(b_t, dproducts)
    db_t = db_t + mm(c_t, dproducts)
    dbc_ref[:STATE] = db_t.astype(BF16)
    dbc_ref[STATE:] = dc_t.astype(BF16)
    dxdt = jnp.concatenate(dxdt_t, 0).T + outward_grad

    member = (iota((heads, channels), 1) // HEADDIM == iota((heads, channels), 0)).astype(F32)

    def per_head(values):
        return lax.dot_general(
            member, values, (((1,), (1,)), ((), ())), precision=HIGH, preferred_element_type=F32
        )

    out_t = per_head(outward)
    run_grad = per_head(inward) - out_t + row_sums.T - jnp.concatenate(col_sums, 0)
    at_end = jnp.sum(out_t, 1, keepdims=True) + jnp.sum(per_head(kept * entering), 1, keepdims=True)
    lower = (iota((rows, rows), 0) >= iota((rows, rows), 1)).astype(F32)
    decay_grad = at_end + jnp.dot(run_grad, lower, precision=HIGH, preferred_element_type=F32)
    step_grad = per_head(dxdt * xs) - jnp.exp(alog_ref[...]) * decay_grad
    dt_grad = step_grad / (1.0 + jnp.exp(-pre))
    ddt_ref[...] = dt_grad.astype(BF16)
    heads_ref[:, 0:1] += jnp.sum(dt_grad, 1, keepdims=True)
    heads_ref[:, 1:2] += jnp.sum(decay_grad * decay_t, 1, keepdims=True)

    dx = dxdt * step + skip_ref[...] * dy
    dconv = dx * (sig_c * (1.0 + conv * (1.0 - sig_c)))
    sums_ref[4:5] += jnp.sum(dconv, 0, keepdims=True)
    for k in range(KERNEL):
        sums_ref[k : k + 1] += jnp.sum(dconv * shifted[k], 0, keepdims=True)
    joined = jnp.concatenate([dconv, rim[...]], 0)
    rim[...] = dconv[:8]
    dx_in = wx_ref[KERNEL - 1 : KERNEL] * dconv
    for k in range(KERNEL - 1):
        ahead = KERNEL - 1 - k
        dx_in = dx_in + wx_ref[k : k + 1] * joined[ahead : ahead + rows]
    grad_ref[:, channels:] = dx_in.astype(BF16)


def whole_spec(array):
    return pl.BlockSpec(array.shape, lambda q, i: (0,) * array.ndim)


def scan_forward(projected, bc, bc_t, dt_t, params, seqs):
    total, channels = projected.shape[0], projected.shape[1] // 2
    heads = channels // HEADDIM
    steps = total // seqs // STRETCH
    row = lambda q, i: q * steps + i
    return pl.pallas_call(
        forward_kernel,
        grid=(seqs, steps),
        in_specs=[
            pl.BlockSpec((STRETCH, channels), lambda q, i: (row(q, i), 1)),
            pl.BlockSpec((STRETCH, channels), lambda q, i: (row(q, i), 0)),
            pl.BlockSpec((STRETCH, 2 * STATE), lambda q, i: (row(q, i), 0)),
            pl.BlockSpec((2 * STATE, STRETCH), lambda q, i: (0, row(q, i))),
            pl.BlockSpec((heads, STRETCH), lambda q, i: (0, row(q, i))),
        ]
        + [whole_spec(p) for p in params],
        out_specs=[
            pl.BlockSpec((STRETCH, channels), lambda q, i: (row(q, i), 0)),
            pl.BlockSpec((1, STATE, channels), lambda q, i: (row(q, i), 0, 0)),
        ],
        out_shape=[
            jax.ShapeDtypeStruct((total, channels), F32),
            jax.ShapeDtypeStruct((seqs * steps, STATE, channels), F32),
        ],
        scratch_shapes=[pltpu.VMEM((STATE, channels), F32), pltpu.VMEM((8, channels), F32)],
        compiler_params=pltpu.CompilerParams(vmem_limit_bytes=48 << 20),
        name="scan_forward",
    )(projected, projected, bc, bc_t, dt_t, *params)


def scan_backward(projected, bc, bc_t, dt_t, params, gain, scanned, states, mixed_grad, norms, seqs):
    total, channels = projected.shape[0], projected.shape[1] // 2
    heads = channels // HEADDIM
    steps = total // seqs // STRETCH
    row = lambda q, i: q * steps + steps - 1 - i
    halo_row = lambda q, i: jnp.maximum(row(q, i) * (STRETCH // 16) - 1, 0)
    return pl.pallas_call(
        backward_kernel,
        grid=(seqs, steps),
        in_specs=[
            pl.BlockSpec((STRETCH, channels), lambda q, i: (row(q, i), 1)),
            pl.BlockSpec((16, channels), lambda q, i: (halo_row(q, i), 1)),
            pl.BlockSpec((STRETCH, channels), lambda q, i: (row(q, i), 0)),
            pl.BlockSpec((STRETCH, 2 * STATE), lambda q, i: (row(q, i), 0)),
            pl.BlockSpec((2 * STATE, STRETCH), lambda q, i: (0, row(q, i))),
            pl.BlockSpec((heads, STRETCH), lambda q, i: (0, row(q, i))),
        ]
        + [whole_spec(p) for p in params]
        + [
            whole_spec(gain),
            pl.BlockSpec((STRETCH, channels), lambda q, i: (row(q, i), 0)),
            pl.BlockSpec((1, STATE, channels), lambda q, i: (row(q, i), 0, 0)),
            pl.BlockSpec((STRETCH, channels), lambda q, i: (row(q, i), 0)),
            pl.BlockSpec((8, STRETCH), lambda q, i: (0, row(q, i))),
        ],
        out_specs=[
            pl.BlockSpec((STRETCH, 2 * channels), lambda q, i: (row(q, i), 0)),
            pl.BlockSpec((2 * STATE, STRETCH), lambda q, i: (0, row(q, i))),
            pl.BlockSpec((heads, STRETCH), lambda q, i: (0, row(q, i))),
            pl.BlockSpec((8, channels), lambda q, i: (0, 0)),
            pl.BlockSpec((heads, 128), lambda q, i: (0, 0)),
        ],
        out_shape=[
            jax.ShapeDtypeStruct((total, 2 * channels), BF16),
            jax.ShapeDtypeStruct((2 * STATE, total), BF16),
            jax.ShapeDtypeStruct((heads, total), BF16),
            jax.ShapeDtypeStruct((8, channels), F32),
            jax.ShapeDtypeStruct((heads, 128), F32),
        ],
        scratch_shapes=[pltpu.VMEM((STATE, channels), F32), pltpu.VMEM((8, channels), F32)],
        compiler_params=pltpu.CompilerParams(vmem_limit_bytes=56 << 20),
        name="scan_backward",
    )(projected, projected, projected, bc, bc_t, dt_t, *params, gain, scanned, states, mixed_grad, norms)


def shift_later(values, by, seqs):
    if by == 0:
        return values
    split = values.reshape(values.shape[0], seqs, -1)
    moved = jnp.pad(split, ((0, 0), (0, 0), (by, 0)))[:, :, : split.shape[2]]
    return moved.reshape(values.shape)


def shift_earlier(values, by, seqs):
    if by == 0:
        return values
    split = values.reshape(values.shape[0], seqs, -1)
    moved = jnp.pad(split, ((0, 0), (0, 0), (0, by)))[:, :, by:]
    return moved.reshape(values.shape)


class Layout:
    def __init__(self, planes, group, rows_out):
        self.planes, self.group = planes, group
        self.aligned = rows_out % HEADDIM == 0
        self.blocks = planes if self.aligned else 1
        self.block = INNER // group // self.blocks
        self.heads = HEADS // group
        self.channels = INNER // group
        self.small = 2 * STATE // group

    def pieces(self, values, unit):
        rows = values.shape[0]
        parts = values.reshape(rows, self.blocks, self.group, self.block // HEADDIM * unit)
        return parts.transpose(0, 2, 1, 3).reshape(rows, self.group, -1)

    def joined(self, values, unit):
        rows = values.shape[0]
        parts = values.reshape(rows, self.group, self.blocks, self.block // HEADDIM * unit)
        return parts.transpose(0, 2, 1, 3).reshape(rows, -1)

    def columns(self, w):
        gate = self.pieces(w[:, :INNER], HEADDIM)
        x = self.pieces(w[:, INNER : 2 * INNER], HEADDIM)
        bc = w[:, 2 * INNER : INNER + CHANNELS].reshape(w.shape[0], self.group, self.small)
        dt = self.pieces(w[:, INNER + CHANNELS :], 1)
        return jnp.concatenate([gate, x, bc, dt], 2)

    def uncolumns(self, g):
        c, s = self.channels, self.small
        gate = self.joined(g[:, :, :c], HEADDIM)
        x = self.joined(g[:, :, c : 2 * c], HEADDIM)
        bc = g[:, :, 2 * c : 2 * c + s].reshape(g.shape[0], -1)
        dt = self.joined(g[:, :, 2 * c + s :], 1)
        return jnp.concatenate([gate, x, bc, dt], 1)


def body(
    tokens, cotangent, lengths, norm_gain, w_in, conv_w, conv_b, dt_bias, a_log, skip_scale, gate_gain, w_out,
):
    row_count = tokens.shape[1]
    planes, group = lax.axis_size("z"), lax.axis_size("y") * lax.axis_size("seq")
    seqs = lax.axis_size("y")
    ny, ns = lax.axis_size("y"), lax.axis_size("seq")
    rank = lax.axis_index("y") * lax.axis_size("seq") + lax.axis_index("seq")
    lay = Layout(planes, group, w_out.shape[0])
    channels, small = lay.channels, lay.small
    inputs = tokens.reshape(row_count, D).astype(F32)
    position = lax.axis_index("seq") * row_count + jnp.arange(row_count, dtype=jnp.int32)
    valid_mask = (position < lengths[0]).astype(F32)[:, None]
    rms = lax.rsqrt(jnp.mean(inputs * inputs, -1, keepdims=True) + EPSILON)
    normed = (inputs * rms * norm_gain).astype(BF16)
    masked_cot = cotangent.reshape(row_count, D).astype(F32) * valid_mask
    branch_grad = masked_cot.astype(BF16)

    columns = lay.columns(w_in.astype(BF16)).transpose(1, 0, 2)
    pieces = columns[:, :, : 2 * channels]
    pieces_small = jnp.pad(columns[:, :, 2 * channels :], ((0, 0), (0, 0), (0, 128 - small - lay.heads)))
    if lay.aligned:
        out_own = lax.all_gather(w_out.astype(BF16), "z", axis=0, tiled=True)
    else:
        out_all = lax.all_gather(w_out.astype(BF16), ("z",) + GROUP, axis=0, tiled=True)
        out_own = lax.dynamic_slice_in_dim(out_all, rank * channels, channels, 0)

    def own(values, unit):
        return lax.dynamic_index_in_dim(lay.pieces(values, unit), rank, 1, keepdims=False)

    conv_wx = own(conv_w[:INNER].T, HEADDIM)
    conv_bx = own(conv_b[None, :INNER], HEADDIM)
    bias_own = own(dt_bias[None], 1).T
    a_own = own(a_log[None], 1).T
    skip_own = jnp.repeat(own(skip_scale[None], 1), HEADDIM, 1)
    gain_own = own(gate_gain[None], HEADDIM)
    params = (conv_wx, conv_bx, bias_own, a_own, skip_own)

    projected, bc_raw, dt_t, normed_t, w_main, w_small = gather_project(
        pieces, pieces_small, normed, planes, ny, ns, lay.heads
    )
    bc_in = bc_raw.astype(F32)
    conv_bc = conv_b[INNER:, None]
    for k in range(KERNEL):
        conv_bc = conv_bc + conv_w[INNER:, k : k + 1] * shift_later(bc_in, KERNEL - 1 - k, seqs)
    bc_t = jax.nn.silu(conv_bc).astype(BF16)
    bc = bc_t.T

    scanned, states = scan_forward(projected, bc, bc_t, dt_t, params, seqs)

    grad_all = lax.all_gather(branch_grad, GROUP, axis=0, tiled=True)
    mixed_grad = lax.dot_general(
        grad_all, out_own, (((1,), (1,)), ((), ())), preferred_element_type=F32
    )
    product = scanned * jax.nn.silu(projected[:, :channels].astype(F32))
    sums = lax.psum(
        jnp.stack([jnp.sum(product * product, 1), jnp.sum(mixed_grad * gain_own * product, 1)]), GROUP
    )
    r = lax.rsqrt(sums[0] / INNER + EPSILON)
    norms = jnp.concatenate([r[None], sums[1:] / INNER, jnp.zeros((6, r.shape[0]), F32)], 0)
    mixed = (product * r[:, None] * gain_own).astype(BF16)

    branch = lax.psum_scatter(
        jnp.dot(mixed, out_own, preferred_element_type=F32).astype(BF16),
        GROUP, scatter_dimension=0, tiled=True,
    ).astype(F32)
    output = (valid_mask * (inputs + branch)).astype(BF16)
    out_part = lax.dot_general(
        mixed, grad_all, (((0,), (0,)), ((), ())), preferred_element_type=F32
    ).astype(BF16)
    if lay.aligned:
        grad_w_out = lax.psum_scatter(out_part, "z", scatter_dimension=0, tiled=True).astype(F32)
    else:
        placed = lax.dynamic_update_slice_in_dim(jnp.zeros((INNER, D), BF16), out_part, rank * channels, 0)
        grad_w_out = lax.psum_scatter(placed, ("z",) + GROUP, scatter_dimension=0, tiled=True).astype(F32)

    proj_grad, dbc_t, ddt_t, sums_x, sums_h = scan_backward(
        projected, bc, bc_t, dt_t, params, gain_own, scanned, states, mixed_grad, norms, seqs
    )
    own_bc = lambda v: lax.dynamic_slice_in_dim(v[INNER:], rank * small, small, 0)
    conv_own = jnp.pad(
        jnp.concatenate([own_bc(conv_w), own_bc(conv_b[:, None])], 1), ((0, 0), (0, 128 - KERNEL - 1))
    )
    in_pieces, in_small, normed_grad, bc_sums = project_grads(
        normed_t, proj_grad, w_main, w_small, dbc_t, ddt_t, bc_raw, conv_own, planes, ny, ns
    )
    lanes = in_small.reshape(group, in_small.shape[1], -1, w_in.shape[0])
    mine = lax.dynamic_index_in_dim(lanes, lax.rem(rank, lanes.shape[2]), 2, keepdims=False)
    mine = mine[:, : small + lay.heads].transpose(2, 0, 1)
    grad_w_in = lay.uncolumns(jnp.concatenate([in_pieces.transpose(1, 0, 2), mine], 2)).astype(F32)
    g = normed_grad * norm_gain
    input_grad = masked_cot + rms * g - inputs * (rms ** 3 * jnp.mean(g * inputs, -1, keepdims=True))
    norm_gain_grad = jnp.sum(normed_grad * inputs * rms, 0)

    own_sums = jnp.concatenate(
        [
            sums_x[: KERNEL + 2].reshape(-1),
            jnp.sum(sums_x[KERNEL + 2].reshape(-1, HEADDIM), 1),
            sums_h[:, 0],
            sums_h[:, 1],
            bc_sums[:, :KERNEL].T.reshape(-1),
            bc_sums[:, KERNEL],
        ]
    )
    count = own_sums.shape[0]
    flat = jnp.concatenate([norm_gain_grad, own_sums, jnp.zeros((-(count + D) % 1024,), F32)])
    by_rank = exchange(flat.reshape(-1, 128), planes, ny, ns).reshape(group, -1)
    grad_norm_gain = jnp.sum(by_rank[:, :D], 0)
    by_rank = by_rank[:, D : D + count]
    at = 0

    def take(size):
        nonlocal at
        at += size
        return by_rank[:, at - size : at]

    taken_x = take((KERNEL + 2) * channels).reshape(group, KERNEL + 2, channels).transpose(1, 0, 2)
    full_x = lay.joined(taken_x, HEADDIM)
    grad_skip, grad_bias, grad_a = (
        lay.joined(take(lay.heads)[None], 1)[0] for _ in range(3)
    )
    conv_w_bc = take(KERNEL * small).reshape(group, KERNEL, small).transpose(1, 0, 2).reshape(KERNEL, -1)
    conv_b_bc = take(small).reshape(-1)
    grad_conv_w = jnp.concatenate([full_x[:KERNEL], conv_w_bc], 1).T
    grad_conv_b = jnp.concatenate([full_x[KERNEL], conv_b_bc])
    return (
        output.reshape(tokens.shape),
        input_grad.reshape(1, row_count, D),
        grad_norm_gain,
        grad_w_in,
        grad_conv_w,
        grad_conv_b,
        grad_bias,
        grad_a,
        grad_skip,
        full_x[KERNEL + 1],
        grad_w_out,
    )


def solution(mesh):
    dp, seq = mesh.shape["dp"], mesh.shape["seq"]
    inner_mesh = Mesh(mesh.devices.reshape(dp // 2, 2, seq), ("z", "y", "seq"))
    placed = P(("z", "y"), "seq", None)
    rows = P(("z", "y", "seq"), None)
    in_specs = (placed, placed, P(("z", "y")), P(), rows, P(), P(), P(), P(), P(), P(), rows)
    out_specs = (placed, placed, P(), rows, P(), P(), P(), P(), P(), P(), rows)
    return jax.shard_map(body, mesh=inner_mesh, in_specs=in_specs, out_specs=out_specs, check_vma=False)
```

```python
import functools

import jax
import jax.numpy as jnp
from jax import lax
from jax.experimental import pallas as pl
from jax.experimental.pallas import tpu as pltpu
from jax.sharding import Mesh
from jax.sharding import PartitionSpec as P

D = 2048
HEADS = 64
HEADDIM = 64
STATE = 128
KERNEL = 4
STRETCH = 256
INNER = 4096
CHANNELS = 4352
EPSILON = 1e-05
HIGH = lax.Precision.HIGHEST
BF16 = jnp.bfloat16
F32 = jnp.float32
GROUP = ("y", "seq")


def mm(a, b):
    return jnp.dot(a.astype(BF16), b.astype(BF16), preferred_element_type=F32)


def mm_last(a, b):
    return lax.dot_general(
        a.astype(BF16), b.astype(BF16), (((1,), (1,)), ((), ())), preferred_element_type=F32
    )


def iota(shape, axis):
    return lax.broadcasted_iota(jnp.int32, shape, axis)


def head_times(raw, bias, a_log):
    pre = raw + bias
    step = jnp.maximum(pre, 0.0) + jnp.log1p(jnp.exp(-jnp.abs(pre)))
    log_decay = step * -jnp.exp(a_log)
    width = raw.shape[1]
    upper = (iota((width, width), 0) <= iota((width, width), 1)).astype(F32)
    running = jnp.dot(log_decay, upper, precision=HIGH, preferred_element_type=F32)
    return pre, step, log_decay, running


def over_channels(values, pair):
    left = values[:, 2 * pair : 2 * pair + 1]
    right = values[:, 2 * pair + 1 : 2 * pair + 2]
    lane = iota((values.shape[0], 2 * HEADDIM), 1)
    return jnp.where(lane < HEADDIM, left, right)


def spread(values):
    pairs = values.shape[1] // 2
    return jnp.concatenate([over_channels(values, i) for i in range(pairs)], axis=1)


def convolved(block, halo, conv_w, conv_b):
    rows = block.shape[0]
    joined = jnp.concatenate([halo, block], axis=0)
    base = halo.shape[0] - KERNEL + 1
    shifted = [joined[base + k : base + k + rows] for k in range(KERNEL)]
    total = conv_b
    for k in range(KERNEL):
        total = total + conv_w[k : k + 1] * shifted[k]
    return total, shifted


MESH = pl.DeviceIdType.MESH


def remote(src, dst, send_sem, recv_sem, device):
    return pltpu.make_async_remote_copy(
        src_ref=src, dst_ref=dst, send_sem=send_sem, recv_sem=recv_sem,
        device_id=device, device_id_type=MESH,
    )


class Place:
    def __init__(self, planes, ny, ns):
        self.planes, self.ny, self.ns, self.group = planes, ny, ns, ny * ns
        self.z, self.y, self.s = lax.axis_index("z"), lax.axis_index("y"), lax.axis_index("seq")
        self.rank = self.y * ns + self.s
        self.up, self.down = (self.z + 1, self.y, self.s), (self.z - 1, self.y, self.s)
        self.has_up, self.has_down = self.z < planes - 1, self.z > 0

    def member(self, rank):
        return (self.z, rank // self.ns, lax.rem(rank, self.ns))

    def peer(self, i):
        return lax.rem(self.rank + i, self.group)

    def far(self):
        chips = self.ns // 2
        x, core = self.s // 2, lax.rem(self.s, 2)
        for dy in range(self.ny):
            for dx in range(chips):
                if dy or dx:
                    yield lax.rem(self.y + dy, self.ny) * self.ns + lax.rem(x + dx, chips) * 2 + core

    def sibling(self, rank):
        return rank + 1 - 2 * lax.rem(rank, 2)

    def greet(self):
        barrier = pltpu.get_barrier_semaphore()
        for i in range(1, self.group):
            pl.semaphore_signal(barrier, inc=1, device_id=self.member(self.peer(i)), device_id_type=MESH)

        @pl.when(self.has_up)
        def _():
            pl.semaphore_signal(barrier, inc=1, device_id=self.up, device_id_type=MESH)

        @pl.when(self.has_down)
        def _():
            pl.semaphore_signal(barrier, inc=1, device_id=self.down, device_id_type=MESH)

        count = self.group - 1 + self.has_up.astype(jnp.int32) + self.has_down.astype(jnp.int32)
        pl.semaphore_wait(barrier, count)


class PlaneGather:
    def __init__(self, at, rows_of, whole, sems):
        self.at, self.rows_of, self.whole = at, rows_of, whole
        self.send, self.recv = sems
        self.square = at.ny == 2 and at.ns == 4
        self.sibling = at.sibling(at.rank)
        self.far = list(at.far())
        if not self.square:
            self.units = [(r, None) for r in self.far]
        else:
            xn, yn, dg = self.far
            self.units = [(xn, 0), (yn, 1), (xn, 1), (yn, 0), (dg, 0), (dg, 1)]

    def count(self):
        return 2 * len(self.units) + 2

    def view(self, rank, half):
        rows = self.rows_of(rank)
        if half is None:
            return self.whole.at[rows]
        size = rows.size // 2
        return self.whole.at[pl.ds(pl.multiple_of(rows.start + half * size, size), size)]

    def copy(self, rank, half, to, n, slot):
        ref = self.view(rank, half)
        return remote(ref, ref, self.send.at[n], self.recv.at[slot], self.at.member(to))

    def slot(self, unit):
        return unit

    def sends(self):
        me = self.at.rank
        if not self.square:
            return [(me, None, r, i) for i, r in enumerate(self.far)]
        xn, yn, _ = self.far
        return [(me, 0, xn, 0), (me, 1, yn, 1), (me, 1, xn, 2), (me, 0, yn, 3)]

    def start(self):
        count = len(self.units)
        self.copy(self.at.rank, None, self.sibling, 0, count).start()
        for n, (rank, half, to, slot) in enumerate(self.sends()):
            self.copy(rank, half, to, 1 + n, slot).start()

    def passed(self, unit):
        count = len(self.units)
        on = [(self.sibling, count + 1 + unit)]
        if self.square and unit == 0:
            on.append((self.far[1], 4))
        if self.square and unit == 1:
            on.append((self.far[0], 5))
        return on

    def first_send(self, unit):
        n = 1 + len(self.sends())
        for before in range(unit):
            n += len(self.passed(before))
        return n

    def arrive(self, unit):
        rank, half = self.units[unit]
        self.copy(rank, half, self.sibling, 0, unit).wait_recv()
        for n, (to, slot) in reversed(list(enumerate(self.passed(unit)))):
            self.copy(rank, half, to, self.first_send(unit) + n, slot).start()

    def rest(self):
        count = len(self.units)
        self.copy(self.sibling, None, self.sibling, 0, count).wait_recv()
        for unit, (rank, half) in enumerate(self.units):
            self.copy(self.at.sibling(rank), half, self.sibling, 0, count + 1 + unit).wait_recv()

    def finish(self):
        self.copy(self.at.rank, None, self.sibling, 0, 0).wait_send()
        for n, (rank, half, to, slot) in enumerate(self.sends()):
            self.copy(rank, half, to, 1 + n, slot).wait_send()
        for unit, (rank, half) in enumerate(self.units):
            for n, (to, slot) in enumerate(self.passed(unit)):
                self.copy(rank, half, to, self.first_send(unit) + n, slot).wait_send()


class Share:
    def __init__(self, planes, group, aligned):
        self.group = group
        self.blocks = planes if aligned else 1
        self.channels = INNER // group
        self.block = self.channels // self.blocks
        self.heads = HEADS // group
        self.small = 2 * STATE // group

    def lanes(self, rank, k, base=0):
        return pl.ds(pl.multiple_of(base + (k * self.group + rank) * self.block, self.block), self.block)

    def channel_rows(self, ref, rank):
        return jnp.concatenate([ref[:, self.lanes(rank, k)] for k in range(self.blocks)], 1)

    def head_column(self, ref, rank):
        each = self.block // HEADDIM
        own = iota((self.heads, HEADS), 0)
        head = (own // each * self.group + rank) * each + lax.rem(own, each)
        return jnp.sum(jnp.where(iota((self.heads, HEADS), 1) == head, ref[...], 0.0), 1, keepdims=True)


def project_kernel(
    planes, ny, ns, cut, share,
    len_ref, tok_ref, cot_ref, w_ref, gain_ref,
    proj_ref, bct_ref, dt_ref, nt_ref, wm_ref, ws_ref, bg_ref, half_ref,
    wmain, wsmall, normed, acc, outb, bcb, turned, pm_ref, ps_ref, grads,
    am_send, am_recv, as_send, as_recv, n_send, n_recv, g_send, g_recv, b_send, b_recv,
    up_send, up_recv, down_send, down_recv, sup_send, sup_recv, sdown_send, sdown_recv, local_sem, turn_sem,
):
    at = Place(planes, ny, ns)
    group, rank, z = at.group, at.rank, at.z
    heads = share.heads
    piece = w_ref.shape[0]
    plane_rows = piece * group
    total, slab = normed.shape[0], 256
    own_rows = tok_ref.shape[0]
    small = bcb.shape[0] // group
    part = plane_rows // cut

    def rows_of(r):
        return pl.ds(pl.multiple_of(z * plane_rows + r * piece, piece), piece)

    def block_rows(p, q):
        return pl.ds(pl.multiple_of(p * plane_rows + q * part, part), part)

    def plane_block(p):
        return pl.ds(pl.multiple_of(p * plane_rows, plane_rows), plane_rows)

    def norm_rows(r):
        return pl.ds(pl.multiple_of(r * own_rows, own_rows), own_rows)

    narrow_t = w_ref[:, 2 * INNER :].T
    filler = jnp.zeros((128 - small - heads, piece), F32)
    each = share.block // HEADDIM
    for r in range(group):
        times = [
            narrow_t[2 * STATE + (k * group + r) * each : 2 * STATE + (k * group + r + 1) * each]
            for k in range(share.blocks)
        ]
        ps_ref[r] = jnp.concatenate([narrow_t[r * small : (r + 1) * small]] + times + [filler], 0).T.astype(BF16)
    for r in range(group):
        for k in range(share.blocks):
            here = pl.ds(k * share.block, share.block)
            pm_ref[r, :, here] = w_ref[:, pl.ds((k * group + r) * share.block, share.block)].astype(BF16)
            here = pl.ds(share.channels + k * share.block, share.block)
            pm_ref[r, :, here] = w_ref[:, pl.ds(INNER + (k * group + r) * share.block, share.block)].astype(BF16)
    at.greet()

    def main_piece(r, i):
        return remote(pm_ref.at[r], wmain.at[rows_of(rank)], am_send.at[i], am_recv.at[rank], at.member(r))

    def small_piece(r, i):
        return remote(ps_ref.at[r], wsmall.at[rows_of(rank)], as_send.at[i], as_recv.at[rank], at.member(r))

    for i in range(1, group):
        small_piece(at.peer(i), i).start()
    for i in range(1, group):
        main_piece(at.peer(i), i).start()
    own_copies = [
        pltpu.make_async_copy(pm_ref.at[rank], wmain.at[rows_of(rank)], local_sem.at[0]),
        pltpu.make_async_copy(ps_ref.at[rank], wsmall.at[rows_of(rank)], local_sem.at[1]),
    ]
    for copy in own_copies:
        copy.start()
    inputs = tok_ref[...].astype(F32)
    rms = lax.rsqrt(jnp.mean(inputs * inputs, 1, keepdims=True) + EPSILON)
    normed[norm_rows(rank), :] = (inputs * rms * gain_ref[...]).astype(BF16)
    norms = PlaneGather(at, norm_rows, normed, (n_send, n_recv))
    norms.start()
    position = at.s * own_rows + iota((own_rows, 1), 0)
    valid = jnp.where(position < len_ref[0], 1.0, 0.0)
    masked = (cot_ref[...].astype(F32) * valid).astype(BF16)
    bg_ref[...] = masked
    grads[norm_rows(rank), :] = masked[:, : D // 2]
    gather_grads = PlaneGather(at, norm_rows, grads, (g_send, g_recv))
    acc[...] = jnp.zeros_like(acc)
    for copy in own_copies:
        copy.wait()

    for i in range(1, group):
        r = at.peer(i)
        remote(ps_ref.at[r], wsmall.at[rows_of(r)], as_send.at[i], as_recv.at[r], at.member(r)).wait_recv()

    def small_up(p, j):
        return remote(wsmall.at[plane_block(p)], wsmall.at[plane_block(p)], sup_send.at[j], sup_recv.at[j], at.up)

    def small_down(p, j):
        return remote(wsmall.at[plane_block(p)], wsmall.at[plane_block(p)], sdown_send.at[j], sdown_recv.at[j], at.down)

    def wide_up(p, q, k):
        return remote(wmain.at[block_rows(p, q)], wmain.at[block_rows(p, q)], up_send.at[k], up_recv.at[k], at.up)

    def wide_down(p, q, k):
        return remote(wmain.at[block_rows(p, q)], wmain.at[block_rows(p, q)], down_send.at[k], down_recv.at[k], at.down)

    def each_way(p, above, fn_up, fn_down):
        @pl.when(at.has_up & jnp.logical_not(above))
        def _():
            fn_up()

        @pl.when(at.has_down & above)
        def _():
            fn_down()

    @pl.when(at.has_up)
    def _():
        small_up(z, 0).start()

    @pl.when(at.has_down)
    def _():
        small_down(z, 0).start()

    ranks_in = group // cut
    for q in range(cut):
        for r in range(q * ranks_in, (q + 1) * ranks_in):
            @pl.when(rank != r)
            def _():
                remote(pm_ref.at[r], wmain.at[rows_of(r)], am_send.at[0], am_recv.at[r], at.member(r)).wait_recv()

        @pl.when(at.has_up)
        def _():
            wide_up(z, q, q).start()

        @pl.when(at.has_down)
        def _():
            wide_down(z, q, q).start()

    def small_step(j, _):
        @pl.when(z + j < planes)
        def _():
            small_down(z + j, j - 1).wait_recv()

            @pl.when(at.has_down)
            def _():
                small_down(z + j, j).start()

        @pl.when(z - j >= 0)
        def _():
            small_up(z - j, j - 1).wait_recv()

            @pl.when(at.has_up)
            def _():
                small_up(z - j, j).start()

        return 0

    lax.fori_loop(1, planes, small_step, 0)

    def plane_in_turn(j):
        return lax.rem(jnp.where(2 * z < planes, z + j, z - j + planes), planes)

    slabs = total // slab

    def product(index):
        j, m = index // slabs, lax.rem(index, slabs)
        p = plane_in_turn(j)
        rows = pl.ds(pl.multiple_of(m * slab, slab), slab)
        lanes = pl.ds(pl.multiple_of(p * plane_rows, 128), plane_rows)
        return rows, acc[rows, :] + jnp.dot(
            normed[rows, lanes], wmain[plane_block(p), :], preferred_element_type=F32
        )

    def narrow(m, _):
        rows = pl.ds(pl.multiple_of(m * slab, slab), slab)
        value = jnp.dot(normed[rows, :], wsmall[...], preferred_element_type=F32).T
        bcb[pl.ds(pl.multiple_of(rank * small, small), small), rows] = value[:small].astype(BF16)
        dt_ref[:, rows] = value[small : small + heads].astype(BF16).astype(F32)
        return 0

    def bc_piece(r, i, owner):
        rows = pl.ds(pl.multiple_of(owner * small, small), small)
        return remote(bcb.at[rows], bcb.at[rows], b_send.at[i], b_recv.at[owner], at.member(r))

    steps = (planes - 1) * cut
    busy = (planes - 2) * cut
    per_step = -(-(planes - 1) * slabs // cut)

    def wide_step(k, _):
        j, q = k // cut + 1, lax.rem(k, cut)

        @pl.when(z + j < planes)
        def _():
            wide_down(z + j, q, k).wait_recv()

            @pl.when(at.has_down)
            def _():
                wide_down(z + j, q, k + cut).start()

        @pl.when(z - j >= 0)
        def _():
            wide_up(z - j, q, k).wait_recv()

            @pl.when(at.has_up)
            def _():
                wide_up(z - j, q, k + cut).start()

        return 0

    units = len(norms.units)
    last = 0
    for i in range(units):
        mark = busy * (5 + 4 * (i // 2)) // 16 if norms.square else cut + i * max(busy - cut, 0) // units
        lax.fori_loop(last, mark, wide_step, 0)
        last = mark
        norms.arrive(i)
        if i == units - 1:
            gather_grads.start()
    lax.fori_loop(last, busy, wide_step, 0)
    norms.rest()
    lax.fori_loop(0, slabs, narrow, 0)
    for i in range(1, group):
        bc_piece(at.peer(i), i, rank).start()

    def turn_copy(m):
        rows = pl.ds(pl.multiple_of(m * slab, slab), slab)
        return pltpu.make_async_copy(turned.at[lax.rem(m, 2)], nt_ref.at[:, rows], turn_sem.at[lax.rem(m, 2)])

    def turn(m):
        @pl.when(m >= 2)
        def _():
            turn_copy(m - 2).wait()

        rows = pl.ds(pl.multiple_of(m * slab, slab), slab)
        turned[lax.rem(m, 2)] = normed[rows, :].T
        turn_copy(m).start()

    ws_copy = pltpu.make_async_copy(wsmall, ws_ref, local_sem.at[1])
    ws_copy.start()

    def busy_step(k, _):
        wide_step(k, 0)

        def one(i, _):
            rows, value = product(jnp.minimum((k - busy) * per_step + i, (planes - 1) * slabs))

            @pl.when((k - busy) * per_step + i < (planes - 1) * slabs)
            def _():
                acc[rows, :] = value

            return 0

        lax.fori_loop(0, per_step, one, 0)

        def other(i, _):
            @pl.when((k - busy) * turns + i < slabs)
            def _():
                turn((k - busy) * turns + i)

            return 0

        lax.fori_loop(0, turns, other, 0)
        return 0

    turns = -(-slabs // cut)
    last = busy
    for i in range(units):
        mark = busy + (steps - busy) * (4 + 2 * (i // 2)) // 8 if norms.square else steps
        lax.fori_loop(last, mark, busy_step, 0)
        last = mark
        gather_grads.arrive(i)
    lax.fori_loop(last, steps, busy_step, 0)
    wm_copy = pltpu.make_async_copy(wmain, wm_ref, local_sem.at[2])
    wm_copy.start()

    def out_copy(m):
        rows = pl.ds(pl.multiple_of(m * slab, slab), slab)
        return pltpu.make_async_copy(outb.at[rows], proj_ref.at[rows], local_sem.at[4 + m])

    def final(m, _):
        rows, value = product((planes - 1) * slabs + m)
        outb[rows, :] = value.astype(BF16)
        out_copy(m).start()
        return 0

    lax.fori_loop(0, slabs, final, 0)

    gather_grads.rest()
    half_copy = pltpu.make_async_copy(grads, half_ref, local_sem.at[0])
    half_copy.start()

    for i in range(1, group):
        r = at.peer(i)
        bc_piece(r, i, r).wait_recv()
    bct_copy = pltpu.make_async_copy(bcb, bct_ref, local_sem.at[3])
    bct_copy.start()
    for i in range(1, group):
        r = at.peer(i)
        main_piece(r, i).wait_send()
        small_piece(r, i).wait_send()
        bc_piece(r, i, rank).wait_send()
    norms.finish()
    gather_grads.finish()
    half_copy.wait()

    def small_sent(j, _):
        @pl.when((z + j < planes) & at.has_down)
        def _():
            small_down(z + j, j).wait_send()

        @pl.when((z - j >= 0) & at.has_up)
        def _():
            small_up(z - j, j).wait_send()

        return 0

    lax.fori_loop(0, planes, small_sent, 0)

    def wide_sent(k, _):
        j, q = k // cut, lax.rem(k, cut)

        @pl.when((z + j < planes) & at.has_down)
        def _():
            wide_down(z + j, q, k).wait_send()

        @pl.when((z - j >= 0) & at.has_up)
        def _():
            wide_up(z - j, q, k).wait_send()

        return 0

    lax.fori_loop(0, planes * cut, wide_sent, 0)
    turn_copy(slabs - 2).wait()
    turn_copy(slabs - 1).wait()
    ws_copy.wait()
    wm_copy.wait()
    bct_copy.wait()
    lax.fori_loop(0, slabs, lambda m, _: (out_copy(m).wait(), 0)[1], 0)


def gather_project(lengths, tokens, cotangent, w_in, norm_gain, planes, ny, ns, share):
    group, width = ny * ns, 2 * share.channels
    rows = w_in.shape[0]
    total = tokens.shape[0] * group
    cut = pieces_per_plane(planes, group)
    units = 6 if (ny, ns) == (2, 4) else group // 2 - 1
    gather = 2 * units + 2
    dma = pltpu.SemaphoreType.DMA
    anywhere = pl.BlockSpec(memory_space=pl.ANY)
    vmem = pl.BlockSpec(memory_space=pltpu.VMEM)
    return pl.pallas_call(
        functools.partial(project_kernel, planes, ny, ns, cut, share),
        in_specs=[pl.BlockSpec(memory_space=pltpu.SMEM)] + [vmem] * 4,
        out_specs=[anywhere, anywhere, vmem, anywhere, anywhere, anywhere, vmem, anywhere],
        out_shape=[
            jax.ShapeDtypeStruct((total, width), BF16),
            jax.ShapeDtypeStruct((2 * STATE, total), BF16),
            jax.ShapeDtypeStruct((share.heads, total), F32),
            jax.ShapeDtypeStruct((D, total), BF16),
            jax.ShapeDtypeStruct((D, width), BF16),
            jax.ShapeDtypeStruct((D, 128), BF16),
            jax.ShapeDtypeStruct(tokens.shape, BF16),
            jax.ShapeDtypeStruct((total, D // 2), BF16),
        ],
        scratch_shapes=[
            pltpu.VMEM((D, width), BF16),
            pltpu.VMEM((D, 128), BF16),
            pltpu.VMEM((total, D), BF16),
            pltpu.VMEM((total, width), F32),
            pltpu.VMEM((total, width), BF16),
            pltpu.VMEM((2 * STATE, total), BF16),
            pltpu.VMEM((2, D, 256), BF16),
            pltpu.VMEM((group, rows, width), BF16),
            pltpu.VMEM((group, rows, 128), BF16),
            pltpu.VMEM((total, D // 2), BF16),
            dma((group,)), dma((group,)), dma((group,)), dma((group,)),
            dma((gather,)), dma((gather,)), dma((gather,)), dma((gather,)), dma((group,)), dma((group,)),
            dma((planes * cut,)), dma((planes * cut,)), dma((planes * cut,)), dma((planes * cut,)),
            dma((planes,)), dma((planes,)), dma((planes,)), dma((planes,)),
            dma((4 + total // 256,)), dma((2,)),
        ],
        compiler_params=pltpu.CompilerParams(
            collective_id=1, has_side_effects=True, vmem_limit_bytes=60 << 20
        ),
        name="gather_project",
    )(lengths, tokens, cotangent, w_in, norm_gain)


def grads_kernel(
    planes, ny, ns, cut,
    nt_ref, dp_ref, dg_ref, wm_ref, ws_ref, dbc_ref, ddt_ref, raw_ref, cw_ref,
    gw_ref, gs_ref, ng_ref, bsum_ref,
    ntb, dp, dg, wmain, dw, passing, dsmall, spassing, smalls, bcs, raw, sib_out, sib_in, far_in, own,
    a_send, a_recv, as_send, as_recv, b_send, b_recv, x_send, x_recv, f_send, f_recv,
    up_send, up_recv, down_send, down_recv, sup_send, sup_recv, sdown_send, sdown_recv, local_sem, nt_sem,
):
    at = Place(planes, ny, ns)
    group, rank, z = at.group, at.rank, at.z
    total, width = dp.shape
    plane_rows = D // planes
    piece, part = plane_rows // group, plane_rows // cut
    block = total // group
    chips = group // 2
    chips_x = ns // 2
    small = bcs.shape[1]
    heads = ddt_ref.shape[0]
    span = total // ny
    rows_small = smalls.shape[0]

    def plane_in_turn(j):
        return lax.rem(jnp.where(2 * z < planes, z + j, z - j + planes), planes)

    def nt_plane(i):
        return plane_in_turn(lax.rem(2 * planes - 1 - i, planes))

    def nt_copy(i):
        rows = pl.ds(pl.multiple_of(nt_plane(i) * plane_rows, plane_rows), plane_rows)
        return pltpu.make_async_copy(nt_ref.at[rows], ntb.at[lax.rem(i, 2)], nt_sem.at[lax.rem(i, 2)])

    nt_copy(0).start()
    dp_copy = pltpu.make_async_copy(dp_ref, dp, local_sem.at[0])
    dp_copy.start()
    nt_copy(1).start()
    wm_copy = pltpu.make_async_copy(wm_ref, wmain, local_sem.at[1])
    wm_copy.start()
    dg_copy = pltpu.make_async_copy(dg_ref, dg, local_sem.at[4])
    dg_copy.start()
    own_small = pl.ds(pl.multiple_of(rank * small, small), small)
    raw_copy = pltpu.make_async_copy(raw_ref.at[own_small], raw, local_sem.at[2])
    raw_copy.start()
    bcs_copy = pltpu.make_async_copy(dbc_ref.at[own_small], bcs.at[rank], local_sem.at[3])
    bcs_copy.start()
    at.greet()

    def bc_piece(r, i, owner):
        rows = pl.ds(pl.multiple_of(r * small, small), small)
        return remote(dbc_ref.at[rows], bcs.at[owner], b_send.at[i], b_recv.at[owner], at.member(r))

    for i in range(1, group):
        bc_piece(at.peer(i), i, rank).start()
    dp_copy.wait()

    half = min(256, plane_rows)

    def weight_plane(i):
        p = nt_plane(i)
        nt_copy(i).wait()

        def one(h, _):
            rows = pl.ds(pl.multiple_of(h * half, half), half)
            there = pl.ds(pl.multiple_of(p * plane_rows + h * half, half), half)
            dw[there, :] = jnp.dot(ntb[lax.rem(i, 2), rows, :], dp[...], preferred_element_type=F32)
            return 0

        lax.fori_loop(0, plane_rows // half, one, 0)
        nt_copy(i + 2).start()

    def narrow_plane(i):
        nt_copy(i).wait()
        dsmall[nt_plane(i)] = mm_last(smalls[...], ntb[lax.rem(i, 2)])

        @pl.when(i + 2 < 2 * planes)
        def _():
            nt_copy(i + 2).start()

    def view(ref, t, q):
        return ref.at[pl.ds(pl.multiple_of(t * plane_rows + q * part, part), part)]

    line = LineSum(at, cut, view, dw, passing, (up_send, up_recv, down_send, down_recv))

    def small_up(t, j):
        return remote(spassing.at[t + 1], spassing.at[t + 1], sup_send.at[j], sup_recv.at[j], at.up)

    def small_down(t, j):
        return remote(spassing.at[t], spassing.at[t], sdown_send.at[j], sdown_recv.at[j], at.down)

    def small_step(j, _):
        t = planes - 1 - j

        @pl.when(t > z)
        def _():
            @pl.when(at.has_down)
            def _():
                small_up(t, j).wait_recv()
                spassing[t + 1] = (dsmall[t] + spassing[t + 1].astype(F32)).astype(BF16)

            @pl.when(jnp.logical_not(at.has_down))
            def _():
                spassing[t + 1] = dsmall[t].astype(BF16)

            small_up(t, j).start()

        @pl.when(j < z)
        def _():
            @pl.when(at.has_up)
            def _():
                small_down(j, j).wait_recv()
                spassing[j] = (dsmall[j] + spassing[j].astype(F32)).astype(BF16)

            @pl.when(jnp.logical_not(at.has_up))
            def _():
                spassing[j] = dsmall[j].astype(BF16)

            small_down(j, j).start()

        return 0

    def normed_part(r):
        rows = pl.ds(pl.multiple_of(r * block, block), block)
        turned = smalls[:, rows].T
        return (
            mm_last(dg[rows, :], wmain[:, :width])
            + mm_last(dp[rows, :], wmain[:, width:])
            + mm_last(turned, ws_ref[:, :rows_small])
        )

    plane = PlaneSum(
        at, normed_part, sib_out, sib_in, far_in, own, (x_send, x_recv, f_send, f_recv)
    )

    def steps(start, stop):
        lax.fori_loop(start, min(stop, line.slots), lambda n, _: (line.step(n), 0)[1], 0)

    def task(n, _):
        line.step(n)
        plane.task(n - early)
        return 0

    early = 0
    for i in range(planes):
        weight_plane(i)
        if planes == 4 and i == 1:
            early = line.skew
            steps(0, early)

    raw_copy.wait()
    bcs_copy.wait()
    for i in range(1, group):
        r = at.peer(i)
        bc_piece(r, i, r).wait_recv()
    dbc = bcs[0].astype(F32)
    for r in range(1, group):
        dbc = dbc + bcs[r].astype(F32)
    values = raw[...].astype(F32)
    place = lax.rem(iota(values.shape, 1), span)
    later = [jnp.where(place >= n, pltpu.roll(values, n, 1), 0.0) if n else values for n in range(KERNEL)]
    conv = cw_ref[:, KERNEL : KERNEL + 1]
    for k in range(KERNEL):
        conv = conv + cw_ref[:, k : k + 1] * later[KERNEL - 1 - k]
    sig = 1.0 / (1.0 + jnp.exp(-conv))
    dconv = dbc * (sig * (1.0 + conv * (1.0 - sig)))
    din = jnp.zeros_like(dconv)
    bsum_ref[...] = jnp.zeros_like(bsum_ref)
    bsum_ref[:, KERNEL : KERNEL + 1] = jnp.sum(dconv, 1, keepdims=True)
    for k in range(KERNEL):
        n = KERNEL - 1 - k
        bsum_ref[:, k : k + 1] = jnp.sum(dconv * later[n], 1, keepdims=True)
        moved = jnp.where(place < span - n, pltpu.roll(dconv, total - n, 1), 0.0) if n else dconv
        din = din + cw_ref[:, k : k + 1] * moved
    filler = jnp.zeros((rows_small - small - heads, total), F32)
    smalls[...] = jnp.concatenate([din, ddt_ref[...].astype(F32), filler], 0).astype(BF16)
    wm_copy.wait()
    dg_copy.wait()

    done = early + 2 * chips
    lax.fori_loop(early, done, task, 0)
    beside = -(-(line.slots - done) // (planes + 1))
    for i in range(planes, 2 * planes):
        narrow_plane(i)
        steps(done, done + beside)
        done = min(done + beside, line.slots)
    lax.fori_loop(0, planes - 1, small_step, 0)
    steps(done, line.slots)

    @pl.when(at.has_down)
    def _():
        small_up(z, planes - 1 - z).wait_recv()

    @pl.when(at.has_up)
    def _():
        small_down(z, z).wait_recv()

    nothing = jnp.zeros((rows_small, plane_rows), F32)
    spassing[z] = (
        dsmall[z]
        + jnp.where(at.has_down, spassing[z + 1].astype(F32), nothing)
        + jnp.where(at.has_up, spassing[z].astype(F32), nothing)
    ).astype(BF16)

    def small_out(r, i, owner):
        lanes = pl.ds(pl.multiple_of(r * piece // 128 * 128, 128), 128)
        return remote(
            spassing.at[z, :, lanes], gs_ref.at[owner], as_send.at[i], as_recv.at[owner], at.member(r)
        )

    own_lanes = pl.ds(pl.multiple_of(rank * piece // 128 * 128, 128), 128)
    small_kept = pltpu.make_async_copy(spassing.at[z, :, own_lanes], gs_ref.at[rank], local_sem.at[2])
    small_kept.start()
    for i in range(1, group):
        small_out(at.peer(i), i, rank).start()

    def piece_rows(r):
        return pl.ds(pl.multiple_of(z * plane_rows + r * piece, piece), piece)

    def wide_out(r, owner):
        return remote(
            passing.at[piece_rows(r)], gw_ref.at[owner], a_send.at[r], a_recv.at[owner], at.member(r)
        )

    wide_kept = pltpu.make_async_copy(passing.at[piece_rows(rank)], gw_ref.at[rank], local_sem.at[3])

    def last_step(q, _):
        view(passing, z, q)[...] = line.total(q).astype(BF16)
        for n in range(group // cut):
            r = q * (group // cut) + n

            @pl.when(r != rank)
            def _():
                wide_out(r, rank).start()

            @pl.when(r == rank)
            def _():
                wide_kept.start()

        return 0

    lax.fori_loop(0, cut, last_step, 0)

    ng_ref[...] = plane.total()

    for i in range(1, group):
        r = at.peer(i)
        bc_piece(r, i, rank).wait_send()
        small_out(r, i, rank).wait_send()
        small_out(r, i, r).wait_recv()
        wide_out(r, rank).wait_send()
        wide_out(r, r).wait_recv()
    small_kept.wait()
    wide_kept.wait()
    plane.finish()
    line.finish()

    def small_sent(j, _):
        @pl.when(planes - 1 - j > z)
        def _():
            small_up(planes - 1 - j, j).wait_send()

        @pl.when(j < z)
        def _():
            small_down(j, j).wait_send()

        return 0

    lax.fori_loop(0, planes - 1, small_sent, 0)


def project_grads(normed_t, proj_grad, gate_grad, w_main, w_small, dbc_t, ddt_t, bc_raw, conv_own, planes, ny, ns):
    total, width = proj_grad.shape
    group = ny * ns
    small, heads = 2 * STATE // group, ddt_t.shape[0]
    rows_small = -(-(small + heads) // 16) * 16
    plane_rows = D // planes
    block = total // group
    chips = group // 2
    cut = 1
    while cut * 2 <= min(group, 32 // planes):
        cut *= 2
    dma = pltpu.SemaphoreType.DMA
    anywhere = pl.BlockSpec(memory_space=pl.ANY)
    vmem = pl.BlockSpec(memory_space=pltpu.VMEM)
    return pl.pallas_call(
        functools.partial(grads_kernel, planes, ny, ns, cut),
        in_specs=[anywhere, anywhere, anywhere, anywhere, vmem, anywhere, vmem, anywhere, vmem],
        out_specs=[anywhere, anywhere, vmem, vmem],
        out_shape=[
            jax.ShapeDtypeStruct((group, plane_rows // group, width), BF16),
            jax.ShapeDtypeStruct((group, rows_small, 128), BF16),
            jax.ShapeDtypeStruct((block, D), F32),
            jax.ShapeDtypeStruct((small, 128), F32),
        ],
        scratch_shapes=[
            pltpu.VMEM((2, plane_rows, total), BF16),
            pltpu.VMEM((total, width), BF16),
            pltpu.VMEM((total, width), BF16),
            pltpu.VMEM((D, 2 * width), BF16),
            pltpu.VMEM((D, width), F32),
            pltpu.VMEM((D + plane_rows, width), BF16),
            pltpu.VMEM((planes, rows_small, plane_rows), F32),
            pltpu.VMEM((planes + 1, rows_small, plane_rows), BF16),
            pltpu.VMEM((rows_small, total), BF16),
            pltpu.VMEM((group, small, total), BF16),
            pltpu.VMEM((small, total), BF16),
            pltpu.VMEM((chips, block, D), BF16),
            pltpu.VMEM((chips, block, D), BF16),
            pltpu.VMEM((chips - 1, block, D), BF16),
            pltpu.VMEM((block, D), F32),
            dma((group,)), dma((group,)), dma((group,)), dma((group,)), dma((group,)), dma((group,)),
            dma((chips,)), dma((chips,)), dma((chips,)), dma((chips,)),
            dma((planes * cut,)), dma((planes * cut,)), dma((planes * cut,)), dma((planes * cut,)),
            dma((planes,)), dma((planes,)), dma((planes,)), dma((planes,)),
            dma((5,)), dma((2,)),
        ],
        compiler_params=pltpu.CompilerParams(
            collective_id=2, has_side_effects=True, vmem_limit_bytes=60 << 20
        ),
        name="project_grads",
    )(normed_t, proj_grad, gate_grad, w_main, w_small, dbc_t, ddt_t, bc_raw, conv_own)


def exchange_kernel(planes, ny, ns, mine_ref, out_ref, along, summed, z_send, z_recv, p_send, p_recv):
    at = Place(planes, ny, ns)
    group, rank, z = at.group, at.rank, at.z
    barrier = pltpu.get_barrier_semaphore()
    for i in range(1, planes):
        pl.semaphore_signal(
            barrier, inc=1, device_id=(lax.rem(z + i, planes), at.y, at.s), device_id_type=MESH
        )
    for i in range(1, group):
        pl.semaphore_signal(barrier, inc=1, device_id=at.member(at.peer(i)), device_id_type=MESH)
    pl.semaphore_wait(barrier, planes + group - 2)

    def over_z(p, i, owner):
        return remote(mine_ref, along.at[owner], z_send.at[i], z_recv.at[owner], (p, at.y, at.s))

    for i in range(1, planes):
        over_z(lax.rem(z + i, planes), i, z).start()
    total = mine_ref[...]
    for i in range(1, planes):
        p = lax.rem(z + i, planes)
        over_z(p, i, p).wait_recv()
        total = total + along[p]
    summed[...] = total

    def over_plane(r, i, owner):
        return remote(summed, out_ref.at[owner], p_send.at[i], p_recv.at[owner], at.member(r))

    for i in range(1, group):
        over_plane(at.peer(i), i, rank).start()
    out_ref[rank] = total
    for i in range(1, group):
        r = at.peer(i)
        over_plane(r, i, r).wait_recv()
        over_plane(r, i, rank).wait_send()
    for i in range(1, planes):
        over_z(lax.rem(z + i, planes), i, z).wait_send()


def exchange(mine, planes, ny, ns):
    group = ny * ns
    dma = pltpu.SemaphoreType.DMA
    vmem = pl.BlockSpec(memory_space=pltpu.VMEM)
    return pl.pallas_call(
        functools.partial(exchange_kernel, planes, ny, ns),
        in_specs=[vmem],
        out_specs=vmem,
        out_shape=jax.ShapeDtypeStruct((group,) + mine.shape, F32),
        scratch_shapes=[
            pltpu.VMEM((planes,) + mine.shape, F32),
            pltpu.VMEM(mine.shape, F32),
            dma((planes,)), dma((planes,)), dma((group,)), dma((group,)),
        ],
        compiler_params=pltpu.CompilerParams(collective_id=3, has_side_effects=True),
        name="exchange",
    )(mine)


class LineSum:
    def __init__(self, at, cut, view, part, passing, sems, base=0, skew=4):
        self.skew = skew
        self.at, self.cut, self.view, self.part, self.passing = at, cut, view, part, passing
        self.up_send, self.up_recv, self.down_send, self.down_recv = sems
        self.steps = (at.planes - 1) * cut
        self.slots = self.steps + (at.planes - 1) * skew
        self.base = base

    def up(self, t, q, k):
        ref = self.view(self.passing, t + 1, q)
        return remote(ref, ref, self.up_send.at[self.base + k], self.up_recv.at[self.base + k], self.at.up)

    def down(self, t, q, k):
        ref = self.view(self.passing, t, q)
        return remote(ref, ref, self.down_send.at[self.base + k], self.down_recv.at[self.base + k], self.at.down)

    def step(self, n):
        at, planes = self.at, self.at.planes
        k = n - at.z * self.skew
        q = lax.rem(k, self.cut)
        t = planes - 1 - k // self.cut

        @pl.when((k >= 0) & (t > at.z))
        def _():
            here, mine = self.view(self.passing, t + 1, q), self.view(self.part, t, q)

            @pl.when(at.has_down)
            def _():
                self.up(t, q, k).wait_recv()
                here[...] = (mine[...].astype(F32) + here[...].astype(F32)).astype(BF16)

            @pl.when(jnp.logical_not(at.has_down))
            def _():
                here[...] = mine[...].astype(BF16)

            self.up(t, q, k).start()

        m = n - (planes - 1 - at.z) * self.skew
        p = lax.rem(m, self.cut)
        j = m // self.cut

        @pl.when((m >= 0) & (j < at.z))
        def _():
            here, mine = self.view(self.passing, j, p), self.view(self.part, j, p)

            @pl.when(at.has_up)
            def _():
                self.down(j, p, m).wait_recv()
                here[...] = (mine[...].astype(F32) + here[...].astype(F32)).astype(BF16)

            @pl.when(jnp.logical_not(at.has_up))
            def _():
                here[...] = mine[...].astype(BF16)

            self.down(j, p, m).start()

    def total(self, q):
        at, planes = self.at, self.at.planes

        @pl.when(at.has_down)
        def _():
            self.up(at.z, q, (planes - 1 - at.z) * self.cut + q).wait_recv()

        @pl.when(at.has_up)
        def _():
            self.down(at.z, q, at.z * self.cut + q).wait_recv()

        value = self.view(self.part, at.z, q)[...].astype(F32)
        nothing = jnp.zeros_like(value)
        below = self.view(self.passing, at.z + 1, q)[...].astype(F32)
        above = self.view(self.passing, at.z, q)[...].astype(F32)
        return value + jnp.where(at.has_down, below, nothing) + jnp.where(at.has_up, above, nothing)

    def finish(self):
        def sent(k, _):
            j, q = k // self.cut, lax.rem(k, self.cut)

            @pl.when(self.at.planes - 1 - j > self.at.z)
            def _():
                self.up(self.at.planes - 1 - j, q, k).wait_send()

            @pl.when(j < self.at.z)
            def _():
                self.down(j, q, k).wait_send()

            return 0

        lax.fori_loop(0, self.steps, sent, 0)


class PlaneSum:
    def __init__(self, at, part, sib_out, sib_in, far_in, own, sems):
        self.at, self.part = at, part
        self.sib_out, self.sib_in, self.far_in, self.own = sib_out, sib_in, far_in, own
        self.x_send, self.x_recv, self.f_send, self.f_recv = sems
        self.chips = at.group // 2
        self.sibling = at.sibling(at.rank)

    def far_rank(self, i):
        at = self.at
        chips_x = at.ns // 2
        x, core = at.s // 2, lax.rem(at.s, 2)
        y = lax.rem(at.y + i // chips_x, at.ny)
        return y * at.ns + lax.rem(x + lax.rem(i, chips_x), chips_x) * 2 + core

    def to_sibling(self, i):
        return remote(
            self.sib_out.at[i], self.sib_in.at[i], self.x_send.at[i], self.x_recv.at[i],
            self.at.member(self.sibling),
        )

    def to_far(self, i):
        return remote(
            self.sib_in.at[i], self.far_in.at[i - 1], self.f_send.at[i], self.f_recv.at[i],
            self.at.member(self.far_rank(i)),
        )

    def first(self, n):
        i = lax.rem(n + 1, self.chips)
        self.sib_out[i] = self.part(self.at.sibling(self.far_rank(i))).astype(BF16)
        self.to_sibling(i).start()

    def second(self, n):
        i = lax.rem(n + 1, self.chips)
        value = self.part(self.far_rank(i))
        self.to_sibling(i).wait_recv()
        value = value + self.sib_in[i].astype(F32)

        @pl.when(i > 0)
        def _():
            self.sib_in[i] = value.astype(BF16)
            self.to_far(i).start()

        @pl.when(i == 0)
        def _():
            self.own[...] = value

    def task(self, n):
        @pl.when(n < self.chips)
        def _():
            self.first(n)

        @pl.when((n >= self.chips) & (n < 2 * self.chips))
        def _():
            self.second(n - self.chips)

    def total(self):
        value = self.own[...]
        for i in range(1, self.chips):
            self.to_far(i).wait_recv()
            value = value + self.far_in[i - 1].astype(F32)
        return value

    def finish(self):
        for i in range(self.chips):
            self.to_sibling(i).wait_send()
            if i:
                self.to_far(i).wait_send()


def blocked(start, size):
    return pl.ds(pl.multiple_of(start * size, size), size)


def mix_forward_kernel(
    planes, ny, ns, cut, relayed, share,
    proj_ref, raw_ref, dt_ref, wout_ref, bg_ref, half_ref,
    convw_ref, convb_ref, gate_gain_ref, dtb_ref, al_ref, sk_ref,
    states_ref, bc_ref, bct_ref, own_ref, dy_ref, mixed_ref, gate_ref, gsum_ref, grad_ref,
    proj, wout, grad, other, scanned, mixed_grad, state, halo, halo_bc, states, dy, mixed, gate_grad, sums,
    up_send, up_recv, down_send, down_recv, s_send, s_recv, g_send, g_recv, load_sem, state_sem, out_sem, own_sem,
):
    at = Place(planes, ny, ns)
    group, rank, z = at.group, at.rank, at.z
    total = proj.shape[0]
    channels = proj.shape[1] // 2
    rows = STRETCH
    count = total // rows
    steps = count // ny

    proj_copy = pltpu.make_async_copy(proj_ref, proj, load_sem.at[0])
    proj_copy.start()
    half_copy = pltpu.make_async_copy(half_ref, grad, load_sem.at[1])
    half_copy.start()
    own_rows = bg_ref.shape[0]

    def norm_rows(r):
        return blocked(r, own_rows)

    block = wout.shape[0] // planes if relayed else wout.shape[0]
    if relayed:
        wout[blocked(z, block), :] = wout_ref[...].astype(BF16)
    else:
        wout[...] = wout_ref[...].astype(BF16)
    other[norm_rows(rank), :] = bg_ref[:, D // 2 :]
    at.greet()
    gather = PlaneGather(at, norm_rows, other, (g_send, g_recv))
    part = block // cut

    def view(p, q):
        return wout.at[pl.ds(pl.multiple_of(p * block + q * part, part), part)]

    def up(p, q, k):
        return remote(view(p, q), view(p, q), up_send.at[k], up_recv.at[k], at.up)

    def down(p, q, k):
        return remote(view(p, q), view(p, q), down_send.at[k], down_recv.at[k], at.down)

    if relayed:

        def first(q, _):
            @pl.when(at.has_up)
            def _():
                up(z, q, q).start()

            @pl.when(at.has_down)
            def _():
                down(z, q, q).start()

            return 0

        lax.fori_loop(0, cut, first, 0)
    gather.start()

    def relay(k, _):
        j, q = k // cut + 1, lax.rem(k, cut)

        @pl.when(z + j < planes)
        def _():
            down(z + j, q, k).wait_recv()

            @pl.when(at.has_down)
            def _():
                down(z + j, q, k + cut).start()

        @pl.when(z - j >= 0)
        def _():
            up(z - j, q, k).wait_recv()

            @pl.when(at.has_up)
            def _():
                up(z - j, q, k + cut).start()

        return 0

    gain = share.channel_rows(gate_gain_ref, rank)
    conv_wx = share.channel_rows(convw_ref, rank)
    conv_bx = share.channel_rows(convb_ref, rank)
    conv_wbc = convw_ref[:, INNER:]
    conv_bbc = convb_ref[:, INNER:]
    bias = share.head_column(dtb_ref, rank)
    a_log = share.head_column(al_ref, rank)
    skip = spread(share.head_column(sk_ref, rank).T)
    relays = (planes - 1) * cut if relayed else 0
    per_chunk = min(2, relays // count)
    proj_copy.wait()
    causal = iota((rows, rows), 0) >= iota((rows, rows), 1)
    lane = iota((rows, 2 * HEADDIM), 1)

    def state_copy(i):
        return pltpu.make_async_copy(states.at[lax.rem(i, 2)], states_ref.at[i], state_sem.at[lax.rem(i, 2)])

    def chunk(i, _):
        here = blocked(i, rows)

        @pl.when(lax.rem(i, steps) == 0)
        def _():
            state[...] = jnp.zeros_like(state)
            halo[...] = jnp.zeros_like(halo)
            halo_bc[...] = jnp.zeros_like(halo_bc)

        raw_bc = raw_ref[:, here].astype(F32).T
        conv_bc, _ = convolved(raw_bc, halo_bc[...], conv_wbc, conv_bbc)
        halo_bc[...] = raw_bc[rows - 8 :]
        active = conv_bc / (1.0 + jnp.exp(-conv_bc))
        bc = active.astype(BF16)
        bc_ref[here, :] = bc
        bct_ref[:, here] = active.T.astype(BF16)
        b_t = bct_ref[:STATE, here]
        c = bc[:, STATE:]
        raw = proj[here, channels:].astype(F32)
        conv, _ = convolved(raw, halo[...], conv_wx, conv_bx)
        halo[...] = raw[rows - 8 :]
        xs = conv / (1.0 + jnp.exp(-conv))
        _, step_t, _, run_t = head_times(dt_ref[:, here], bias, a_log)
        run = run_t.T
        xdt = xs * spread(step_t.T)
        products = jnp.where(causal, mm(c, b_t), 0.0)
        entering = state[...]

        @pl.when(i >= 2)
        def _():
            state_copy(i - 2).wait()

        states[lax.rem(i, 2)] = entering
        state_copy(i).start()
        inward = mm(c, entering) * spread(jnp.exp(run))
        skipped = skip * xs
        for pair in range(channels // 128):
            cols = slice(pair * 128, pair * 128 + 128)
            piece = xdt[:, cols]
            value = inward[:, cols] + skipped[:, cols]
            for side in range(2):
                h = 2 * pair + side
                decay = jnp.exp(jnp.minimum(run[:, h : h + 1] - run_t[h : h + 1], 0.0))
                own = (lane < HEADDIM) if side == 0 else (lane >= HEADDIM)
                value = value + mm(products * decay, jnp.where(own, piece, 0.0))
            scanned[here, cols] = value
        last = run[rows - 1 :]
        to_end = spread(jnp.exp(last - run))
        state[...] = entering * spread(jnp.exp(last)) + mm(b_t, xdt * to_end)
        lax.fori_loop(i * per_chunk, (i + 1) * per_chunk, relay, 0)
        return 0

    units = len(gather.units)
    last = 0
    for i in range(units):
        mark = min(count, 3 + 2 * (i // 2)) if gather.square else count * (i + 1) // units
        lax.fori_loop(last, mark, chunk, 0)
        last = mark
        gather.arrive(i)
    lax.fori_loop(last, count, chunk, 0)
    lax.fori_loop(count * per_chunk, relays, relay, 0)
    gather.rest()
    half_copy.wait()
    grad_copies = [
        pltpu.make_async_copy(grad, grad_ref.at[:, pl.ds(0, D // 2)], load_sem.at[1]),
        pltpu.make_async_copy(other, grad_ref.at[:, pl.ds(D // 2, D // 2)], load_sem.at[2]),
    ]
    for copy in grad_copies:
        copy.start()
    own_copy = pltpu.make_async_copy(wout, own_ref, own_sem.at[0])
    own_copy.start()

    def gated(m):
        here = blocked(m, rows)
        gate = proj[here, :channels].astype(F32)
        sig = 1.0 / (1.0 + jnp.exp(-gate))
        return here, gate, sig, scanned[here, :]

    def sum_slab(m, _):
        here, gate, sig, inner = gated(m)
        value = mm_last(grad[here, :], wout[:, : D // 2]) + mm_last(other[here, :], wout[:, D // 2 :])
        mixed_grad[here, :] = value
        product = inner * (gate * sig)
        squares = jnp.sum(product * product, 1, keepdims=True)
        along = jnp.sum(value * gain * product, 1, keepdims=True)
        sums[rank, pl.ds(m, 1), :] = squares.T
        sums[rank, pl.ds(count + m, 1), :] = along.T
        return 0

    lax.fori_loop(0, count, sum_slab, 0)

    def sums_piece(r, i, owner):
        return remote(sums.at[owner], sums.at[owner], s_send.at[i], s_recv.at[owner], at.member(r))

    for i in range(1, group):
        sums_piece(at.peer(i), i, rank).start()
    for i in range(1, group):
        r = at.peer(i)
        sums_piece(r, i, r).wait_recv()
    whole = sums[0]
    for r in range(1, group):
        whole = whole + sums[r]
    whole = whole * (1.0 / INNER)
    scale = lax.rsqrt(whole + EPSILON)
    gsum_ref[...] = jnp.zeros_like(gsum_ref)

    def out_copies(m):
        here = blocked(m, rows)
        return [
            pltpu.make_async_copy(dy.at[lax.rem(m, 2)], dy_ref.at[here], out_sem.at[0, lax.rem(m, 2)]),
            pltpu.make_async_copy(mixed.at[lax.rem(m, 2)], mixed_ref.at[here], out_sem.at[1, lax.rem(m, 2)]),
            pltpu.make_async_copy(gate_grad.at[lax.rem(m, 2)], gate_ref.at[here], out_sem.at[2, lax.rem(m, 2)]),
        ]

    ids = iota(whole.shape, 0)

    def grad_slab(m, _):
        here, gate, sig, inner = gated(m)
        r = jnp.sum(jnp.where(ids == m, scale, 0.0), 0, keepdims=True).T
        mean = jnp.sum(jnp.where(ids == count + m, whole, 0.0), 0, keepdims=True).T
        silu = gate * sig
        product = inner * silu
        value = mixed_grad[here, :]
        normal = product * r
        product_grad = r * (value * gain) - product * (r * r * r * mean)
        gsum_ref[0:1] += jnp.sum(value * normal, 0, keepdims=True)

        @pl.when(m >= 2)
        def _():
            for copy in out_copies(m - 2):
                copy.wait()

        dy[lax.rem(m, 2)] = product_grad * silu
        mixed[lax.rem(m, 2)] = (normal * gain).astype(BF16)
        gate_grad[lax.rem(m, 2)] = (product_grad * inner * (sig * (1.0 + gate * (1.0 - sig)))).astype(BF16)
        for copy in out_copies(m):
            copy.start()
        return 0

    lax.fori_loop(0, count, grad_slab, 0)

    for n in range(2):
        state_copy(count - 2 + n).wait()
        for copy in out_copies(count - 2 + n):
            copy.wait()
    own_copy.wait()
    for copy in grad_copies:
        copy.wait()
    gather.finish()
    for i in range(1, group):
        sums_piece(at.peer(i), i, rank).wait_send()
    if relayed:

        def sent(k, _):
            j, q = k // cut, lax.rem(k, cut)

            @pl.when((z + j < planes) & at.has_down)
            def _():
                down(z + j, q, k).wait_send()

            @pl.when((z - j >= 0) & at.has_up)
            def _():
                up(z - j, q, k).wait_send()

            return 0

        lax.fori_loop(0, planes * cut, sent, 0)


def pieces_per_plane(planes, group):
    cut = 1
    while cut * 2 <= min(group, 32 // planes):
        cut *= 2
    return cut


def mix_forward(projected, bc_raw, dt_t, w_out, branch_grad, grad_half, vectors, planes, ny, ns, relayed, share):
    total, channels = projected.shape[0], projected.shape[1] // 2
    group = ny * ns
    count = total // STRETCH
    cut = pieces_per_plane(planes, group)
    units = 6 if (ny, ns) == (2, 4) else group // 2 - 1
    gather = 2 * units + 2
    dma = pltpu.SemaphoreType.DMA
    anywhere = pl.BlockSpec(memory_space=pl.ANY)
    vmem = pl.BlockSpec(memory_space=pltpu.VMEM)
    line = dma((planes * cut,))
    return pl.pallas_call(
        functools.partial(mix_forward_kernel, planes, ny, ns, cut, relayed, share),
        in_specs=[anywhere] + [vmem] * 4 + [anywhere] + [vmem] * 6,
        out_specs=[anywhere, vmem, vmem, anywhere, anywhere, anywhere, anywhere, vmem, anywhere],
        out_shape=[
            jax.ShapeDtypeStruct((count, STATE, channels), F32),
            jax.ShapeDtypeStruct((total, 2 * STATE), BF16),
            jax.ShapeDtypeStruct((2 * STATE, total), BF16),
            jax.ShapeDtypeStruct((channels, D), BF16),
            jax.ShapeDtypeStruct((total, channels), F32),
            jax.ShapeDtypeStruct((total, channels), BF16),
            jax.ShapeDtypeStruct((total, channels), BF16),
            jax.ShapeDtypeStruct((8, channels), F32),
            jax.ShapeDtypeStruct((total, D), BF16),
        ],
        scratch_shapes=[
            pltpu.VMEM((total, 2 * channels), BF16),
            pltpu.VMEM((channels, D), BF16),
            pltpu.VMEM((total, D // 2), BF16),
            pltpu.VMEM((total, D // 2), BF16),
            pltpu.VMEM((total, channels), F32),
            pltpu.VMEM((total, channels), F32),
            pltpu.VMEM((STATE, channels), F32),
            pltpu.VMEM((8, channels), F32),
            pltpu.VMEM((8, 2 * STATE), F32),
            pltpu.VMEM((2, STATE, channels), F32),
            pltpu.VMEM((2, STRETCH, channels), F32),
            pltpu.VMEM((2, STRETCH, channels), BF16),
            pltpu.VMEM((2, STRETCH, channels), BF16),
            pltpu.VMEM((group, 2 * count, STRETCH), F32),
            line, line, line, line,
            dma((group,)), dma((group,)), dma((gather,)), dma((gather,)),
            dma((3,)), dma((2,)), dma((3, 2)), dma((1,)),
        ],
        compiler_params=pltpu.CompilerParams(
            collective_id=4, has_side_effects=True, vmem_limit_bytes=60 << 20
        ),
        name="mix_forward",
    )(projected, bc_raw, dt_t, w_out, branch_grad, grad_half, *vectors)


def mix_backward_kernel(
    planes, ny, ns, cut, relayed, share,
    proj_ref, bc_ref, bct_ref, dt_ref, dy_ref, states_ref, mixed_ref, gate_ref, own_ref, grad_ref, nt_ref,
    convw_ref, convb_ref, dtb_ref, al_ref, sk_ref,
    dx_ref, dbc_ref, ddt_ref, sums_ref, heads_ref, wout_ref, branch_ref, wgate_ref,
    xin, dyb, stb, mixed, mixed_t, gate_grad, own, tile, ntb, dwo, passing_o, dwg, passing_g,
    sib_out, sib_in, far_in, kept_sum, dxb, lam, rim,
    up_send, up_recv, down_send, down_recv, x_send, x_recv, f_send, f_recv, a_send, a_recv,
    load_sem, tile_sem, nt_sem, in_sem, dx_sem,
):
    at = Place(planes, ny, ns)
    group, rank, z = at.group, at.rank, at.z
    total, channels = mixed.shape
    heads = channels // HEADDIM
    rows = STRETCH
    count = total // rows
    steps = count // ny
    plane_rows = D // planes
    piece, part = plane_rows // group, plane_rows // cut
    block = total // group
    width = tile.shape[2]
    tiles = D // width
    span = channels // planes

    mixed_copy = pltpu.make_async_copy(mixed_ref, mixed, load_sem.at[0])
    mixed_copy.start()

    def tile_copy(q):
        return pltpu.make_async_copy(
            grad_ref.at[:, blocked(q, width)], tile.at[lax.rem(q, 2)], tile_sem.at[lax.rem(q, 2)]
        )

    def plane_in_turn(j):
        return lax.rem(jnp.where(2 * z < planes, z + j, z - j + planes), planes)

    def nt_plane(i):
        return plane_in_turn(planes - 1 - i)

    def nt_copy(i):
        return pltpu.make_async_copy(
            nt_ref.at[blocked(nt_plane(i), plane_rows)], ntb.at[lax.rem(i, 2)], nt_sem.at[lax.rem(i, 2)]
        )

    tile_copy(0).start()
    tile_copy(1).start()
    gate_copy = pltpu.make_async_copy(gate_ref, gate_grad, load_sem.at[1])
    gate_copy.start()
    nt_copy(0).start()
    nt_copy(1).start()
    own_copy = pltpu.make_async_copy(own_ref, own, load_sem.at[2])
    own_copy.start()
    x_copy = pltpu.make_async_copy(proj_ref.at[:, pl.ds(channels, channels)], xin, load_sem.at[3])
    x_copy.start()

    def chunk_of(n):
        return n // steps * steps + steps - 1 - lax.rem(n, steps)

    def in_copies(n):
        i, slot = chunk_of(n), lax.rem(n, 2)
        return [
            pltpu.make_async_copy(dy_ref.at[blocked(i, rows)], dyb.at[slot], in_sem.at[0, slot]),
            pltpu.make_async_copy(states_ref.at[i], stb.at[slot], in_sem.at[1, slot]),
        ]

    for n in range(2):
        for copy in in_copies(n):
            copy.start()
    at.greet()

    def view_out(ref, t, q):
        return ref.at[blocked(t, span), blocked(q, width)]

    sems = (up_send, up_recv, down_send, down_recv)
    line_out = LineSum(at, tiles, view_out, dwo, passing_o, sems)

    def view_gate(ref, t, q):
        return ref.at[pl.ds(pl.multiple_of(t * plane_rows + q * part, part), part)]

    line_gate = LineSum(at, cut, view_gate, dwg, passing_g, sems, line_out.steps if relayed else 0)
    mixed_copy.wait()

    def turn(m, _):
        here = blocked(m, rows)
        mixed_t[:, here] = mixed[here, :].T
        return 0

    lax.fori_loop(0, count, turn, 0)

    def out_tile(q, _):
        tile_copy(q).wait()
        value = jnp.dot(mixed_t[...], tile[lax.rem(q, 2)], preferred_element_type=F32)
        dwo[:, blocked(q, width)] = value.astype(BF16)

        @pl.when(q + 2 < tiles)
        def _():
            tile_copy(q + 2).start()

        if relayed:
            line_out.step(q)
        return 0

    lax.fori_loop(0, tiles, out_tile, 0)
    if not relayed:
        kept_out = pltpu.make_async_copy(dwo, wout_ref, load_sem.at[0])
        kept_out.start()

    own_copy.wait()

    def branch_part(r):
        return jnp.dot(mixed[blocked(r, block), :], own[...], preferred_element_type=F32)

    plane = PlaneSum(
        at, branch_part, sib_out, sib_in, far_in, kept_sum, (x_send, x_recv, f_send, f_recv)
    )

    gate_copy.wait()
    half = min(256, plane_rows)

    def weight_plane(i, _):
        nt_copy(i).wait()

        def one(h, _):
            there = pl.ds(pl.multiple_of(nt_plane(i) * plane_rows + h * half, half), half)
            dwg[there, :] = jnp.dot(
                ntb[lax.rem(i, 2), blocked(h, half), :], gate_grad[...], preferred_element_type=F32
            ).astype(BF16)
            return 0

        lax.fori_loop(0, plane_rows // half, one, 0)

        @pl.when(i + 2 < planes)
        def _():
            nt_copy(i + 2).start()

        out_steps(tiles + i * beside, tiles + (i + 1) * beside)
        return 0

    def out_steps(start, stop):
        if relayed:
            lax.fori_loop(start, jnp.minimum(stop, line_out.slots), lambda n, _: (line_out.step(n), 0)[1], 0)

    def gate_steps(start, stop):
        lax.fori_loop(start, jnp.minimum(stop, line_gate.slots), lambda n, _: (line_gate.step(n), 0)[1], 0)

    beside = -(-tiles // planes)
    lax.fori_loop(0, planes, weight_plane, 0)
    out_done = tiles + planes * beside

    def task(n, _):
        plane.task(n)
        out_steps(out_done + n, out_done + n + 1)
        gate_steps(n, n + 1)
        return 0

    tasks = 2 * plane.chips
    lax.fori_loop(0, tasks, task, 0)
    out_done = out_done + tasks
    per_out = -(-max(line_out.slots - out_done, 0) // count)
    per_gate = -(-(line_gate.slots - tasks) // count)

    sums_ref[...] = jnp.zeros_like(sums_ref)
    heads_ref[...] = jnp.zeros_like(heads_ref)
    x_copy.wait()
    conv_wx = share.channel_rows(convw_ref, rank)
    conv_bx = share.channel_rows(convb_ref, rank)
    bias = share.head_column(dtb_ref, rank)
    a_log = share.head_column(al_ref, rank)
    skip = spread(share.head_column(sk_ref, rank).T)
    causal = iota((rows, rows), 0) >= iota((rows, rows), 1)
    lower = causal.astype(F32)
    lane = iota((rows, 2 * HEADDIM), 1)
    wide = iota((rows, heads), 1)
    member = (iota((heads, channels), 1) // HEADDIM == iota((heads, channels), 0)).astype(F32)

    def per_head(values):
        return lax.dot_general(
            member, values, (((1,), (1,)), ((), ())), precision=HIGH, preferred_element_type=F32
        )

    def dx_copy(n):
        return pltpu.make_async_copy(
            dxb.at[lax.rem(n, 2)], dx_ref.at[blocked(chunk_of(n), rows)], dx_sem.at[lax.rem(n, 2)]
        )

    def chunk(n, _):
        i, slot = chunk_of(n), lax.rem(n, 2)
        here = blocked(i, rows)
        start = lax.rem(n, steps) == 0

        @pl.when(start)
        def _():
            lam[...] = jnp.zeros_like(lam)
            rim[...] = jnp.zeros_like(rim)

        for copy in in_copies(n):
            copy.wait()
        dy = dyb[slot]
        entering = stb[slot]
        raw = xin[here, :].astype(F32)
        ahead = pl.ds(pl.multiple_of(jnp.maximum(i * rows - 16, 0), 16), 16)
        before = jnp.where(lax.rem(i, steps) == 0, 0.0, xin[ahead, :].astype(F32))
        conv, shifted = convolved(raw, before, conv_wx, conv_bx)
        sig_c = 1.0 / (1.0 + jnp.exp(-conv))
        xs = conv * sig_c
        sums_ref[6:7] += jnp.sum(dy * xs, 0, keepdims=True)
        pre, step_t, decay_t, run_t = head_times(dt_ref[:, here], bias, a_log)
        run = run_t.T
        step = spread(step_t.T)
        xdt = xs * step
        b = bc_ref[here, :STATE]
        c = bc_ref[here, STATE:]
        b_t = bct_ref[:STATE, here]
        c_t = bct_ref[STATE:, here]
        products = jnp.where(causal, mm(c, b_t), 0.0)
        leaving = lam[...]
        last = run[rows - 1 :]
        to_end = spread(jnp.exp(last - run))
        dye = dy * spread(jnp.exp(run))
        xend = xdt * to_end
        inward = dye * mm(c, entering)
        outward_grad = mm(b, leaving) * to_end
        outward = outward_grad * xdt
        dc_t = mm_last(entering, dye)
        db_t = mm_last(leaving, xend)
        kept = leaving * spread(jnp.exp(last))
        lam[...] = kept + mm(c_t, dye)

        dy_t = dy.T.astype(BF16)
        dproducts = jnp.zeros((rows, rows), F32)
        row_sums = jnp.zeros((rows, heads), F32)
        col_sums = []
        dxdt_t = []
        for h in range(heads):
            cols = slice((h // 2) * 128, (h // 2) * 128 + 128)
            mine = (lane < HEADDIM) if h % 2 == 0 else (lane >= HEADDIM)
            decay = jnp.exp(jnp.minimum(run[:, h : h + 1] - run_t[h : h + 1], 0.0))
            weights = products * decay
            dweights = mm_last(dy[:, cols], jnp.where(mine, xdt[:, cols], 0.0))
            dproducts = dproducts + dweights * decay
            shares = dweights * weights
            row_sums = jnp.where(wide == h, jnp.sum(shares, 1, keepdims=True), row_sums)
            col_sums.append(jnp.sum(shares, 0, keepdims=True))
            dxdt_t.append(mm(dy_t[h * HEADDIM : (h + 1) * HEADDIM], weights))
        dproducts = jnp.where(causal, dproducts, 0.0)
        dbc_ref[:STATE, here] = (db_t + mm(c_t, dproducts)).astype(BF16)
        dbc_ref[STATE:, here] = (dc_t + mm_last(b_t, dproducts)).astype(BF16)
        dxdt = jnp.concatenate(dxdt_t, 0).T + outward_grad

        out_t = per_head(outward)
        run_grad = per_head(inward) - out_t + row_sums.T - jnp.concatenate(col_sums, 0)
        at_end = jnp.sum(out_t, 1, keepdims=True) + jnp.sum(per_head(kept * entering), 1, keepdims=True)
        decay_grad = at_end + jnp.dot(run_grad, lower, precision=HIGH, preferred_element_type=F32)
        step_grad = per_head(dxdt * xs) - jnp.exp(a_log) * decay_grad
        dt_grad = step_grad / (1.0 + jnp.exp(-pre))
        ddt_ref[:, here] = dt_grad.astype(BF16)
        heads_ref[:, 0:1] += jnp.sum(dt_grad, 1, keepdims=True)
        heads_ref[:, 1:2] += jnp.sum(decay_grad * decay_t, 1, keepdims=True)

        dx = dxdt * step + skip * dy
        dconv = dx * (sig_c * (1.0 + conv * (1.0 - sig_c)))
        sums_ref[4:5] += jnp.sum(dconv, 0, keepdims=True)
        for k in range(KERNEL):
            sums_ref[k : k + 1] += jnp.sum(dconv * shifted[k], 0, keepdims=True)
        joined = jnp.concatenate([dconv, rim[...]], 0)
        rim[...] = dconv[:8]
        dx_in = conv_wx[KERNEL - 1 : KERNEL] * dconv
        for k in range(KERNEL - 1):
            later = KERNEL - 1 - k
            dx_in = dx_in + conv_wx[k : k + 1] * joined[later : later + rows]

        @pl.when(n >= 2)
        def _():
            dx_copy(n - 2).wait()

        dxb[slot] = dx_in.astype(BF16)
        dx_copy(n).start()

        @pl.when(n + 2 < count)
        def _():
            for copy in in_copies(n + 2):
                copy.start()

        out_steps(out_done + n * per_out, out_done + (n + 1) * per_out)
        gate_steps(tasks + n * per_gate, tasks + (n + 1) * per_gate)
        return 0

    lax.fori_loop(0, count, chunk, 0)

    if relayed:

        def out_total(q, _):
            wout_ref[:, blocked(q, width)] = line_out.total(q)
            return 0

        lax.fori_loop(0, tiles, out_total, 0)

    def piece_rows(r):
        return pl.ds(pl.multiple_of(z * plane_rows + r * piece, piece), piece)

    def wide_out(r, owner):
        return remote(
            passing_g.at[piece_rows(r)], wgate_ref.at[owner], a_send.at[r], a_recv.at[owner], at.member(r)
        )

    wide_kept = pltpu.make_async_copy(passing_g.at[piece_rows(rank)], wgate_ref.at[rank], load_sem.at[1])

    def last_step(q, _):
        view_gate(passing_g, z, q)[...] = line_gate.total(q).astype(BF16)
        for m in range(group // cut):
            r = q * (group // cut) + m

            @pl.when(r != rank)
            def _():
                wide_out(r, rank).start()

            @pl.when(r == rank)
            def _():
                wide_kept.start()

        return 0

    lax.fori_loop(0, cut, last_step, 0)
    branch_ref[...] = plane.total()

    for n in range(2):
        dx_copy(count - 2 + n).wait()
    for i in range(1, group):
        r = at.peer(i)
        wide_out(r, rank).wait_send()
        wide_out(r, r).wait_recv()
    wide_kept.wait()
    plane.finish()
    if relayed:
        line_out.finish()
    else:
        kept_out.wait()
    line_gate.finish()


def mix_backward(
    projected, bc, bc_t, dt_t, dy, states, mixed, gate_grad, own, grad_all, normed_t, vectors, planes, ny, ns, relayed, share
):
    total, channels = projected.shape[0], projected.shape[1] // 2
    heads = channels // HEADDIM
    group = ny * ns
    cut = pieces_per_plane(planes, group)
    width = D // 8
    span = channels // planes
    plane_rows = D // planes
    block = total // group
    chips = group // 2
    dma = pltpu.SemaphoreType.DMA
    anywhere = pl.BlockSpec(memory_space=pl.ANY)
    vmem = pl.BlockSpec(memory_space=pltpu.VMEM)
    line = dma(((planes - 1) * (8 + cut),))
    slots = channels + span if relayed else 16
    return pl.pallas_call(
        functools.partial(mix_backward_kernel, planes, ny, ns, cut, relayed, share),
        in_specs=[anywhere, vmem, vmem, vmem] + [anywhere] * 7 + [vmem] * 5,
        out_specs=[anywhere, vmem, vmem, vmem, vmem, vmem if relayed else anywhere, vmem, anywhere],
        out_shape=[
            jax.ShapeDtypeStruct((total, channels), BF16),
            jax.ShapeDtypeStruct((2 * STATE, total), BF16),
            jax.ShapeDtypeStruct((heads, total), BF16),
            jax.ShapeDtypeStruct((8, channels), F32),
            jax.ShapeDtypeStruct((heads, 128), F32),
            jax.ShapeDtypeStruct((span, D), F32) if relayed else jax.ShapeDtypeStruct((channels, D), BF16),
            jax.ShapeDtypeStruct((block, D), F32),
            jax.ShapeDtypeStruct((group, plane_rows // group, channels), BF16),
        ],
        scratch_shapes=[
            pltpu.VMEM((total, channels), BF16),
            pltpu.VMEM((2, STRETCH, channels), F32),
            pltpu.VMEM((2, STATE, channels), F32),
            pltpu.VMEM((total, channels), BF16),
            pltpu.VMEM((channels, total), BF16),
            pltpu.VMEM((total, channels), BF16),
            pltpu.VMEM((channels, D), BF16),
            pltpu.VMEM((2, total, width), BF16),
            pltpu.VMEM((2, plane_rows, total), BF16),
            pltpu.VMEM((channels, D), BF16),
            pltpu.VMEM((slots, D), BF16),
            pltpu.VMEM((D, channels), BF16),
            pltpu.VMEM((D + plane_rows, channels), BF16),
            pltpu.VMEM((chips, block, D), BF16),
            pltpu.VMEM((chips, block, D), BF16),
            pltpu.VMEM((chips - 1, block, D), BF16),
            pltpu.VMEM((block, D), F32),
            pltpu.VMEM((2, STRETCH, channels), BF16),
            pltpu.VMEM((STATE, channels), F32),
            pltpu.VMEM((8, channels), F32),
            line, line, line, line,
            dma((chips,)), dma((chips,)), dma((chips,)), dma((chips,)), dma((group,)), dma((group,)),
            dma((4,)), dma((2,)), dma((2,)), dma((2, 2)), dma((2,)),
        ],
        compiler_params=pltpu.CompilerParams(
            collective_id=5, has_side_effects=True, vmem_limit_bytes=62 << 20
        ),
        name="mix_backward",
    )(projected, bc, bc_t, dt_t, dy, states, mixed, gate_grad, own, grad_all, normed_t, *vectors)


class Layout:
    def __init__(self, planes, group, rows_out):
        self.planes, self.group = planes, group
        self.aligned = rows_out % HEADDIM == 0
        self.blocks = planes if self.aligned else 1
        self.block = INNER // group // self.blocks
        self.heads = HEADS // group
        self.channels = INNER // group
        self.small = 2 * STATE // group

    def pieces(self, values, unit):
        rows = values.shape[0]
        parts = values.reshape(rows, self.blocks, self.group, self.block // HEADDIM * unit)
        return parts.transpose(0, 2, 1, 3).reshape(rows, self.group, -1)

    def joined(self, values, unit):
        rows = values.shape[0]
        parts = values.reshape(rows, self.group, self.blocks, self.block // HEADDIM * unit)
        return parts.transpose(0, 2, 1, 3).reshape(rows, -1)

    def columns(self, w):
        gate = self.pieces(w[:, :INNER], HEADDIM)
        x = self.pieces(w[:, INNER : 2 * INNER], HEADDIM)
        bc = w[:, 2 * INNER : INNER + CHANNELS].reshape(w.shape[0], self.group, self.small)
        dt = self.pieces(w[:, INNER + CHANNELS :], 1)
        return jnp.concatenate([gate, x, bc, dt], 2)

    def uncolumns(self, g):
        c, s = self.channels, self.small
        gate = self.joined(g[:, :, :c], HEADDIM)
        x = self.joined(g[:, :, c : 2 * c], HEADDIM)
        bc = g[:, :, 2 * c : 2 * c + s].reshape(g.shape[0], -1)
        dt = self.joined(g[:, :, 2 * c + s :], 1)
        return jnp.concatenate([gate, x, bc, dt], 1)


def body(
    tokens, cotangent, lengths, norm_gain, w_in, conv_w, conv_b, dt_bias, a_log, skip_scale, gate_gain, w_out,
):
    row_count = tokens.shape[1]
    planes, group = lax.axis_size("z"), lax.axis_size("y") * lax.axis_size("seq")
    seqs = lax.axis_size("y")
    ny, ns = lax.axis_size("y"), lax.axis_size("seq")
    rank = lax.axis_index("y") * lax.axis_size("seq") + lax.axis_index("seq")
    lay = Layout(planes, group, w_out.shape[0])
    channels, small = lay.channels, lay.small
    inputs = tokens.reshape(row_count, D).astype(F32)
    position = lax.axis_index("seq") * row_count + jnp.arange(row_count, dtype=jnp.int32)
    valid_mask = (position < lengths[0]).astype(F32)[:, None]
    rms = lax.rsqrt(jnp.mean(inputs * inputs, -1, keepdims=True) + EPSILON)
    masked_cot = cotangent.reshape(row_count, D).astype(F32) * valid_mask

    share = Share(planes, group, lay.aligned)
    projected, bc_raw, dt_t, normed_t, w_main, w_small, branch_grad, grad_half = gather_project(
        lengths, tokens.reshape(row_count, D), cotangent.reshape(row_count, D), w_in, norm_gain[None],
        planes, ny, ns, share,
    )
    out_rows = w_out
    if not lay.aligned:
        out_all = lax.all_gather(w_out.astype(BF16), ("z",) + GROUP, axis=0, tiled=True)
        out_rows = lax.dynamic_slice_in_dim(out_all, rank * channels, channels, 0)
    taps, offsets = conv_w.T, conv_b[None]
    head_vectors = (dt_bias[None], a_log[None], skip_scale[None])
    states, bc, bc_t, out_own, dy, mixed, gate_grad, gain_sums, grad_all = mix_forward(
        projected, bc_raw, dt_t, out_rows, branch_grad, grad_half,
        (taps, offsets, gate_gain[None]) + head_vectors, planes, ny, ns, lay.aligned, share,
    )
    x_grad, dbc_t, ddt_t, sums_x, sums_h, out_part, branch, gate_pieces = mix_backward(
        projected, bc, bc_t, dt_t, dy, states, mixed, gate_grad, out_own, grad_all, normed_t,
        (taps, offsets) + head_vectors, planes, ny, ns, lay.aligned, share,
    )
    output = (valid_mask * (inputs + branch)).astype(BF16)
    if lay.aligned:
        grad_w_out = out_part
    else:
        placed = lax.dynamic_update_slice_in_dim(jnp.zeros((INNER, D), BF16), out_part, rank * channels, 0)
        grad_w_out = lax.psum_scatter(placed, ("z",) + GROUP, scatter_dimension=0, tiled=True).astype(F32)

    own_bc = lambda v: lax.dynamic_slice_in_dim(v[INNER:], rank * small, small, 0)
    conv_own = jnp.pad(
        jnp.concatenate([own_bc(conv_w), own_bc(conv_b[:, None])], 1), ((0, 0), (0, 128 - KERNEL - 1))
    )
    in_pieces, in_small, normed_grad, bc_sums = project_grads(
        normed_t, x_grad, gate_grad, w_main, w_small, dbc_t, ddt_t, bc_raw, conv_own, planes, ny, ns
    )
    lanes = in_small.reshape(group, in_small.shape[1], -1, w_in.shape[0])
    mine = lax.dynamic_index_in_dim(lanes, lax.rem(rank, lanes.shape[2]), 2, keepdims=False)
    mine = mine[:, : small + lay.heads].transpose(2, 0, 1)
    grad_w_in = lay.uncolumns(jnp.concatenate([gate_pieces.transpose(1, 0, 2), in_pieces.transpose(1, 0, 2), mine], 2)).astype(F32)
    g = normed_grad * norm_gain
    input_grad = masked_cot + rms * g - inputs * (rms ** 3 * jnp.mean(g * inputs, -1, keepdims=True))
    norm_gain_grad = jnp.sum(normed_grad * inputs * rms, 0)

    own_sums = jnp.concatenate(
        [
            sums_x[: KERNEL + 1].reshape(-1),
            gain_sums[0],
            jnp.sum(sums_x[KERNEL + 2].reshape(-1, HEADDIM), 1),
            sums_h[:, 0],
            sums_h[:, 1],
            bc_sums[:, :KERNEL].T.reshape(-1),
            bc_sums[:, KERNEL],
        ]
    )
    count = own_sums.shape[0]
    flat = jnp.concatenate([norm_gain_grad, own_sums, jnp.zeros((-(count + D) % 1024,), F32)])
    by_rank = exchange(flat.reshape(-1, 128), planes, ny, ns).reshape(group, -1)
    grad_norm_gain = jnp.sum(by_rank[:, :D], 0)
    by_rank = by_rank[:, D : D + count]
    at = 0

    def take(size):
        nonlocal at
        at += size
        return by_rank[:, at - size : at]

    taken_x = take((KERNEL + 2) * channels).reshape(group, KERNEL + 2, channels).transpose(1, 0, 2)
    full_x = lay.joined(taken_x, HEADDIM)
    grad_skip, grad_bias, grad_a = (
        lay.joined(take(lay.heads)[None], 1)[0] for _ in range(3)
    )
    conv_w_bc = take(KERNEL * small).reshape(group, KERNEL, small).transpose(1, 0, 2).reshape(KERNEL, -1)
    conv_b_bc = take(small).reshape(-1)
    grad_conv_w = jnp.concatenate([full_x[:KERNEL], conv_w_bc], 1).T
    grad_conv_b = jnp.concatenate([full_x[KERNEL], conv_b_bc])
    return (
        output.reshape(tokens.shape),
        input_grad.reshape(1, row_count, D),
        grad_norm_gain,
        grad_w_in,
        grad_conv_w,
        grad_conv_b,
        grad_bias,
        grad_a,
        grad_skip,
        full_x[KERNEL + 1],
        grad_w_out,
    )


def solution(mesh):
    dp, seq = mesh.shape["dp"], mesh.shape["seq"]
    inner_mesh = Mesh(mesh.devices.reshape(dp // 2, 2, seq), ("z", "y", "seq"))
    placed = P(("z", "y"), "seq", None)
    rows = P(("z", "y", "seq"), None)
    in_specs = (placed, placed, P(("z", "y")), P(), rows, P(), P(), P(), P(), P(), P(), rows)
    out_specs = (placed, placed, P(), rows, P(), P(), P(), P(), P(), P(), rows)
    return jax.shard_map(body, mesh=inner_mesh, in_specs=in_specs, out_specs=out_specs, check_vma=False)
```
